32 devices in a mesh: segment: 4 (over y, x), wide: 8 (over z, core).
Axes of the slice: x: 2, y: 2, z: 4, core: 2. Of those that a mesh axis runs over, the one named last changes fastest.
Arguments:
- entering_hidden: bfloat16 [2, 16, 8192], P(None, 'wide'), may hold values from -6 to 6
- row_adapter_index: int32 [2, 16, 1], P(None, 'wide'), may hold values from 0 to 7; in each aligned block of 16 rows (0 to 15, 16 to 31, ..., all dimensions but the last counted through in order) at most 4 rows name the same one
- lengths: int32 [2, 16], P(None, 'wide'), may hold values from 2 to 384
- input_norm_gain: bfloat16 [4, 8192], P('segment'), may hold values from 0.099609375 to 1.8984375
- query_matrix: bfloat16 [4, 8192, 8192], P('segment', None, 'wide'), may hold values from -0.0625 to 0.0625
- key_matrix: bfloat16 [4, 8192, 1024], P('segment', None, 'wide'), may hold values from -0.0625 to 0.0625
- value_matrix: bfloat16 [4, 8192, 1024], P('segment', None, 'wide'), may hold values from -0.0625 to 0.0625
- output_matrix: bfloat16 [4, 8192, 8192], P('segment', None, 'wide'), may hold values from -0.0625 to 0.0625
- adapter_down_maps: bfloat16 [4, 8, 8192, 128], P('segment', 'wide'), may hold values from -0.0625 to 0.0625
- adapter_up_query: bfloat16 [4, 8, 64, 8192], P('segment', 'wide'), may hold values from -0.75 to 0.75
- adapter_up_value: bfloat16 [4, 8, 64, 1024], P('segment', 'wide'), may hold values from -0.75 to 0.75
- rotated_key_cache: bfloat16 [4, 2, 16, 384, 1024], P('segment', None, 'wide'), may hold values from -480 to 480
- cached_values: bfloat16 [4, 2, 16, 384, 1024], P('segment', None, 'wide'), may hold values from -6 to 6
Outputs:
- layer_out: bfloat16 [4, 2, 16, 8192], P('segment', None, 'wide')
The draws below stay inside these ranges and needn't reach their ends.
Inputs may be any that keep to these rules, and one draw needn't show every extreme that they name: `row_adapter_index`: in each micro-batch no adapter is named by more than 4 rows.
All inputs are finite; a program needn't handle non-finite values.
Results may differ from the reference program's by a relative error of at most 0.038.
Values may be sent and summed in bfloat16 or wider, within the bound.
No kernel may reach another device: no remote copies, remote signals or barrier semaphores. Data moves between devices by JAX's collectives and lax.ppermute only.
A program may use at most 128 MiB of HBM per device.

```python
import math
import jax
import jax.numpy as jnp
import numpy as np
from jax import lax

MODEL_WIDTH = 8192
HEADS = 64
KVH = 8
HD = 128
ADAPTER_RANK = 64
CAP = 4
MICRO = 2
CTX = 384
KEY_FEATURES = 1024
ADAPTER_COUNT = 8
ROWS_MB = 16
N_SEGMENT = 4


def draw_lengths(key, part):
    first, second = jax.random.split(key)
    values = jax.random.randint(first, (MICRO * ROWS_MB,), 2, CTX + 1)
    spot = jax.random.randint(second, (), 0, MICRO * ROWS_MB)
    values = values.at[spot].set(CTX)
    return values.reshape(MICRO, ROWS_MB).astype(jnp.int32)


def draw_rotated_key_cache(key, part):
    first = jax.random.fold_in(key, 0)
    array_shape = (N_SEGMENT, MICRO, ROWS_MB, CTX, KEY_FEATURES)
    entries = jax.random.truncated_normal(first, -6.0, 6.0, array_shape, jnp.float32)
    return entries.astype(jnp.bfloat16)


def shard_levels(own_key, dims, pieces, low, top_value):
    def one(dim, blocks):
        steps = jax.random.uniform(jax.random.fold_in(jax.random.fold_in(own_key, 6), dim), (blocks,), jnp.float32, low / len(pieces), top_value / len(pieces))
        return jnp.repeat(jnp.exp(steps), dims[dim] // blocks).reshape((-1,) + (1,) * (len(dims) - dim - 1))

    loudness = one(*pieces[0])
    for cut in pieces[1:]:
        loudness = loudness * one(*cut)
    return loudness


def shared_out(stream_key, own, number, rows, number_of, top, bound, lean):
    ranking = jax.random.permutation(stream_key, number_of)
    crowded, ordinary = shares(number_of, rows * top, bound, lean, True), shares(number_of, rows * top, bound, lean, False)
    places = jnp.arange(number_of)

    def named(tallies, turn):
        used = int((tallies > 0).sum())
        fixed = max(1, used // 4)
        shifted = fixed + (places - fixed + turn * (used - fixed)) % max(1, number_of - fixed)
        return jnp.zeros((number_of,), jnp.int32).at[ranking[jnp.where(places < fixed, places, shifted)]].set(jnp.asarray(tallies, jnp.int32))

    tallies = jnp.where(number % 4 == 0, named(crowded, number // 4), named(ordinary, number - number // 4 - 1))
    mixed = jax.random.permutation(jax.random.fold_in(own, 3), number_of)
    donor, receiver = mixed[0:number_of // 2 * 2:2], mixed[1:number_of // 2 * 2:2]
    room = jnp.minimum(tallies[donor] - 1, bound - tallies[receiver]) // 2
    room = jnp.where((donor == ranking[0]) | (receiver == ranking[0]) | (tallies[receiver] == 0), 0, jnp.maximum(room, 0))
    shifted = jax.random.randint(jax.random.fold_in(own, 4), (number_of // 2,), 0, 1 << 20) % (room + 1)
    tallies = tallies.at[donor].add(-shifted).at[receiver].add(shifted)
    members = jnp.searchsorted(jnp.cumsum(tallies), jnp.arange(rows * top), side="right").astype(jnp.int32)
    listing = members.reshape(top, rows).T
    listing = listing[jax.random.permutation(jax.random.fold_in(own, 1), rows)]
    turn = jax.random.randint(jax.random.fold_in(own, 2), (rows, 1), 0, top)
    return jnp.take_along_axis(listing, (jnp.arange(top)[None, :] + turn) % top, axis=1)


def shares(amount, total, bound, slope, full):
    loads = [(1 << 20) // math.isqrt(standing ** slope) + 1 for standing in range(1, amount + 1)]
    largest = bound if full else min(bound, max(-(-total // amount), total * loads[0] // sum(loads)))
    least = 1 if total - largest >= amount - 1 else 0
    holding, spare = [largest] + [least] * (amount - 1), total - largest - least * (amount - 1)
    while spare > 0:
        free = [i for i in range(1, amount) if holding[i] < largest] or [i for i in range(1, amount) if holding[i] < bound]
        mass, left = sum([loads[i] for i in free]), spare
        for i in free:
            extra = min(bound - holding[i], max(1, left * loads[i] // mass), spare)
            holding[i] = holding[i] + extra
            spare = spare - extra
    return np.array(holding)


def scatter_about(key, extent, width, most, cuts=(), kind=jnp.bfloat16):
    level = shard_levels(key, extent, cuts, -0.22, 0.18) if cuts else 1.0
    drawn = jax.random.normal(key, extent, jnp.float32) * width * level
    return jnp.minimum(jnp.maximum(drawn, -most), most).astype(kind)


def setup_inputs(seed: int = 0) -> dict:
    splits = jax.random.split(jax.random.key(seed), 14)
    entering_hidden = scatter_about(splits[0], (MICRO, ROWS_MB, MODEL_WIDTH), 1.0, 6.0, ((1, 8),))
    row_adapter_index_keys = jax.random.split(jax.random.fold_in(splits[1], 1), MICRO * ROWS_MB // ROWS_MB)
    row_adapter_index_turns = jax.random.permutation(jax.random.fold_in(splits[1], 3), MICRO * ROWS_MB // ROWS_MB)
    row_adapter_index = jax.vmap(lambda own, number: shared_out(jax.random.fold_in(splits[1], 2), own, number, ROWS_MB, ADAPTER_COUNT, 1, CAP, 2))(row_adapter_index_keys, row_adapter_index_turns).reshape((MICRO, ROWS_MB, 1))
    lengths = draw_lengths(jax.random.fold_in(splits[13], 71), 0)
    input_norm_gain = jnp.clip(1.0 + 0.18 * jax.random.normal(splits[3], (N_SEGMENT, MODEL_WIDTH), jnp.float32), 0.099609375, 1.8984375).astype(jnp.bfloat16)
    query_matrix = scatter_about(splits[4], (N_SEGMENT, MODEL_WIDTH, MODEL_WIDTH), MODEL_WIDTH ** -0.5, 0.0625, ((0, 4), (2, 8)))
    key_matrix = scatter_about(splits[5], (N_SEGMENT, MODEL_WIDTH, KEY_FEATURES), MODEL_WIDTH ** -0.5, 0.0625, ((0, 4), (2, 8)))
    value_matrix = scatter_about(splits[6], (N_SEGMENT, MODEL_WIDTH, KEY_FEATURES), MODEL_WIDTH ** -0.5, 0.0625, ((0, 4), (2, 8)))
    output_matrix = scatter_about(splits[7], (N_SEGMENT, MODEL_WIDTH, MODEL_WIDTH), MODEL_WIDTH ** -0.5, 0.0625, ((0, 4), (2, 8)))
    adapter_down_maps = scatter_about(splits[8], (N_SEGMENT, ADAPTER_COUNT, MODEL_WIDTH, 2 * ADAPTER_RANK), MODEL_WIDTH ** -0.5, 0.0625, ((0, 4), (1, 8)))
    adapter_up_query = scatter_about(splits[9], (N_SEGMENT, ADAPTER_COUNT, ADAPTER_RANK, MODEL_WIDTH), ADAPTER_RANK ** -0.5, 0.75, ((0, 4), (1, 8)))
    adapter_up_value = scatter_about(splits[10], (N_SEGMENT, ADAPTER_COUNT, ADAPTER_RANK, KEY_FEATURES), ADAPTER_RANK ** -0.5, 0.75, ((0, 4), (1, 8)))
    rotated_key_cache = draw_rotated_key_cache(jax.random.fold_in(splits[13], 71), 0)
    cached_values = scatter_about(splits[12], (N_SEGMENT, MICRO, ROWS_MB, CTX, KEY_FEATURES), 1.0, 6.0, ((0, 4), (2, 8)))
    return {"entering_hidden": entering_hidden, "row_adapter_index": row_adapter_index, "lengths": lengths, "input_norm_gain": input_norm_gain, "query_matrix": query_matrix, "key_matrix": key_matrix, "value_matrix": value_matrix, "output_matrix": output_matrix, "adapter_down_maps": adapter_down_maps, "adapter_up_query": adapter_up_query, "adapter_up_value": adapter_up_value, "rotated_key_cache": rotated_key_cache, "cached_values": cached_values}


adapter_scale = 0.5
rope_base = 500000.0
epsilon = 1e-05

def rotary(vectors, positions):
    half = vectors.shape[-1] // 2
    inverse = rope_base ** (-jnp.arange(half, dtype=jnp.float32) / half)
    angles = positions.astype(jnp.float32)[:, None] * inverse[None, :]
    cosine = jnp.cos(angles)[:, None, :]
    sine = jnp.sin(angles)[:, None, :]
    front = vectors[..., :half]
    back = vectors[..., half:]
    return jnp.concatenate([front * cosine - back * sine, back * cosine + front * sine], -1)

def adapter_deltas(normalized_rows, idents, down, up_query, up_value):

    def one_row(inputs):
        row, ident = inputs
        low = jnp.dot(row, down[ident], preferred_element_type=jnp.float32).astype(jnp.bfloat16)
        query_adjustment = jnp.dot(low[:ADAPTER_RANK], up_query[ident], preferred_element_type=jnp.float32)
        value_adjustment = jnp.dot(low[ADAPTER_RANK:], up_value[ident], preferred_element_type=jnp.float32)
        return (query_adjustment, value_adjustment)
    return lax.map(one_row, (normalized_rows, idents))

def apply_layer(hidden_rows, idents, positions, gain, query_matrix, key_matrix, value_matrix, output_matrix, down, up_query, up_value, key_block, value_block):
    rows = hidden_rows.shape[0]
    values = hidden_rows.astype(jnp.float32)
    normalized_rows = (values * lax.rsqrt(lax.optimization_barrier(jnp.mean(values * values, 1, keepdims=True)) + epsilon) * gain.astype(jnp.float32)).astype(jnp.bfloat16)
    query_adjustment, value_adjustment = adapter_deltas(normalized_rows, idents, down, up_query, up_value)
    query_vector = (jnp.dot(normalized_rows, query_matrix, preferred_element_type=jnp.float32) + adapter_scale * query_adjustment).astype(jnp.bfloat16)
    new_key = jnp.dot(normalized_rows, key_matrix, preferred_element_type=jnp.float32).astype(jnp.bfloat16)
    fresh_value = (jnp.dot(normalized_rows, value_matrix, preferred_element_type=jnp.float32) + adapter_scale * value_adjustment).astype(jnp.bfloat16)
    group = HEADS // KVH
    rotated_rows = rotary(query_vector.astype(jnp.float32).reshape(rows, HEADS, HD), positions).astype(jnp.bfloat16)
    rotated_rows = rotated_rows.reshape(rows, KVH, group, HD).astype(jnp.float32)
    self_key = rotary(new_key.astype(jnp.float32).reshape(rows, KVH, HD), positions).astype(jnp.bfloat16).astype(jnp.float32)
    keys_past = key_block.reshape(rows, CTX, KVH, HD).astype(jnp.float32)
    values_past = value_block.reshape(rows, CTX, KVH, HD).astype(jnp.float32)
    score_scale = HD ** (-0.5)
    past = jnp.einsum('bkgd,bpkd->bkgp', rotated_rows, keys_past) * score_scale
    self_scores = jnp.einsum('rice,rie->ric', rotated_rows, self_key) * score_scale
    valid = jnp.arange(CTX)[None, :] < positions[:, None]
    past = jnp.where(valid[:, None, None, :], past, -1e+30)
    top = jnp.maximum(lax.optimization_barrier(jnp.max(past, -1)), self_scores)
    past_exp = jnp.where(valid[:, None, None, :], jnp.exp(past - top[..., None]), 0.0)
    own_exp = jnp.exp(self_scores - top)
    total = lax.optimization_barrier(jnp.sum(past_exp, -1)) + own_exp
    past_weights = (past_exp / total[..., None]).astype(jnp.bfloat16).astype(jnp.float32)
    own_weights = (own_exp / total).astype(jnp.bfloat16).astype(jnp.float32)
    mixed = jnp.einsum('bkgp,bpkd->bkgd', past_weights, values_past)
    mixed = mixed + own_weights[..., None] * fresh_value.reshape(rows, KVH, HD).astype(jnp.float32)[:, :, None, :]
    attended = mixed.reshape(rows, HEADS * HD).astype(jnp.bfloat16)
    projected = jnp.dot(attended, output_matrix, preferred_element_type=jnp.float32)
    return (values + projected).astype(jnp.bfloat16)

def reference(entering_hidden, row_adapter_index, lengths, input_norm_gain, query_matrix, key_matrix, value_matrix, output_matrix, adapter_down_maps, adapter_up_query, adapter_up_value, rotated_key_cache, cached_values):
    per_layer = [[None] * MICRO for layer_number in range(N_SEGMENT)]
    for small_batch in range(MICRO):
        hidden_rows = entering_hidden[small_batch]
        for layer_number in range(N_SEGMENT):
            hidden_rows = apply_layer(hidden_rows, row_adapter_index[small_batch, :, 0], lengths[small_batch], input_norm_gain[layer_number], query_matrix[layer_number], key_matrix[layer_number], value_matrix[layer_number], output_matrix[layer_number], adapter_down_maps[layer_number], adapter_up_query[layer_number], adapter_up_value[layer_number], rotated_key_cache[layer_number, small_batch], cached_values[layer_number, small_batch])
            per_layer[layer_number][small_batch] = hidden_rows
    return jnp.stack([jnp.stack(per_layer[layer_number]) for layer_number in range(N_SEGMENT)])
```

```python
import functools

import jax
import jax.numpy as jnp
from jax import lax
from jax.experimental import pallas as pl
from jax.experimental.pallas import tpu as pltpu
from jax.sharding import PartitionSpec as P

HEADS = 64
KVH = 8
HD = 128
ADAPTER_RANK = 64
CAP = 4


adapter_scale = 0.5
rope_base = 500000.0
epsilon = 1e-05

GROUP = HEADS // KVH
MIB = 1 << 20
VMEM = pl.BlockSpec(memory_space=pltpu.VMEM)
SMEM = pl.BlockSpec(memory_space=pltpu.SMEM)


def swapped(value, bits):
    count = lax.axis_size("wide")
    return lax.ppermute(value, "wide", [(i, i ^ bits) for i in range(count)])


def gathered(value):
    count = lax.axis_size("wide")
    found = [None] * count
    found[0] = value
    found[1] = swapped(value, 1)
    for far in range(2, count, 2):
        found[far] = swapped(value, far)
    for far in range(2, count, 2):
        found[far + 1] = swapped(found[far], 1)
    return found


def exchanged(blocks):
    found = []
    for k, block in enumerate(blocks):
        found.append(swapped(block, 2 * k) if k else block)
    return [part for far in found for part in (far, swapped(far, 1))]


def own_half(j, block):
    half = block.shape[0] // 2
    return block[(j % 2) * half : (j % 2 + 1) * half, :]


def resident(weight):
    return pltpu.with_memory_space_constraint(weight, pltpu.VMEM)


def call(body, out_shape, operands, scratch=(), limit=8, kept=(), name=None):
    outs = list(out_shape)
    found = pl.pallas_call(
        body,
        out_shape=outs,
        in_specs=[spec for _, spec in operands] + [VMEM] * len(kept),
        out_specs=[VMEM] * len(outs),
        scratch_shapes=list(scratch),
        compiler_params=pltpu.CompilerParams(vmem_limit_bytes=limit * MIB),
        name=name,
    )(*[array for array, _ in operands], *[resident(array) for array in kept])
    return [*found, *kept]


def dot(left, right):
    return jnp.dot(left, right, preferred_element_type=jnp.float32)


def matmul_into(store, source, weight, step):
    def one(i, carry):
        columns = pl.ds(pl.multiple_of(i * step, step), step)
        store(columns, dot(source[...], weight[:, columns]))
        return carry

    lax.fori_loop(0, weight.shape[1] // step, one, 0)


def by_part(owner, chunks, own_rows):
    count = len(chunks)
    parts = chunks[0].shape[0] // own_rows
    total = count * parts * own_rows
    stack = jnp.concatenate([chunk[...] for chunk in chunks], 0)
    out = lax.broadcasted_iota(jnp.int32, (total, total), 0)
    src = lax.broadcasted_iota(jnp.int32, (total, total), 1)
    rows = own_rows
    part_out = out // (rows * count)
    device_out = (out // rows) % count
    part_src = (src // rows) % parts
    device_src = (src // (rows * parts)) ^ owner
    hit = (part_out == part_src) & (device_out == device_src) & (out % rows == src % rows)
    return dot(jnp.where(hit, 1.0, 0.0).astype(jnp.bfloat16), stack)


def adapter_part(owner, ident, normed, down, up_query, up_value, outs, capacity):
    rows = normed.shape[0]
    low = dot(normed[...], down[0]).astype(jnp.bfloat16)
    place = lax.broadcasted_iota(jnp.int32, (rows, rows), 0)
    other = lax.broadcasted_iota(jnp.int32, (rows, rows), 1)
    mine = jnp.where(ident[:, :1] == owner.astype(jnp.float32), 1.0, 0.0)
    flat = jnp.where(place == other, mine, 0.0).astype(jnp.bfloat16)
    before = jnp.where(place < other, mine, 0.0).astype(jnp.bfloat16)
    ones = jnp.ones((capacity, rows), jnp.bfloat16)
    member = dot(ones, flat)
    rank = dot(ones, before)
    slot = lax.broadcasted_iota(jnp.int32, (capacity, rows), 0).astype(jnp.float32)
    chosen = jnp.where((member > 0.5) & (rank == slot), 1.0, 0.0).astype(jnp.bfloat16)
    picked = dot(chosen, low).astype(jnp.bfloat16)
    count = 2 * len(outs)
    query_cols = up_query.shape[2] // count
    value_cols = up_value.shape[2] // count
    for j in range(count):
        out = outs[j // 2]
        slots = slice((j % 2) * capacity, (j % 2 + 1) * capacity)
        columns = pl.ds(pl.multiple_of((owner ^ j) * query_cols, query_cols), query_cols)
        for_query = dot(picked[:, :ADAPTER_RANK], up_query[0, :, columns]) * adapter_scale
        out[slots, :query_cols] = for_query.astype(jnp.bfloat16)
        columns = pl.ds(pl.multiple_of((owner ^ j) * value_cols, value_cols), value_cols)
        for_value = dot(picked[:, ADAPTER_RANK:], up_value[0, :, columns]) * adapter_scale
        out[slots, query_cols:] = for_value.astype(jnp.bfloat16)


def enter_kernel(count, own_rows, capacity, owner_ref, *refs):
    chunks, rest = refs[:count], refs[count:]
    gain, down, up_query, up_value, normed, held, ident, *correction, spread = rest
    owner = owner_ref[0]
    rows = count * own_rows
    part = gain.shape[1] // count
    spread[...] = by_part(owner, chunks, own_rows)
    ident[...] = spread[:rows, part:]
    squares = jnp.zeros((rows, 1), jnp.float32)
    for i in range(count):
        block = spread[i * rows : (i + 1) * rows, :part]
        squares += jnp.sum(block * block, 1, keepdims=True)
    scale = lax.rsqrt(squares / gain.shape[1] + epsilon)
    for i in range(count):
        block = spread[i * rows : (i + 1) * rows, :part]
        columns = slice(i * part, (i + 1) * part)
        weight = gain[:, columns].astype(jnp.float32)
        normed[:, columns] = (block * scale * weight).astype(jnp.bfloat16)
    own = pl.ds(pl.multiple_of(owner * rows, rows), rows)
    held[...] = spread[own, :part].astype(jnp.bfloat16)
    adapter_part(owner, ident, normed, down, up_query, up_value, correction, capacity)


def norm_kernel(count, capacity, owner_ref, *refs):
    chunks, rest = refs[:count], refs[count:]
    ident, gain, down, up_query, up_value, normed, *correction = rest
    owner = owner_ref[0]
    rows, part = chunks[0].shape
    squares = jnp.zeros((rows, 1), jnp.float32)
    for chunk in chunks:
        block = chunk[...].astype(jnp.float32)
        squares += jnp.sum(block * block, 1, keepdims=True)
    scale = lax.rsqrt(squares / gain.shape[1] + epsilon)
    for k, chunk in enumerate(chunks):
        columns = pl.ds(pl.multiple_of((owner ^ k) * part, part), part)
        weight = gain[:, columns].astype(jnp.float32)
        normed[:, columns] = (chunk[...].astype(jnp.float32) * scale * weight).astype(jnp.bfloat16)
    adapter_part(owner, ident, normed, down, up_query, up_value, correction, capacity)


def project_kernel(normed, query, key, value, out):
    wide, narrow = query.shape[1], key.shape[1]

    def store(columns, product):
        out[:, columns] = product

    matmul_into(store, normed, query, 256)
    out[:, wide : wide + narrow] = dot(normed[...], key[...])
    out[:, wide + narrow :] = dot(normed[...], value[...])


def correct_kernel(count, capacity, query_cols, key_cols, owner_ref, base, ident, *refs):
    received, outs = refs[:count], refs[count:]
    owner = owner_ref[0]
    rows = base.shape[0]
    own_rows = rows // count
    slots = count * capacity
    place = lax.broadcasted_iota(jnp.int32, (rows, rows), 0)
    other = lax.broadcasted_iota(jnp.int32, (rows, rows), 1)
    own = ident[:, :1]
    flat = jnp.where(place == other, own, 0.0).astype(jnp.bfloat16)
    line = dot(jnp.ones((rows, rows), jnp.bfloat16), flat)
    rank = jnp.sum(jnp.where((own == line) & (other < place), 1.0, 0.0), 1, keepdims=True)
    slot = lax.broadcasted_iota(jnp.int32, (rows, slots), 1)
    source = ((slot // capacity) ^ owner).astype(jnp.float32)
    hit = (source == own) & ((slot % capacity).astype(jnp.float32) == rank)
    table = jnp.where(hit, 1.0, 0.0).astype(jnp.bfloat16)
    placed = dot(table, jnp.concatenate([own_half(j, ref) for j, ref in enumerate(received)], 0))
    whole = base[...]
    first = whole[:, :query_cols] + placed[:, :query_cols]
    middle = whole[:, query_cols : query_cols + key_cols]
    last = whole[:, query_cols + key_cols :] + placed[:, query_cols:]
    packed = jnp.concatenate([first, middle, last], 1).astype(jnp.bfloat16)
    by_destination(owner, packed, own_rows, outs)


def by_destination(owner, packed, own_rows, outs):
    rows = packed.shape[0]
    place = lax.broadcasted_iota(jnp.int32, (rows, rows), 0)
    other = lax.broadcasted_iota(jnp.int32, (rows, rows), 1)
    hit = (((place // own_rows) ^ owner) == other // own_rows) & (
        place % own_rows == other % own_rows
    )
    order = jnp.where(hit, 1.0, 0.0).astype(jnp.bfloat16)
    sorted_rows = dot(order, packed).astype(jnp.bfloat16)
    for k, out in enumerate(outs):
        out[...] = sorted_rows[k * 2 * own_rows : (k + 1) * 2 * own_rows, :]


def attend_kernel(count, owner_ref, lengths, *refs):
    arrived, (cosine, sine, keys, values, out) = refs[:count], refs[count:]
    owner = owner_ref[0]
    own_rows, span = keys.shape[:2]
    rows = GROUP * own_rows
    cos, sin = cosine[...], sine[...]
    row_of = lax.broadcasted_iota(jnp.int32, (rows, span), 0) % own_rows
    position = lax.broadcasted_iota(jnp.int32, (rows, span), 1)
    limit = jnp.zeros((rows, span), jnp.int32)
    for r in range(own_rows):
        limit = jnp.where(row_of == r, lengths[r], limit)
    valid = position < limit
    score_scale = HD ** (-0.5)

    def turned(vectors):
        return vectors * cos + pltpu.roll(vectors, HD // 2, 1) * sin

    def rounded(vectors):
        return vectors.astype(jnp.bfloat16).astype(jnp.float32)

    for j, ref in enumerate(arrived):
        packed = own_half(j, ref).astype(jnp.float32)
        query = jnp.concatenate([packed[:, i * HD : (i + 1) * HD] for i in range(GROUP)], 0)
        new_key = packed[:, GROUP * HD : (GROUP + 1) * HD]
        new_value = packed[:, (GROUP + 1) * HD :]
        new_key = jnp.concatenate([new_key] * GROUP, 0)
        new_value = jnp.concatenate([new_value] * GROUP, 0)
        query = turned(query).astype(jnp.bfloat16)
        new_key = rounded(turned(new_key))
        lanes = pl.ds(pl.multiple_of((owner ^ j) * HD, HD), HD)
        scores = jnp.zeros((rows, span), jnp.float32)
        for r in range(own_rows):
            one = lax.dot_general(
                query,
                keys[r, :, lanes],
                (((1,), (1,)), ((), ())),
                preferred_element_type=jnp.float32,
            )
            scores = jnp.where(row_of == r, one, scores)
        scores = jnp.where(valid, scores * score_scale, -1e30)
        own = jnp.sum(query.astype(jnp.float32) * new_key, 1, keepdims=True) * score_scale
        top = jnp.maximum(jnp.max(scores, 1, keepdims=True), own)
        past = jnp.where(valid, jnp.exp(scores - top), 0.0)
        own = jnp.exp(own - top)
        total = jnp.sum(past, 1, keepdims=True) + own
        past = (past / total).astype(jnp.bfloat16)
        mixed = rounded(own / total) * new_value
        for r in range(own_rows):
            weights = jnp.where(row_of == r, past, jnp.zeros_like(past))
            mixed += dot(weights, values[r, :, lanes])
        out[:, lanes] = mixed.astype(jnp.bfloat16)


def leave_kernel(count, own_rows, tick, owner_ref, segment_ref, *refs):
    chunks, (held, result, matrix, out, kept, *outs, spread, rows_ref) = refs[:count], refs[count:]
    rows = count * own_rows
    spread[...] = by_part(owner_ref[0], chunks, own_rows).astype(jnp.bfloat16)
    for g in range(KVH):
        for j in range(GROUP):
            head = g * GROUP + j
            rows_ref[:, head * HD : (head + 1) * HD] = spread[
                j * rows : (j + 1) * rows, g * HD : (g + 1) * HD
            ]

    def store(columns, product):
        out[:, columns] = (held[:, columns].astype(jnp.float32) + product).astype(jnp.bfloat16)

    matmul_into(store, rows_ref, matrix, 256)
    kept[...] = jnp.where(segment_ref[0] == tick, out[...], result[...])
    if outs:
        by_destination(owner_ref[0], kept[...], own_rows, outs)


def join_kernel(count, owner_ref, *refs):
    blocks, out = refs[:count], refs[count]
    for j, block in enumerate(blocks):
        half = own_half(j, block)
        width = half.shape[1]
        out[:, pl.ds(pl.multiple_of((owner_ref[0] ^ j) * width, width), width)] = half


def on_device_by_head(
    entering_hidden,
    row_adapter_index,
    lengths,
    input_norm_gain,
    query_matrix,
    key_matrix,
    value_matrix,
    output_matrix,
    adapter_down_maps,
    adapter_up_query,
    adapter_up_value,
    rotated_key_cache,
    cached_values,
):
    segments = lax.axis_size("segment")
    segment = lax.axis_index("segment")
    count = lax.axis_size("wide")
    owner = lax.axis_index("wide")
    owner_ref = owner.astype(jnp.int32).reshape(1)
    segment_ref = segment.astype(jnp.int32).reshape(1)
    micro, local_rows, width = entering_hidden.shape
    own_rows = micro * local_rows
    rows = own_rows * count
    capacity = CAP * micro
    part = width // count
    query_cols, key_cols = query_matrix.shape[2], key_matrix.shape[2]
    packed_cols = query_cols + 2 * key_cols
    span = rotated_key_cache.shape[3]

    query_weight = query_matrix[0]
    key_weight = key_matrix[0]
    value_weight = value_matrix[0]
    output_weight = output_matrix[0]
    down = adapter_down_maps[0]
    up_query = adapter_up_query[0]
    up_value = adapter_up_value[0]
    keys = rotated_key_cache[0].reshape(own_rows, span, -1)
    values = cached_values[0].reshape(own_rows, span, -1)
    gain = input_norm_gain

    positions = lengths.reshape(-1)
    half = HD // 2
    inverse = rope_base ** (-jnp.arange(half, dtype=jnp.float32) / half)
    angles = positions.astype(jnp.float32)[:, None] * inverse[None, :]
    cosine = jnp.tile(jnp.concatenate([jnp.cos(angles)] * 2, 1), (GROUP, 1))
    sine = jnp.tile(jnp.concatenate([-jnp.sin(angles), jnp.sin(angles)], 1), (GROUP, 1))

    def blocks_of(slots, columns):
        return [jax.ShapeDtypeStruct((2 * slots, columns), jnp.bfloat16)] * (count // 2)

    normed_shape = jax.ShapeDtypeStruct((rows, width), jnp.bfloat16)
    held_shape = jax.ShapeDtypeStruct((rows, part), jnp.bfloat16)
    ident_shape = jax.ShapeDtypeStruct((rows, HD), jnp.float32)
    correction_shapes = blocks_of(capacity, query_cols + key_cols)

    own = entering_hidden.reshape(own_rows, count, part).transpose(1, 0, 2)
    names = row_adapter_index.reshape(1, own_rows, 1).astype(jnp.bfloat16)
    names = jnp.broadcast_to(names, (count, own_rows, HD))
    entering = jnp.concatenate([own, names], 2).reshape(count * own_rows, part + HD)

    adapters = [down, up_query, up_value]
    projections = [query_weight, key_weight, value_weight]
    caches = [keys, values]
    outputs = [output_weight]
    held = ident = None
    result = jnp.zeros((rows, part), jnp.bfloat16)
    blocks = []
    for tick in range(segments):
        if tick == 0:
            chunks = gathered(entering)
            normed, held, ident, *found = call(
                functools.partial(enter_kernel, count, own_rows, capacity),
                [normed_shape, held_shape, ident_shape] + correction_shapes,
                [(owner_ref, SMEM)] + [(c, VMEM) for c in chunks] + [(gain, VMEM)],
                [pltpu.VMEM((count * rows, part + HD), jnp.float32)],
                kept=adapters,
                name="enter",
            )
        else:
            held = lax.ppermute(
                held, "segment", [(s, (s + 1) % segments) for s in range(segments)]
            )
            chunks = gathered(held)
            normed, *found = call(
                functools.partial(norm_kernel, count, capacity),
                [normed_shape] + correction_shapes,
                [(owner_ref, SMEM)] + [(c, VMEM) for c in chunks] + [(ident, VMEM), (gain, VMEM)],
                kept=adapters,
                name="norm",
            )
        correction, adapters = found[: count // 2], found[count // 2 :]
        received = exchanged(correction)
        base, *projections = call(
            project_kernel,
            [jax.ShapeDtypeStruct((rows, packed_cols), jnp.float32)],
            [(normed, VMEM)],
            kept=projections,
            name="project",
        )
        packed = call(
            functools.partial(correct_kernel, count, capacity, query_cols, key_cols),
            blocks_of(own_rows, packed_cols),
            [(owner_ref, SMEM), (base, VMEM), (ident, VMEM)] + [(r, VMEM) for r in received],
            name="correct",
        )
        arrived = exchanged(packed)
        attended, *caches = call(
            functools.partial(attend_kernel, count),
            [jax.ShapeDtypeStruct((GROUP * own_rows, KVH * HD), jnp.bfloat16)],
            [(owner_ref, SMEM), (positions, SMEM)] + [(a, VMEM) for a in arrived]
            + [(cosine, VMEM), (sine, VMEM)],
            kept=caches,
            name="attend",
        )
        chunks = gathered(attended)
        last = tick == segments - 1
        held, result, *found = call(
            functools.partial(leave_kernel, count, own_rows, tick),
            [held_shape, held_shape] + (blocks_of(own_rows, part) if last else []),
            [(owner_ref, SMEM), (segment_ref, SMEM)] + [(c, VMEM) for c in chunks]
            + [(held, VMEM), (result, VMEM)],
            [
                pltpu.VMEM((GROUP * rows, KVH * HD), jnp.bfloat16),
                pltpu.VMEM((rows, width), jnp.bfloat16),
            ],
            kept=outputs,
            name="leave",
        )
        blocks, outputs = found[:-1], found[-1:]
    (joined,) = call(
        functools.partial(join_kernel, count),
        [jax.ShapeDtypeStruct((own_rows, width), jnp.bfloat16)],
        [(owner_ref, SMEM)] + [(b, VMEM) for b in exchanged(blocks)],
        name="join",
    )
    return joined.reshape(1, micro, local_rows, width)


def passed_along(value, axis, steps):
    count = lax.axis_size(axis)
    leading, last = (max(0, -steps), min(count, count - steps))
    return lax.ppermute(value, axis, [(source, source + steps) for source in range(leading, last)])


def rotary(vectors, positions):
    half = vectors.shape[-1] // 2
    inverse = rope_base ** (-jnp.arange(half, dtype=jnp.float32) / half)
    angles = positions.astype(jnp.float32)[:, None] * inverse[None, :]
    cosine = jnp.cos(angles)[:, None, :]
    sine = jnp.sin(angles)[:, None, :]
    front = vectors[..., :half]
    back = vectors[..., half:]
    return jnp.concatenate([front * cosine - back * sine, back * cosine + front * sine], -1)


def attend(query_vector, new_key, fresh_value, positions, key_block, value_block):
    rows = query_vector.shape[0]
    group = HEADS // KVH
    rotated_rows = rotary(
        query_vector.astype(jnp.float32).reshape(rows, HEADS, HD), positions
    ).astype(jnp.bfloat16)
    rotated_rows = rotated_rows.reshape(rows, KVH, group, HD)
    self_key = rotary(new_key.astype(jnp.float32).reshape(rows, KVH, HD), positions).astype(
        jnp.bfloat16
    )
    keys_past = key_block.reshape(rows, -1, KVH, HD)
    values_past = value_block.reshape(rows, -1, KVH, HD)
    score_scale = HD ** (-0.5)
    past = (
        jnp.einsum("bkgd,bpkd->bkgp", rotated_rows, keys_past, preferred_element_type=jnp.float32)
        * score_scale
    )
    self_scores = (
        jnp.einsum("rice,rie->ric", rotated_rows, self_key, preferred_element_type=jnp.float32)
        * score_scale
    )
    valid = jnp.arange(keys_past.shape[1])[None, :] < positions[:, None]
    past = jnp.where(valid[:, None, None, :], past, -1e30)
    top = jnp.maximum(jnp.max(past, -1), self_scores)
    past_exp = jnp.where(valid[:, None, None, :], jnp.exp(past - top[..., None]), 0.0)
    own_exp = jnp.exp(self_scores - top)
    total = jnp.sum(past_exp, -1) + own_exp
    past_weights = (past_exp / total[..., None]).astype(jnp.bfloat16)
    own_weights = (own_exp / total).astype(jnp.bfloat16)
    mixed = jnp.einsum(
        "bkgp,bpkd->bkgd", past_weights, values_past, preferred_element_type=jnp.float32
    )
    mixed = (
        mixed
        + own_weights.astype(jnp.float32)[..., None]
        * fresh_value.reshape(rows, KVH, HD).astype(jnp.float32)[:, :, None, :]
    )
    return mixed.reshape(rows, HEADS * HD).astype(jnp.bfloat16)


def on_device(
    entering_hidden,
    row_adapter_index,
    lengths,
    input_norm_gain,
    query_matrix,
    key_matrix,
    value_matrix,
    output_matrix,
    adapter_down_maps,
    adapter_up_query,
    adapter_up_value,
    rotated_key_cache,
    cached_values,
):
    segments = lax.axis_size("segment")
    segment = lax.axis_index("segment")
    devices = lax.axis_size("wide")
    owner = lax.axis_index("wide")
    small_batch, local_rows, width = entering_hidden.shape
    listed = lax.all_gather(row_adapter_index, "wide", axis=1, tiled=True)[:, :, 0]
    groups = small_batch // small_batch
    capacity = CAP * small_batch
    kept_entries = adapter_down_maps.shape[1]
    adapters = kept_entries * devices
    mine = owner * kept_entries + jnp.arange(kept_entries)
    gain = input_norm_gain[0].astype(jnp.float32)
    query_cols = query_matrix.shape[2]
    key_cols = key_matrix.shape[2]
    passed = jnp.zeros((small_batch * local_rows, width), jnp.bfloat16)
    results = jnp.zeros((small_batch, local_rows, width), jnp.bfloat16)
    ticks = groups + segments - 1
    for tick in range(ticks):
        if tick < groups:
            fresh = entering_hidden.reshape(small_batch * local_rows, width)
        else:
            fresh = jnp.zeros_like(passed)
        rows = jnp.where(segment == 0, fresh, passed)
        index = tick - segment
        live = (index >= 0) & (index < groups)
        index = jnp.clip(index, 0, groups - 1)
        block_rows = rows.shape[0]
        idents = listed
        idents = idents.reshape(small_batch, devices, local_rows).transpose(1, 0, 2).reshape(-1)
        positions = lengths.reshape(-1)
        key_block = rotated_key_cache[0]
        key_block = key_block.reshape(block_rows, key_block.shape[2], key_block.shape[3])
        value_block = cached_values[0]
        value_block = value_block.reshape(block_rows, value_block.shape[2], value_block.shape[3])
        values = rows.astype(jnp.float32)
        normalized_rows = (
            values * lax.rsqrt(jnp.mean(values * values, 1, keepdims=True) + epsilon) * gain
        ).astype(jnp.bfloat16)
        gathered = lax.all_gather(normalized_rows, "wide", axis=0, tiled=True)
        total_rows = gathered.shape[0]
        matches = (idents[None, :] == mine[:, None]).astype(jnp.int32)
        ranks = jnp.cumsum(matches, 1) - 1
        chosen = (matches[:, None, :] == 1) & (
            ranks[:, None, :] == jnp.arange(capacity)[None, :, None]
        )
        chosen = chosen.reshape(kept_entries * capacity, total_rows)
        selected_rows = jnp.dot(
            chosen.astype(jnp.bfloat16), gathered, preferred_element_type=jnp.float32
        ).astype(jnp.bfloat16)
        selected_rows = selected_rows.reshape(kept_entries, capacity, width)
        reduced = jnp.einsum(
            "bpy,byf->bpf", selected_rows, adapter_down_maps[0], preferred_element_type=jnp.float32
        ).astype(jnp.bfloat16)
        member = (idents[:, None] == jnp.arange(adapters)[None, :]).astype(jnp.int32)
        order = jnp.sum(jnp.cumsum(member, 0) * member, 1) - 1
        slot = idents * capacity + order
        slot_table = slot[:, None] == jnp.arange(adapters * capacity)[None, :]
        query_slots = jnp.einsum(
            "acr,are->ace",
            reduced[..., :ADAPTER_RANK],
            adapter_up_query[0],
            preferred_element_type=jnp.float32,
        )
        value_slots = jnp.einsum(
            "acr,are->ace",
            reduced[..., ADAPTER_RANK:],
            adapter_up_value[0],
            preferred_element_type=jnp.float32,
        )
        joined = jnp.concatenate(
            [
                query_slots.reshape(kept_entries * capacity, devices, -1),
                value_slots.reshape(kept_entries * capacity, devices, -1),
            ],
            2,
        )
        received = lax.all_to_all(joined, "wide", split_axis=1, concat_axis=0, tiled=True)
        received = received.reshape(adapters * capacity, -1)
        placed = jnp.dot(slot_table.astype(jnp.float32), received, precision=lax.Precision.HIGHEST)
        query_adjustment = placed[:, :query_cols]
        value_adjustment = placed[:, query_cols:]
        query_vector = (
            jnp.dot(gathered, query_matrix[0], preferred_element_type=jnp.float32)
            + adapter_scale * query_adjustment
        ).astype(jnp.bfloat16)
        new_key = jnp.dot(gathered, key_matrix[0], preferred_element_type=jnp.float32).astype(
            jnp.bfloat16
        )
        fresh_value = (
            jnp.dot(gathered, value_matrix[0], preferred_element_type=jnp.float32)
            + adapter_scale * value_adjustment
        ).astype(jnp.bfloat16)
        packed = jnp.concatenate([query_vector, new_key, fresh_value], 1)
        arrived = lax.all_to_all(packed, "wide", split_axis=0, concat_axis=1, tiled=True).reshape(
            block_rows, devices, -1
        )
        query_rows_local = arrived[:, :, :query_cols].reshape(block_rows, -1)
        key_rows_local = arrived[:, :, query_cols : query_cols + key_cols].reshape(block_rows, -1)
        value_rows_local = arrived[:, :, query_cols + key_cols :].reshape(block_rows, -1)
        attended = attend(
            query_rows_local, key_rows_local, value_rows_local, positions, key_block, value_block
        )
        columns = jnp.dot(
            lax.all_gather(attended, "wide", axis=0, tiled=True),
            output_matrix[0],
            preferred_element_type=jnp.float32,
        )
        returned = lax.all_to_all(columns, "wide", split_axis=0, concat_axis=1, tiled=True)
        outcome = (values + returned).astype(jnp.bfloat16)
        updated = outcome.reshape(small_batch, local_rows, width)
        results = jnp.where(live, updated, results)
        if tick + 1 < ticks:
            passed = passed_along(outcome, "segment", 1)
    return results[None]


def solution(mesh):
    placed = (
        P(None, "wide", None),
        P(None, "wide", None),
        P(None, "wide"),
        P("segment", None),
        P("segment", None, "wide"),
        P("segment", None, "wide"),
        P("segment", None, "wide"),
        P("segment", None, "wide"),
        P("segment", "wide", None, None),
        P("segment", "wide", None, None),
        P("segment", "wide", None, None),
        P("segment", None, "wide", None, None),
        P("segment", None, "wide", None, None),
    )
    by_head = mesh.shape["wide"] == KVH
    return jax.shard_map(
        on_device_by_head if by_head else on_device,
        mesh=mesh,
        in_specs=placed,
        out_specs=P("segment", None, "wide", None),
        check_vma=False,
    )
```

```python
import functools

import jax
import jax.numpy as jnp
import numpy as np
from jax import lax
from jax.experimental import pallas as pl
from jax.experimental.pallas import tpu as pltpu
from jax.sharding import PartitionSpec as P

HEADS = 64
KVH = 8
HD = 128
ADAPTER_RANK = 64
CAP = 4


adapter_scale = 0.5
rope_base = 500000.0
epsilon = 1e-05

GROUP = HEADS // KVH
MIB = 1 << 20
VMEM = pl.BlockSpec(memory_space=pltpu.VMEM)
SMEM = pl.BlockSpec(memory_space=pltpu.SMEM)


def swapped(value, bits):
    count = lax.axis_size("wide")
    return lax.ppermute(value, "wide", [(i, i ^ bits) for i in range(count)])


def then(arrays, work):
    if work is None:
        return arrays, None
    done = work()
    arrays = pl.pallas_call(
        lambda *refs: None,
        out_shape=[jax.ShapeDtypeStruct(array.shape, array.dtype) for array in arrays],
        in_specs=[VMEM] * len(arrays) + [pl.BlockSpec(memory_space=pl.ANY)],
        out_specs=[VMEM] * len(arrays),
        input_output_aliases={i: i for i in range(len(arrays))},
        compiler_params=pltpu.CompilerParams(vmem_limit_bytes=MIB),
        name="then",
    )(*arrays, done)
    return arrays, done


def gathered(value, work=None):
    count = lax.axis_size("wide")
    far = [swapped(value, k) for k in range(2, count, 2)]
    far, done = then(far, work)
    found = [part for one in [value, *far] for part in (one, swapped(one, 1))]
    return found, done


def exchanged(blocks, work=None):
    far = [swapped(block, 2 * k) for k, block in enumerate(blocks) if k]
    far, done = then(far, work)
    found = [part for one in [blocks[0], *far] for part in (one, swapped(one, 1))]
    return found, done


def own_half(j, block):
    half = block.shape[0] // 2
    return block[(j % 2) * half : (j % 2 + 1) * half, :]


def resident(weight):
    return pltpu.with_memory_space_constraint(weight, pltpu.VMEM)


def call(body, out_shape, operands, scratch=(), limit=8, kept=(), cost=1, name=None):
    outs = list(out_shape)
    found = pl.pallas_call(
        body,
        out_shape=outs,
        in_specs=[spec for _, spec in operands] + [VMEM] * len(kept),
        out_specs=[VMEM] * len(outs),
        scratch_shapes=list(scratch),
        compiler_params=pltpu.CompilerParams(vmem_limit_bytes=limit * MIB),
        cost_estimate=pl.CostEstimate(flops=0, transcendentals=0, bytes_accessed=cost * MIB),
        name=name,
    )(*[array for array, _ in operands], *[resident(array) for array in kept])
    return [*found, *kept]


def load_kernel(count, *refs):
    sources, after, outs, token, sems = refs[:count], refs[count], refs[count + 1 : -2], refs[-2], refs[-1]
    copies = [
        pltpu.make_async_copy(source, out, sems.at[i])
        for i, (source, out) in enumerate(zip(sources, outs, strict=True))
    ]
    for copy in copies:
        copy.start()
    token[...] = after[:8, :HD].astype(jnp.float32)
    for copy in copies:
        copy.wait()


def loaded(arrays, after):
    *found, token = pl.pallas_call(
        functools.partial(load_kernel, len(arrays)),
        out_shape=[pltpu.VMEM(array.shape, array.dtype) for array in arrays]
        + [jax.ShapeDtypeStruct((8, HD), jnp.float32)],
        in_specs=[pl.BlockSpec(memory_space=pl.ANY)] * len(arrays) + [VMEM],
        out_specs=[VMEM] * (len(arrays) + 1),
        scratch_shapes=[pltpu.SemaphoreType.DMA((len(arrays),))],
        compiler_params=pltpu.CompilerParams(vmem_limit_bytes=4 * MIB),
        cost_estimate=pl.CostEstimate(
            flops=0, transcendentals=0, bytes_accessed=sum(array.nbytes for array in arrays)
        ),
        name="load",
    )(*[pltpu.with_memory_space_constraint(array, pltpu.HBM) for array in arrays], after)
    return found, token


def dot(left, right):
    return jnp.dot(left, right, preferred_element_type=jnp.float32)


def matmul_into(store, source, weight, step):
    def one(i, carry):
        columns = pl.ds(pl.multiple_of(i * step, step), step)
        store(columns, dot(source[...], weight[:, columns]))
        return carry

    lax.fori_loop(0, weight.shape[1] // step, one, 0)


def by_part(owner, chunks, own_rows):
    count = len(chunks)
    parts = chunks[0].shape[0] // own_rows
    total = count * parts * own_rows
    stack = jnp.concatenate([chunk[...] for chunk in chunks], 0)
    out = lax.broadcasted_iota(jnp.int32, (total, total), 0)
    src = lax.broadcasted_iota(jnp.int32, (total, total), 1)
    rows = own_rows
    part_out = out // (rows * count)
    device_out = (out // rows) % count
    part_src = (src // rows) % parts
    device_src = (src // (rows * parts)) ^ owner
    hit = (part_out == part_src) & (device_out == device_src) & (out % rows == src % rows)
    return dot(jnp.where(hit, 1.0, 0.0).astype(jnp.bfloat16), stack)


def adapter_part(owner, ident, normed, down, up_query, up_value, outs, capacity):
    rows = normed.shape[0]
    low = dot(normed[...], down[0]).astype(jnp.bfloat16)
    place = lax.broadcasted_iota(jnp.int32, (rows, rows), 0)
    other = lax.broadcasted_iota(jnp.int32, (rows, rows), 1)
    mine = jnp.where(ident[:, :1] == owner.astype(jnp.float32), 1.0, 0.0)
    flat = jnp.where(place == other, mine, 0.0).astype(jnp.bfloat16)
    before = jnp.where(place < other, mine, 0.0).astype(jnp.bfloat16)
    ones = jnp.ones((capacity, rows), jnp.bfloat16)
    member = dot(ones, flat)
    rank = dot(ones, before)
    slot = lax.broadcasted_iota(jnp.int32, (capacity, rows), 0).astype(jnp.float32)
    chosen = jnp.where((member > 0.5) & (rank == slot), 1.0, 0.0).astype(jnp.bfloat16)
    picked = dot(chosen, low).astype(jnp.bfloat16)
    count = 2 * len(outs)
    query_cols = up_query.shape[2] // count
    value_cols = up_value.shape[2] // count
    for j in range(count):
        out = outs[j // 2]
        slots = slice((j % 2) * capacity, (j % 2 + 1) * capacity)
        columns = pl.ds(pl.multiple_of((owner ^ j) * query_cols, query_cols), query_cols)
        for_query = dot(picked[:, :ADAPTER_RANK], up_query[0, :, columns]) * adapter_scale
        out[slots, :query_cols] = for_query.astype(jnp.bfloat16)
        columns = pl.ds(pl.multiple_of((owner ^ j) * value_cols, value_cols), value_cols)
        for_value = dot(picked[:, ADAPTER_RANK:], up_value[0, :, columns]) * adapter_scale
        out[slots, query_cols:] = for_value.astype(jnp.bfloat16)


def open_kernel(hidden, names, lengths, inverse, entering, cosine, sine):
    micro, local_rows, width = hidden.shape
    own_rows = micro * local_rows
    part = entering.shape[1] - HD
    count = width // part
    rows = jnp.concatenate([hidden[m].astype(jnp.float32) for m in range(micro)], 0)
    entering[:, :part] = jnp.concatenate(
        [rows[:, i * part : (i + 1) * part] for i in range(count)], 0
    ).astype(jnp.bfloat16)
    row = lax.broadcasted_iota(jnp.int32, (count * own_rows, HD), 0) % own_rows
    name = jnp.zeros((count * own_rows, HD), jnp.float32)
    for r in range(own_rows):
        one = names[r // local_rows, r % local_rows, 0].astype(jnp.float32)
        name = jnp.where(row == r, one, name)
    entering[:, part:] = name.astype(jnp.bfloat16)
    row = lax.broadcasted_iota(jnp.int32, cosine.shape, 0) % own_rows
    position = jnp.zeros(cosine.shape, jnp.float32)
    for r in range(own_rows):
        one = lengths[r // local_rows, r % local_rows].astype(jnp.float32)
        position = jnp.where(row == r, one, position)
    angles = position * inverse[...]
    front = lax.broadcasted_iota(jnp.int32, cosine.shape, 1) < HD // 2
    cosine[...] = jnp.cos(angles)
    sine[...] = jnp.where(front, -jnp.sin(angles), jnp.sin(angles))


def enter_kernel(count, own_rows, capacity, *refs):
    chunks, rest = refs[:count], refs[count:]
    gain, down, up_query, up_value, normed, held, ident, *correction, spread = rest
    owner = lax.axis_index("wide")
    rows = count * own_rows
    part = gain.shape[1] // count
    spread[...] = by_part(owner, chunks, own_rows)
    ident[...] = spread[:rows, part:]
    squares = jnp.zeros((rows, 1), jnp.float32)
    for i in range(count):
        block = spread[i * rows : (i + 1) * rows, :part]
        squares += jnp.sum(block * block, 1, keepdims=True)
    scale = lax.rsqrt(squares / gain.shape[1] + epsilon)
    for i in range(count):
        block = spread[i * rows : (i + 1) * rows, :part]
        columns = slice(i * part, (i + 1) * part)
        weight = gain[:, columns].astype(jnp.float32)
        normed[:, columns] = (block * scale * weight).astype(jnp.bfloat16)
    own = pl.ds(pl.multiple_of(owner * rows, rows), rows)
    held[...] = spread[own, :part].astype(jnp.bfloat16)
    adapter_part(owner, ident, normed, down, up_query, up_value, correction, capacity)


def norm_kernel(count, capacity, *refs):
    chunks, rest = refs[:count], refs[count:]
    ident, gain, down, up_query, up_value, normed, *correction = rest
    owner = lax.axis_index("wide")
    rows, part = chunks[0].shape
    squares = jnp.zeros((rows, 1), jnp.float32)
    for chunk in chunks:
        block = chunk[...].astype(jnp.float32)
        squares += jnp.sum(block * block, 1, keepdims=True)
    scale = lax.rsqrt(squares / gain.shape[1] + epsilon)
    for k, chunk in enumerate(chunks):
        columns = pl.ds(pl.multiple_of((owner ^ k) * part, part), part)
        weight = gain[:, columns].astype(jnp.float32)
        normed[:, columns] = (chunk[...].astype(jnp.float32) * scale * weight).astype(jnp.bfloat16)
    adapter_part(owner, ident, normed, down, up_query, up_value, correction, capacity)


def project_kernel(normed, query, key, value, out):
    wide, narrow = query.shape[1], key.shape[1]

    def store(columns, product):
        out[:, columns] = product

    matmul_into(store, normed, query, 256)
    out[:, wide : wide + narrow] = dot(normed[...], key[...])
    out[:, wide + narrow :] = dot(normed[...], value[...])


def correct_kernel(count, capacity, query_cols, key_cols, base, ident, *refs):
    received, outs = refs[:count], refs[count:]
    owner = lax.axis_index("wide")
    rows = base.shape[0]
    own_rows = rows // count
    slots = count * capacity
    place = lax.broadcasted_iota(jnp.int32, (rows, rows), 0)
    other = lax.broadcasted_iota(jnp.int32, (rows, rows), 1)
    own = ident[:, :1]
    flat = jnp.where(place == other, own, 0.0).astype(jnp.bfloat16)
    line = dot(jnp.ones((rows, rows), jnp.bfloat16), flat)
    rank = jnp.sum(jnp.where((own == line) & (other < place), 1.0, 0.0), 1, keepdims=True)
    slot = lax.broadcasted_iota(jnp.int32, (rows, slots), 1)
    source = ((slot // capacity) ^ owner).astype(jnp.float32)
    hit = (source == own) & ((slot % capacity).astype(jnp.float32) == rank)
    table = jnp.where(hit, 1.0, 0.0).astype(jnp.bfloat16)
    placed = dot(table, jnp.concatenate([own_half(j, ref) for j, ref in enumerate(received)], 0))
    whole = base[...]
    first = whole[:, :query_cols] + placed[:, :query_cols]
    middle = whole[:, query_cols : query_cols + key_cols]
    last = whole[:, query_cols + key_cols :] + placed[:, query_cols:]
    packed = jnp.concatenate([first, middle, last], 1).astype(jnp.bfloat16)
    by_destination(owner, packed, own_rows, outs)


def by_destination(owner, packed, own_rows, outs):
    rows = packed.shape[0]
    place = lax.broadcasted_iota(jnp.int32, (rows, rows), 0)
    other = lax.broadcasted_iota(jnp.int32, (rows, rows), 1)
    hit = (((place // own_rows) ^ owner) == other // own_rows) & (
        place % own_rows == other % own_rows
    )
    order = jnp.where(hit, 1.0, 0.0).astype(jnp.bfloat16)
    sorted_rows = dot(order, packed).astype(jnp.bfloat16)
    for k, out in enumerate(outs):
        out[...] = sorted_rows[k * 2 * own_rows : (k + 1) * 2 * own_rows, :]


def attend_kernel(count, lengths, *refs):
    arrived, rest = refs[:count], refs[count:]
    cosine, sine, keys, values, out, scores, weights = rest
    owner = lax.axis_index("wide")
    own_rows, span = keys.shape[:2]
    local_rows = lengths.shape[1]
    rows = GROUP * own_rows
    cos, sin = cosine[...], sine[...]
    row_of = lax.broadcasted_iota(jnp.int32, (rows, span), 0) % own_rows
    position = lax.broadcasted_iota(jnp.int32, (rows, span), 1)
    limit = jnp.zeros((rows, span), jnp.int32)
    for r in range(own_rows):
        limit = jnp.where(row_of == r, lengths[r // local_rows, r % local_rows], limit)
    valid = position < limit
    score_scale = HD ** (-0.5)

    def turned(vectors):
        return vectors * cos + pltpu.roll(vectors, HD // 2, 1) * sin

    def rounded(vectors):
        return vectors.astype(jnp.bfloat16).astype(jnp.float32)

    fresh = []
    for j, ref in enumerate(arrived):
        packed = own_half(j, ref).astype(jnp.float32)
        query = jnp.concatenate([packed[:, i * HD : (i + 1) * HD] for i in range(GROUP)], 0)
        new_key = packed[:, GROUP * HD : (GROUP + 1) * HD]
        new_value = packed[:, (GROUP + 1) * HD :]
        new_key = jnp.concatenate([new_key] * GROUP, 0)
        new_value = jnp.concatenate([new_value] * GROUP, 0)
        query = turned(query).astype(jnp.bfloat16)
        new_key = rounded(turned(new_key))
        lanes = pl.ds(pl.multiple_of((owner ^ j) * HD, HD), HD)
        found = jnp.zeros((rows, span), jnp.float32)
        for r in range(own_rows):
            one = lax.dot_general(
                query,
                keys[r, :, lanes],
                (((1,), (1,)), ((), ())),
                preferred_element_type=jnp.float32,
            )
            found = jnp.where(row_of == r, one, found)
        scores[j * rows : (j + 1) * rows, :] = jnp.where(valid, found * score_scale, -1e30)
        own = jnp.sum(query.astype(jnp.float32) * new_key, 1, keepdims=True) * score_scale
        fresh.append((own, new_value))
    parts = []
    for j, (own, new_value) in enumerate(fresh):
        found = scores[j * rows : (j + 1) * rows, :]
        top = jnp.maximum(jnp.max(found, 1, keepdims=True), own)
        past = jnp.where(valid, jnp.exp(found - top), 0.0)
        own = jnp.exp(own - top)
        total = jnp.sum(past, 1, keepdims=True) + own
        weights[j * rows : (j + 1) * rows, :] = (past / total).astype(jnp.bfloat16)
        parts.append(rounded(own / total) * new_value)
    for j, mixed in enumerate(parts):
        lanes = pl.ds(pl.multiple_of((owner ^ j) * HD, HD), HD)
        past = weights[j * rows : (j + 1) * rows, :]
        for r in range(own_rows):
            one = jnp.where(row_of == r, past, jnp.zeros_like(past))
            mixed += dot(one, values[r, :, lanes])
        out[:, lanes] = mixed.astype(jnp.bfloat16)


def leave_kernel(count, own_rows, tick, *refs):
    chunks, rest = refs[:count], refs[count:]
    held, result = rest[0], rest[1] if tick else None
    matrix, out, kept, *outs, spread, rows_ref = rest[2 if tick else 1 :]
    rows = count * own_rows
    spread[...] = by_part(lax.axis_index("wide"), chunks, own_rows).astype(jnp.bfloat16)
    for g in range(KVH):
        for j in range(GROUP):
            head = g * GROUP + j
            rows_ref[:, head * HD : (head + 1) * HD] = spread[
                j * rows : (j + 1) * rows, g * HD : (g + 1) * HD
            ]

    def store(columns, product):
        out[:, columns] = (held[:, columns].astype(jnp.float32) + product).astype(jnp.bfloat16)

    matmul_into(store, rows_ref, matrix, 256)
    before = result[...] if tick else jnp.zeros_like(out)
    kept[...] = jnp.where(lax.axis_index("segment") == tick, out[...], before)
    if outs:
        by_destination(lax.axis_index("wide"), kept[...], own_rows, outs)


def join_kernel(count, *refs):
    blocks, out = refs[:count], refs[count]
    for j, block in enumerate(blocks):
        half = own_half(j, block)
        width = half.shape[1]
        columns = pl.ds(pl.multiple_of((lax.axis_index("wide") ^ j) * width, width), width)
        for m in range(out.shape[1]):
            local_rows = out.shape[2]
            out[0, m, :, columns] = half[m * local_rows : (m + 1) * local_rows, :]


def on_device_by_head(
    entering_hidden,
    row_adapter_index,
    lengths,
    input_norm_gain,
    query_matrix,
    key_matrix,
    value_matrix,
    output_matrix,
    adapter_down_maps,
    adapter_up_query,
    adapter_up_value,
    rotated_key_cache,
    cached_values,
):
    segments = lax.axis_size("segment")
    count = lax.axis_size("wide")
    micro, local_rows, width = entering_hidden.shape
    own_rows = micro * local_rows
    rows = own_rows * count
    capacity = CAP * micro
    part = width // count
    query_cols, key_cols = query_matrix.shape[2], key_matrix.shape[2]
    packed_cols = query_cols + 2 * key_cols
    span = rotated_key_cache.shape[3]

    query_weight = query_matrix[0]
    key_weight = key_matrix[0]
    value_weight = value_matrix[0]
    output_weight = output_matrix[0]
    down = adapter_down_maps[0]
    up_query = adapter_up_query[0]
    up_value = adapter_up_value[0]
    keys = rotated_key_cache[0].reshape(own_rows, span, -1)
    values = cached_values[0].reshape(own_rows, span, -1)
    gain = input_norm_gain
    half = HD // 2
    inverse = np.tile(rope_base ** (-np.arange(half) / half), 2).astype(np.float32)[None]

    def blocks_of(slots, columns):
        return [jax.ShapeDtypeStruct((2 * slots, columns), jnp.bfloat16)] * (count // 2)

    normed_shape = jax.ShapeDtypeStruct((rows, width), jnp.bfloat16)
    held_shape = jax.ShapeDtypeStruct((rows, part), jnp.bfloat16)
    ident_shape = jax.ShapeDtypeStruct((rows, HD), jnp.float32)
    correction_shapes = blocks_of(capacity, query_cols + key_cols)

    angle_shape = jax.ShapeDtypeStruct((GROUP * own_rows, HD), jnp.float32)
    entering, cosine, sine = call(
        open_kernel,
        [jax.ShapeDtypeStruct((rows, part + HD), jnp.bfloat16), angle_shape, angle_shape],
        [(entering_hidden, VMEM), (row_adapter_index, SMEM), (lengths, SMEM)]
        + [(jnp.asarray(inverse), VMEM)],
        name="open",
    )
    adapters = [down, up_query, up_value]
    projections = [query_weight, key_weight, value_weight]
    caches = [keys, values]
    outputs = [output_weight]
    held = ident = None
    result = None
    blocks = []
    for tick in range(segments):
        if tick == 0:
            weights = []

            def load_first():
                weights[:], token = loaded([*adapters, *projections], entering)
                return token

            chunks, _ = gathered(entering, load_first)
            adapters, projections = weights[:3], weights[3:]
            normed, held, ident, *found = call(
                functools.partial(enter_kernel, count, own_rows, capacity),
                [normed_shape, held_shape, ident_shape] + correction_shapes,
                [(c, VMEM) for c in chunks] + [(gain, VMEM)],
                [pltpu.VMEM((count * rows, part + HD), jnp.float32)],
                kept=adapters,
                name="enter",
            )
        else:
            held = lax.ppermute(
                held, "segment", [(s, (s + 1) % segments) for s in range(segments)]
            )
            chunks, _ = gathered(held)
            normed, *found = call(
                functools.partial(norm_kernel, count, capacity),
                [normed_shape] + correction_shapes,
                [(c, VMEM) for c in chunks] + [(ident, VMEM), (gain, VMEM)],
                kept=adapters,
                name="norm",
            )
        correction = found[: count // 2]

        def project():
            return call(
                project_kernel,
                [jax.ShapeDtypeStruct((rows, packed_cols), jnp.float32)],
                [(normed, VMEM)],
                kept=projections,
                cost=16,
                name="project",
            )[0]

        received, base = exchanged(correction, project)
        packed = call(
            functools.partial(correct_kernel, count, capacity, query_cols, key_cols),
            blocks_of(own_rows, packed_cols),
            [(base, VMEM), (ident, VMEM)] + [(r, VMEM) for r in received],
            name="correct",
        )

        def load_caches():
            caches[:], token = loaded(caches, packed[0])
            return token

        def load_output():
            outputs[:], token = loaded(outputs, attended)
            return token

        arrived, _ = exchanged(packed, None if tick else load_caches)
        attended, *_ = call(
            functools.partial(attend_kernel, count),
            [jax.ShapeDtypeStruct((GROUP * own_rows, KVH * HD), jnp.bfloat16)],
            [(lengths, SMEM)] + [(a, VMEM) for a in arrived]
            + [(cosine, VMEM), (sine, VMEM)],
            [
                pltpu.VMEM((GROUP * rows, span), jnp.float32),
                pltpu.VMEM((GROUP * rows, span), jnp.bfloat16),
            ],
            kept=caches,
            name="attend",
        )
        chunks, _ = gathered(attended, None if tick else load_output)
        last = tick == segments - 1
        held, result, *found = call(
            functools.partial(leave_kernel, count, own_rows, tick),
            [held_shape, held_shape] + (blocks_of(own_rows, part) if last else []),
            [(c, VMEM) for c in chunks]
            + [(held, VMEM)] + ([(result, VMEM)] if tick else []),
            [
                pltpu.VMEM((GROUP * rows, KVH * HD), jnp.bfloat16),
                pltpu.VMEM((rows, width), jnp.bfloat16),
            ],
            kept=outputs,
            name="leave",
        )
        blocks = found[:-1]
    (joined,) = call(
        functools.partial(join_kernel, count),
        [jax.ShapeDtypeStruct((1, micro, local_rows, width), jnp.bfloat16)],
        [(b, VMEM) for b in exchanged(blocks)[0]],
        name="join",
    )
    return joined


def passed_along(value, axis, steps):
    count = lax.axis_size(axis)
    leading, last = (max(0, -steps), min(count, count - steps))
    return lax.ppermute(value, axis, [(source, source + steps) for source in range(leading, last)])


def rotary(vectors, positions):
    half = vectors.shape[-1] // 2
    inverse = rope_base ** (-jnp.arange(half, dtype=jnp.float32) / half)
    angles = positions.astype(jnp.float32)[:, None] * inverse[None, :]
    cosine = jnp.cos(angles)[:, None, :]
    sine = jnp.sin(angles)[:, None, :]
    front = vectors[..., :half]
    back = vectors[..., half:]
    return jnp.concatenate([front * cosine - back * sine, back * cosine + front * sine], -1)


def attend(query_vector, new_key, fresh_value, positions, key_block, value_block):
    rows = query_vector.shape[0]
    group = HEADS // KVH
    rotated_rows = rotary(
        query_vector.astype(jnp.float32).reshape(rows, HEADS, HD), positions
    ).astype(jnp.bfloat16)
    rotated_rows = rotated_rows.reshape(rows, KVH, group, HD)
    self_key = rotary(new_key.astype(jnp.float32).reshape(rows, KVH, HD), positions).astype(
        jnp.bfloat16
    )
    keys_past = key_block.reshape(rows, -1, KVH, HD)
    values_past = value_block.reshape(rows, -1, KVH, HD)
    score_scale = HD ** (-0.5)
    past = (
        jnp.einsum("bkgd,bpkd->bkgp", rotated_rows, keys_past, preferred_element_type=jnp.float32)
        * score_scale
    )
    self_scores = (
        jnp.einsum("rice,rie->ric", rotated_rows, self_key, preferred_element_type=jnp.float32)
        * score_scale
    )
    valid = jnp.arange(keys_past.shape[1])[None, :] < positions[:, None]
    past = jnp.where(valid[:, None, None, :], past, -1e30)
    top = jnp.maximum(jnp.max(past, -1), self_scores)
    past_exp = jnp.where(valid[:, None, None, :], jnp.exp(past - top[..., None]), 0.0)
    own_exp = jnp.exp(self_scores - top)
    total = jnp.sum(past_exp, -1) + own_exp
    past_weights = (past_exp / total[..., None]).astype(jnp.bfloat16)
    own_weights = (own_exp / total).astype(jnp.bfloat16)
    mixed = jnp.einsum(
        "bkgp,bpkd->bkgd", past_weights, values_past, preferred_element_type=jnp.float32
    )
    mixed = (
        mixed
        + own_weights.astype(jnp.float32)[..., None]
        * fresh_value.reshape(rows, KVH, HD).astype(jnp.float32)[:, :, None, :]
    )
    return mixed.reshape(rows, HEADS * HD).astype(jnp.bfloat16)


def on_device(
    entering_hidden,
    row_adapter_index,
    lengths,
    input_norm_gain,
    query_matrix,
    key_matrix,
    value_matrix,
    output_matrix,
    adapter_down_maps,
    adapter_up_query,
    adapter_up_value,
    rotated_key_cache,
    cached_values,
):
    segments = lax.axis_size("segment")
    segment = lax.axis_index("segment")
    devices = lax.axis_size("wide")
    owner = lax.axis_index("wide")
    small_batch, local_rows, width = entering_hidden.shape
    listed = lax.all_gather(row_adapter_index, "wide", axis=1, tiled=True)[:, :, 0]
    groups = small_batch // small_batch
    capacity = CAP * small_batch
    kept_entries = adapter_down_maps.shape[1]
    adapters = kept_entries * devices
    mine = owner * kept_entries + jnp.arange(kept_entries)
    gain = input_norm_gain[0].astype(jnp.float32)
    query_cols = query_matrix.shape[2]
    key_cols = key_matrix.shape[2]
    passed = jnp.zeros((small_batch * local_rows, width), jnp.bfloat16)
    results = jnp.zeros((small_batch, local_rows, width), jnp.bfloat16)
    ticks = groups + segments - 1
    for tick in range(ticks):
        if tick < groups:
            fresh = entering_hidden.reshape(small_batch * local_rows, width)
        else:
            fresh = jnp.zeros_like(passed)
        rows = jnp.where(segment == 0, fresh, passed)
        index = tick - segment
        live = (index >= 0) & (index < groups)
        index = jnp.clip(index, 0, groups - 1)
        block_rows = rows.shape[0]
        idents = listed
        idents = idents.reshape(small_batch, devices, local_rows).transpose(1, 0, 2).reshape(-1)
        positions = lengths.reshape(-1)
        key_block = rotated_key_cache[0]
        key_block = key_block.reshape(block_rows, key_block.shape[2], key_block.shape[3])
        value_block = cached_values[0]
        value_block = value_block.reshape(block_rows, value_block.shape[2], value_block.shape[3])
        values = rows.astype(jnp.float32)
        normalized_rows = (
            values * lax.rsqrt(jnp.mean(values * values, 1, keepdims=True) + epsilon) * gain
        ).astype(jnp.bfloat16)
        gathered = lax.all_gather(normalized_rows, "wide", axis=0, tiled=True)
        total_rows = gathered.shape[0]
        matches = (idents[None, :] == mine[:, None]).astype(jnp.int32)
        ranks = jnp.cumsum(matches, 1) - 1
        chosen = (matches[:, None, :] == 1) & (
            ranks[:, None, :] == jnp.arange(capacity)[None, :, None]
        )
        chosen = chosen.reshape(kept_entries * capacity, total_rows)
        selected_rows = jnp.dot(
            chosen.astype(jnp.bfloat16), gathered, preferred_element_type=jnp.float32
        ).astype(jnp.bfloat16)
        selected_rows = selected_rows.reshape(kept_entries, capacity, width)
        reduced = jnp.einsum(
            "bpy,byf->bpf", selected_rows, adapter_down_maps[0], preferred_element_type=jnp.float32
        ).astype(jnp.bfloat16)
        member = (idents[:, None] == jnp.arange(adapters)[None, :]).astype(jnp.int32)
        order = jnp.sum(jnp.cumsum(member, 0) * member, 1) - 1
        slot = idents * capacity + order
        slot_table = slot[:, None] == jnp.arange(adapters * capacity)[None, :]
        query_slots = jnp.einsum(
            "acr,are->ace",
            reduced[..., :ADAPTER_RANK],
            adapter_up_query[0],
            preferred_element_type=jnp.float32,
        )
        value_slots = jnp.einsum(
            "acr,are->ace",
            reduced[..., ADAPTER_RANK:],
            adapter_up_value[0],
            preferred_element_type=jnp.float32,
        )
        joined = jnp.concatenate(
            [
                query_slots.reshape(kept_entries * capacity, devices, -1),
                value_slots.reshape(kept_entries * capacity, devices, -1),
            ],
            2,
        )
        received = lax.all_to_all(joined, "wide", split_axis=1, concat_axis=0, tiled=True)
        received = received.reshape(adapters * capacity, -1)
        placed = jnp.dot(slot_table.astype(jnp.float32), received, precision=lax.Precision.HIGHEST)
        query_adjustment = placed[:, :query_cols]
        value_adjustment = placed[:, query_cols:]
        query_vector = (
            jnp.dot(gathered, query_matrix[0], preferred_element_type=jnp.float32)
            + adapter_scale * query_adjustment
        ).astype(jnp.bfloat16)
        new_key = jnp.dot(gathered, key_matrix[0], preferred_element_type=jnp.float32).astype(
            jnp.bfloat16
        )
        fresh_value = (
            jnp.dot(gathered, value_matrix[0], preferred_element_type=jnp.float32)
            + adapter_scale * value_adjustment
        ).astype(jnp.bfloat16)
        packed = jnp.concatenate([query_vector, new_key, fresh_value], 1)
        arrived = lax.all_to_all(packed, "wide", split_axis=0, concat_axis=1, tiled=True).reshape(
            block_rows, devices, -1
        )
        query_rows_local = arrived[:, :, :query_cols].reshape(block_rows, -1)
        key_rows_local = arrived[:, :, query_cols : query_cols + key_cols].reshape(block_rows, -1)
        value_rows_local = arrived[:, :, query_cols + key_cols :].reshape(block_rows, -1)
        attended = attend(
            query_rows_local, key_rows_local, value_rows_local, positions, key_block, value_block
        )
        columns = jnp.dot(
            lax.all_gather(attended, "wide", axis=0, tiled=True),
            output_matrix[0],
            preferred_element_type=jnp.float32,
        )
        returned = lax.all_to_all(columns, "wide", split_axis=0, concat_axis=1, tiled=True)
        outcome = (values + returned).astype(jnp.bfloat16)
        updated = outcome.reshape(small_batch, local_rows, width)
        results = jnp.where(live, updated, results)
        if tick + 1 < ticks:
            passed = passed_along(outcome, "segment", 1)
    return results[None]


def solution(mesh):
    placed = (
        P(None, "wide", None),
        P(None, "wide", None),
        P(None, "wide"),
        P("segment", None),
        P("segment", None, "wide"),
        P("segment", None, "wide"),
        P("segment", None, "wide"),
        P("segment", None, "wide"),
        P("segment", "wide", None, None),
        P("segment", "wide", None, None),
        P("segment", "wide", None, None),
        P("segment", None, "wide", None, None),
        P("segment", None, "wide", None, None),
    )
    by_head = mesh.shape["wide"] == KVH
    return jax.shard_map(
        on_device_by_head if by_head else on_device,
        mesh=mesh,
        in_specs=placed,
        out_specs=P("segment", None, "wide", None),
        check_vma=False,
    )
```

```python
import functools

import jax
import jax.numpy as jnp
import numpy as np
from jax import lax
from jax.experimental import pallas as pl
from jax.experimental.pallas import tpu as pltpu
from jax.sharding import PartitionSpec as P

HEADS = 64
KVH = 8
HD = 128
ADAPTER_RANK = 64
CAP = 4


adapter_scale = 0.5
rope_base = 500000.0
epsilon = 1e-05

GROUP = HEADS // KVH
MIB = 1 << 20
VMEM = pl.BlockSpec(memory_space=pltpu.VMEM)
SMEM = pl.BlockSpec(memory_space=pltpu.SMEM)


def swapped(value, bits):
    count = lax.axis_size("wide")
    return lax.ppermute(value, "wide", [(i, i ^ bits) for i in range(count)])


def then(arrays, work):
    if work is None:
        return arrays, None
    done = work()
    arrays = pl.pallas_call(
        lambda *refs: None,
        out_shape=[jax.ShapeDtypeStruct(array.shape, array.dtype) for array in arrays],
        in_specs=[VMEM] * len(arrays) + [pl.BlockSpec(memory_space=pl.ANY)],
        out_specs=[VMEM] * len(arrays),
        input_output_aliases={i: i for i in range(len(arrays))},
        compiler_params=pltpu.CompilerParams(vmem_limit_bytes=MIB),
        name="then",
    )(*arrays, done)
    return arrays, done


def gathered(value, work=None):
    count = lax.axis_size("wide")
    far = [swapped(value, k) for k in range(2, count, 2)]
    far, done = then(far, work)
    found = [part for one in [value, *far] for part in (one, swapped(one, 1))]
    return found, done


def passed_on(value, s):
    count = lax.axis_size("wide")

    def shifted(bits):
        pairs = [(s * count + i, (s + 1) * count + (i ^ bits)) for i in range(count)]
        return lax.ppermute(value, ("segment", "wide"), pairs)

    far = [shifted(bits) for bits in range(0, count, 2)]
    return [part for one in far for part in (one, swapped(one, 1))]


def exchanged(blocks, work=None):
    far = [swapped(block, 2 * k) for k, block in enumerate(blocks) if k]
    far, done = then(far, work)
    return [blocks[0], *far], done


def resident(weight):
    return pltpu.with_memory_space_constraint(weight, pltpu.VMEM)


def call(body, out_shape, operands, scratch=(), limit=8, kept=(), through=(), cost=1, name=None):
    outs, count = list(out_shape), len(operands) + len(kept)
    inner = body
    if through:

        def inner(*refs):
            inputs = count + len(through)
            shown = inputs + len(outs)
            body(*refs[:count], *refs[inputs:shown], *refs[shown + len(through) :])

    found = pl.pallas_call(
        inner,
        out_shape=outs + [pltpu.VMEM(array.shape, array.dtype) for array in through],
        in_specs=[spec for _, spec in operands] + [VMEM] * (len(kept) + len(through)),
        out_specs=[VMEM] * (len(outs) + len(through)),
        input_output_aliases={count + i: len(outs) + i for i in range(len(through))},
        scratch_shapes=list(scratch),
        compiler_params=pltpu.CompilerParams(vmem_limit_bytes=limit * MIB),
        cost_estimate=pl.CostEstimate(flops=0, transcendentals=0, bytes_accessed=cost * MIB),
        name=name,
    )(*[array for array, _ in operands], *[resident(array) for array in [*kept, *through]])
    return list(found)


def load_kernel(sizes, plan, work, *refs):
    sources, small, outs, more = [], [], [], []
    refs = list(refs)
    for group, size in zip((sources, small, outs, more), sizes, strict=True):
        group.extend(refs[:size])
        del refs[:size]
    copies = [
        pltpu.make_async_copy(source, out, refs[0].at[i])
        for i, (source, out) in enumerate(plan(sources, outs))
    ]
    for copy in copies:
        copy.start()
    work(small, more)
    for copy in copies:
        copy.wait()


def loaded(sources, shapes, plan, copies, small, more, work):
    moved = sum(2 * int(np.prod(shape)) for shape in shapes)
    found = pl.pallas_call(
        functools.partial(
            load_kernel, (len(sources), len(small), len(shapes), len(more)), plan, work
        ),
        out_shape=[pltpu.VMEM(shape, jnp.bfloat16) for shape in shapes] + list(more),
        in_specs=[pl.BlockSpec(memory_space=pl.ANY)] * len(sources) + [spec for _, spec in small],
        out_specs=[VMEM] * (len(shapes) + len(more)),
        scratch_shapes=[pltpu.SemaphoreType.DMA((copies,))],
        compiler_params=pltpu.CompilerParams(vmem_limit_bytes=4 * MIB),
        cost_estimate=pl.CostEstimate(flops=0, transcendentals=0, bytes_accessed=moved),
        name="load",
    )(
        *[pltpu.with_memory_space_constraint(source, pltpu.HBM) for source in sources],
        *[array for array, _ in small],
    )
    return found[: len(shapes)], found[len(shapes) :]


TOKEN = jax.ShapeDtypeStruct((8, HD), jnp.float32)


def token_of(small, more):
    more[0][...] = small[0][:8, :HD].astype(jnp.float32)


def dot(left, right):
    return jnp.dot(left, right, preferred_element_type=jnp.float32)


def matmul_into(store, source, weights, step):
    first = 0
    for weight in weights:
        for i in range(0, weight.shape[1], step):
            product = dot(source[...], weight[:, i : i + step])
            store(slice(first + i, first + i + step), product)
        first += weight.shape[1]


def while_live(tick, body):
    def run(*refs):
        pl.when(lax.axis_index("segment") == tick)(lambda: body(*refs))

    return run


def by_part(owner, chunks, own_rows):
    count = len(chunks)
    parts = chunks[0].shape[0] // own_rows
    total = count * parts * own_rows
    stack = jnp.concatenate([chunk[...] for chunk in chunks], 0)
    out = lax.broadcasted_iota(jnp.int32, (total, total), 0)
    src = lax.broadcasted_iota(jnp.int32, (total, total), 1)
    rows = own_rows
    part_out = out // (rows * count)
    device_out = (out // rows) % count
    part_src = (src // rows) % parts
    device_src = (src // (rows * parts)) ^ owner
    hit = (part_out == part_src) & (device_out == device_src) & (out % rows == src % rows)
    return dot(jnp.where(hit, 1.0, 0.0).astype(jnp.bfloat16), stack)


def adapter_part(owner, ident, normed, adapter, outs, capacity):
    down, up_query, up_value = adapter
    rows = normed.shape[0]
    count = 2 * len(outs)
    low = dot(normed[...], down[0]).astype(jnp.bfloat16)
    place = lax.broadcasted_iota(jnp.int32, (rows, rows), 0)
    other = lax.broadcasted_iota(jnp.int32, (rows, rows), 1)
    mine = jnp.where(ident[:, :1] == owner.astype(jnp.float32), 1.0, 0.0)
    flat = jnp.where(place == other, mine, 0.0).astype(jnp.bfloat16)
    before = jnp.where(place < other, mine, 0.0).astype(jnp.bfloat16)
    ones = jnp.ones((capacity, rows), jnp.bfloat16)
    member = dot(ones, flat)
    rank = dot(ones, before)
    slot = lax.broadcasted_iota(jnp.int32, (capacity, rows), 0).astype(jnp.float32)
    chosen = jnp.where((member > 0.5) & (rank == slot), 1.0, 0.0).astype(jnp.bfloat16)
    picked = dot(chosen, low).astype(jnp.bfloat16)
    query_cols = up_query.shape[2] // count
    value_cols = up_value.shape[2] // count
    for j in range(count):
        out, there = outs[j // 2], owner ^ j
        slots = slice((j % 2) * capacity, (j % 2 + 1) * capacity)
        columns = pl.ds(pl.multiple_of(there * query_cols, query_cols), query_cols)
        for_query = dot(picked[:, :ADAPTER_RANK], up_query[0, :, columns]) * adapter_scale
        out[slots, :query_cols] = for_query.astype(jnp.bfloat16)
        columns = pl.ds(pl.multiple_of(there * value_cols, value_cols), value_cols)
        for_value = dot(picked[:, ADAPTER_RANK:], up_value[0, :, columns]) * adapter_scale
        out[slots, query_cols:] = for_value.astype(jnp.bfloat16)


def open_kernel(hidden, names, entering):
    micro, local_rows, width = hidden.shape
    own_rows = micro * local_rows
    part = entering.shape[1] - HD
    count = width // part
    rows = jnp.concatenate([hidden[m].astype(jnp.float32) for m in range(micro)], 0)
    entering[:, :part] = jnp.concatenate(
        [rows[:, i * part : (i + 1) * part] for i in range(count)], 0
    ).astype(jnp.bfloat16)
    row = lax.broadcasted_iota(jnp.int32, (count * own_rows, HD), 0) % own_rows
    name = jnp.zeros((count * own_rows, HD), jnp.float32)
    for r in range(own_rows):
        one = names[r // local_rows, 0, r % local_rows].astype(jnp.float32)
        name = jnp.where(row == r, one, name)
    entering[:, part:] = name.astype(jnp.bfloat16)


def row_lengths(lengths, near_lengths, shape, each=GROUP):
    micro, local_rows = lengths.shape
    own_rows = micro * local_rows
    row = lax.broadcasted_iota(jnp.int32, shape, 0) // each
    found = jnp.zeros(shape, jnp.int32)
    for i in range(2 * own_rows):
        source, r = (lengths, near_lengths)[i // own_rows], i % own_rows
        found = jnp.where(row == i, source[r // local_rows, r % local_rows], found)
    return found


def angle_work(small, more):
    lengths, near_lengths, inverse = small
    cosine, sine = more
    angles = row_lengths(lengths, near_lengths, cosine.shape).astype(jnp.float32) * inverse[...]
    front = lax.broadcasted_iota(jnp.int32, cosine.shape, 1) < HD // 2
    cosine[...] = jnp.cos(angles)
    sine[...] = jnp.where(front, -jnp.sin(angles), jnp.sin(angles))


def enter_kernel(count, own_rows, capacity, tick, *refs):
    chunks, rest = refs[:count], refs[count:]
    _, gain, *adapters, normed, held, ident = rest[:8]
    *correction, spread = rest[8:]
    owner = lax.axis_index("wide")
    rows = count * own_rows
    part = gain.shape[1] // count
    spread[...] = by_part(owner, chunks, own_rows)
    ident[...] = spread[:rows, part:]

    @pl.when(lax.axis_index("segment") == tick)
    def _():
        squares = jnp.zeros((rows, 1), jnp.float32)
        for i in range(count):
            block = spread[i * rows : (i + 1) * rows, :part]
            squares += jnp.sum(block * block, 1, keepdims=True)
        scale = lax.rsqrt(squares / gain.shape[1] + epsilon)
        for i in range(count):
            block = spread[i * rows : (i + 1) * rows, :part]
            columns = slice(i * part, (i + 1) * part)
            weight = gain[:, columns].astype(jnp.float32)
            normed[:, columns] = (block * scale * weight).astype(jnp.bfloat16)
        own = pl.ds(pl.multiple_of(owner * rows, rows), rows)
        held[...] = spread[own, :part].astype(jnp.bfloat16)
        adapter_part(owner, ident, normed, adapters, correction, capacity)


def norm_kernel(count, capacity, *refs):
    chunks, rest = refs[:count], refs[count:]
    ident, gain, *adapters, normed = rest[:6]
    correction = rest[6:]
    owner = lax.axis_index("wide")
    rows, part = chunks[0].shape
    squares = jnp.zeros((rows, 1), jnp.float32)
    for chunk in chunks:
        block = chunk[...].astype(jnp.float32)
        squares += jnp.sum(block * block, 1, keepdims=True)
    scale = lax.rsqrt(squares / gain.shape[1] + epsilon)
    for k, chunk in enumerate(chunks):
        columns = pl.ds(pl.multiple_of((owner ^ k) * part, part), part)
        weight = gain[:, columns].astype(jnp.float32)
        normed[:, columns] = (chunk[...].astype(jnp.float32) * scale * weight).astype(jnp.bfloat16)
    adapter_part(owner, ident, normed, adapters, correction, capacity)


def project_kernel(normed, query, query_rest, key, value, out):
    def store(columns, product):
        out[:, columns] = product

    matmul_into(store, normed, [query, query_rest], 256)
    narrow_into(normed, key, value, out)


def narrow_into(normed, key, value, out):
    narrow = key.shape[1]
    wide = out.shape[1] - 2 * narrow
    out[:, wide : wide + narrow] = dot(normed[...], key[...])
    out[:, wide + narrow :] = dot(normed[...], value[...])


def project_first_kernel(step, tick, normed, whole_query, query, key, value, out, query_rest, sems):
    first = query.shape[1]
    copies = []
    for i in range(query_rest.shape[1] // step):
        here = pl.ds(i * step, step)
        source = whole_query.at[:, pl.ds(first + i * step, step)]
        copies.append(pltpu.make_async_copy(source, query_rest.at[:, here], sems.at[i]))
    for copy in copies[:2]:
        copy.start()

    live = lax.axis_index("segment") == tick

    def store(columns, product):
        out[:, columns] = product

    @pl.when(live)
    def _():
        narrow_into(normed, key, value, out)
        matmul_into(store, normed, [query], 256)

    for i, copy in enumerate(copies):
        copy.wait()
        if i + 2 < len(copies):
            copies[i + 2].start()

        @pl.when(live)
        def _():
            here = slice(i * step, (i + 1) * step)
            target = slice(first + i * step, first + (i + 1) * step)
            out[:, target] = dot(normed[...], query_rest[:, here])


def received_rows(received):
    half = received[0].shape[0] // 2
    return [ref[(j % 2) * half : (j % 2 + 1) * half, :] for j, ref in enumerate(received)]


def correct_kernel(count, capacity, query_cols, key_cols, base, ident, *refs):
    received, outs = refs[:count], refs[count:]
    owner = lax.axis_index("wide")
    rows = base.shape[0]
    own_rows = rows // count
    slots = count * capacity
    place = lax.broadcasted_iota(jnp.int32, (rows, rows), 0)
    other = lax.broadcasted_iota(jnp.int32, (rows, rows), 1)
    own = ident[:, :1]
    flat = jnp.where(place == other, own, 0.0).astype(jnp.bfloat16)
    line = dot(jnp.ones((rows, rows), jnp.bfloat16), flat)
    rank = jnp.sum(jnp.where((own == line) & (other < place), 1.0, 0.0), 1, keepdims=True)
    slot = lax.broadcasted_iota(jnp.int32, (rows, slots), 1)
    source = ((slot // capacity) ^ owner).astype(jnp.float32)
    hit = (source == own) & ((slot % capacity).astype(jnp.float32) == rank)
    table = jnp.where(hit, 1.0, 0.0).astype(jnp.bfloat16)
    placed = dot(table, jnp.concatenate(received_rows(received), 0))
    whole = base[...]
    first = whole[:, :query_cols] + placed[:, :query_cols]
    middle = whole[:, query_cols : query_cols + key_cols]
    last = whole[:, query_cols + key_cols :] + placed[:, query_cols:]
    packed = jnp.concatenate([first, middle, last], 1).astype(jnp.bfloat16)
    by_destination(owner, packed, own_rows, outs)


def by_destination(owner, packed, own_rows, outs):
    rows = packed.shape[0]
    place = lax.broadcasted_iota(jnp.int32, (rows, rows), 0)
    other = lax.broadcasted_iota(jnp.int32, (rows, rows), 1)
    hit = (((place // own_rows) ^ owner) == other // own_rows) & (
        place % own_rows == other % own_rows
    )
    order = jnp.where(hit, 1.0, 0.0).astype(jnp.bfloat16)
    sorted_rows = dot(order, packed).astype(jnp.bfloat16)
    for k, out in enumerate(outs):
        out[...] = sorted_rows[k * 2 * own_rows : (k + 1) * 2 * own_rows, :]


def attend_kernel(chips, lengths, near_lengths, *refs):
    arrived, rest = refs[:chips], refs[chips:]
    cosine, sine, keys, values, near_keys, near_values, out, scores, weights = rest
    chip = lax.axis_index("wide") // 2
    own_rows, span = keys.shape[:2]
    chip_rows = 2 * own_rows
    rows = GROUP * chip_rows
    cos, sin = cosine[...], sine[...]
    position = lax.broadcasted_iota(jnp.int32, (2 * rows, span), 1)
    valid = position < row_lengths(lengths, near_lengths, (2 * rows, span), 2 * GROUP)
    score_scale = HD ** (-0.5)

    def turned(vectors):
        return vectors * cos + pltpu.roll(vectors, HD // 2, 1) * sin

    def rounded(vectors):
        return vectors.astype(jnp.bfloat16).astype(jnp.float32)

    pieces = []
    for ref in arrived:
        packed = ref[...].astype(jnp.float32)
        heads = [packed[:, i * HD : (i + 1) * HD] for i in range(GROUP)]
        fresh = [packed[:, GROUP * HD :]] * GROUP
        pieces += [jnp.concatenate(heads, 0), jnp.concatenate(fresh, 0)]
    out_row = lax.broadcasted_iota(jnp.int32, (rows, rows), 0)
    src_row = lax.broadcasted_iota(jnp.int32, (rows, rows), 1)
    same = (out_row // GROUP == src_row % chip_rows) & (out_row % GROUP == src_row // chip_rows)
    order = jnp.where(same, 1.0, 0.0).astype(jnp.bfloat16)
    sorted_rows = dot(order, jnp.concatenate(pieces, 1).astype(jnp.bfloat16))
    band = 2 * GROUP

    def woven(one, two):
        bands = [slice(r * GROUP, (r + 1) * GROUP) for r in range(chip_rows)]
        return jnp.concatenate([part[rows_of] for rows_of in bands for part in (one, two)], 0)

    def pair_lanes(p):
        return pl.ds(pl.multiple_of((chip // 2 ^ p) * 2 * HD, 2 * HD), 2 * HD)

    even = chip % 2 == 0
    zero = jnp.zeros((rows, HD), jnp.float32)
    pairs = range(chips // 2)
    fresh = []
    for p in pairs:
        wide, own, new_values = [], [], []
        for n in range(2):
            piece = sorted_rows[:, (2 * p + n) * 3 * HD : (2 * p + n + 1) * 3 * HD]
            query = rounded(turned(piece[:, :HD]))
            new_key = rounded(turned(piece[:, HD : 2 * HD]))
            own.append(jnp.sum(query * new_key, 1, keepdims=True) * score_scale)
            new_values.append(piece[:, 2 * HD :])
            left = even if n == 0 else jnp.logical_not(even)
            wide.append(
                jnp.concatenate([jnp.where(left, query, zero), jnp.where(left, zero, query)], 1)
            )
        fresh.append((woven(*own), woven(*new_values)))
        wide = woven(*wide).astype(jnp.bfloat16)
        for r in range(chip_rows):
            first = (p * chip_rows + r) * band
            scores[first : first + band, :] = lax.dot_general(
                wide[r * band : (r + 1) * band, :],
                (keys, near_keys)[r // own_rows][r % own_rows, :, pair_lanes(p)],
                (((1,), (1,)), ((), ())),
                preferred_element_type=jnp.float32,
            )
    parts = []
    for p, (own, new_value) in enumerate(fresh):
        here = slice(p * 2 * rows, (p + 1) * 2 * rows)
        found = jnp.where(valid, scores[here, :] * score_scale, -1e30)
        top = jnp.maximum(jnp.max(found, 1, keepdims=True), own)
        past = jnp.where(valid, jnp.exp(found - top), 0.0)
        own = jnp.exp(own - top)
        total = jnp.sum(past, 1, keepdims=True) + own
        weights[here, :] = (past / total).astype(jnp.bfloat16)
        parts.append(rounded(own / total) * new_value)
    for p, own_part in enumerate(parts):
        mixed = []
        for r in range(chip_rows):
            first = (p * chip_rows + r) * band
            found = dot(
                weights[first : first + band, :],
                (values, near_values)[r // own_rows][r % own_rows, :, pair_lanes(p)],
            )
            mine = own_part[r * band : (r + 1) * band, :]
            one = jnp.where(even, found[:GROUP, :HD], found[:GROUP, HD:]) + mine[:GROUP]
            two = jnp.where(even, found[GROUP:, HD:], found[GROUP:, :HD]) + mine[GROUP:]
            both = [jnp.where(even, one, two), jnp.where(even, two, one)]
            mixed.append(jnp.concatenate(both, 1))
        out[:, pair_lanes(p)] = jnp.concatenate(mixed, 0).astype(jnp.bfloat16)


def attended_rows(owner, chunks, own_rows, rows_ref):
    count = len(chunks)
    chips = count // 2
    rows = own_rows * count
    total = rows * GROUP
    out = lax.broadcasted_iota(jnp.int32, (total, total), 0)
    src = lax.broadcasted_iota(jnp.int32, (total, total), 1)
    device_out = (out // own_rows) % count
    chip_rows = 2 * own_rows
    row_src = (src // GROUP) % chip_rows
    near = (out // rows == src % GROUP) & (out % own_rows == row_src % own_rows)
    for core in range(2):
        stack = jnp.concatenate([chunks[2 * k + core][...] for k in range(chips)], 0)
        device_src = owner ^ (2 * (src // (GROUP * chip_rows)) + core) ^ (row_src // own_rows)
        hit = near & (device_out == device_src)
        spread = dot(jnp.where(hit, 1.0, 0.0).astype(jnp.bfloat16), stack).astype(jnp.bfloat16)
        first = (owner ^ core) % 2
        for i in range(chips):
            for j in range(GROUP):
                head = (2 * i + first) * GROUP + j
                rows_ref[:, pl.ds(pl.multiple_of(head * HD, HD), HD)] = spread[
                    j * rows : (j + 1) * rows, i * HD : (i + 1) * HD
                ]


def leave_kernel(count, own_rows, tick, *refs):
    chunks, rest = refs[:count], refs[count:]
    held, result = rest[0], rest[1] if tick else None
    matrix, matrix_rest, out, kept, *outs, rows_ref = rest[2 if tick else 1 :]
    kept[...] = result[...] if tick else jnp.zeros_like(kept)

    @pl.when(lax.axis_index("segment") == tick)
    def _():
        attended_rows(lax.axis_index("wide"), chunks, own_rows, rows_ref)

        def store(columns, product):
            total = held[:, columns].astype(jnp.float32) + product
            out[:, columns] = total.astype(jnp.bfloat16)
            kept[:, columns] = total.astype(jnp.bfloat16)

        matmul_into(store, rows_ref, [matrix, matrix_rest], 256)

    if outs:
        by_destination(lax.axis_index("wide"), kept[...], own_rows, outs)


def join_kernel(count, *refs):
    blocks, out = refs[:count], refs[count]
    for j, block in enumerate(blocks):
        rows = block.shape[0] // 2
        half = block[(j % 2) * rows : (j % 2 + 1) * rows, :]
        width = half.shape[1]
        columns = pl.ds(pl.multiple_of((lax.axis_index("wide") ^ j) * width, width), width)
        for m in range(out.shape[1]):
            local_rows = out.shape[2]
            out[0, m, :, columns] = half[m * local_rows : (m + 1) * local_rows, :]


def on_device_by_head(
    entering_hidden,
    row_adapter_index,
    lengths,
    input_norm_gain,
    query_matrix,
    key_matrix,
    value_matrix,
    output_matrix,
    adapter_down_maps,
    adapter_up_query,
    adapter_up_value,
    rotated_key_cache,
    cached_values,
):
    segments = lax.axis_size("segment")
    count = lax.axis_size("wide")
    micro, local_rows, width = entering_hidden.shape
    own_rows = micro * local_rows
    rows = own_rows * count
    capacity = CAP * micro
    part = width // count
    query_cols, key_cols = query_matrix.shape[2], key_matrix.shape[2]
    packed_cols = query_cols + 2 * key_cols
    span = rotated_key_cache.shape[3]

    chips = count // 2
    head_lanes = chips * HD
    query_weight = query_matrix[0]
    output_weight = output_matrix[0]
    adapters = [adapter_down_maps[0], adapter_up_query[0], adapter_up_value[0]]
    caches = [cache[0].reshape(own_rows, span, -1) for cache in (rotated_key_cache, cached_values)]
    near_lengths = swapped(lengths, 1)
    gain = input_norm_gain
    half = HD // 2
    inverse = np.tile(rope_base ** (-np.arange(half) / half), 2).astype(np.float32)[None]

    def blocks_of(slots, columns):
        return [jax.ShapeDtypeStruct((2 * slots, columns), jnp.bfloat16)] * chips

    normed_shape = jax.ShapeDtypeStruct((rows, width), jnp.bfloat16)
    held_shape = jax.ShapeDtypeStruct((rows, part), jnp.bfloat16)
    ident_shape = jax.ShapeDtypeStruct((rows, HD), jnp.float32)
    base_shape = jax.ShapeDtypeStruct((rows, packed_cols), jnp.float32)
    angle_shape = jax.ShapeDtypeStruct((GROUP * 2 * own_rows, HD), jnp.float32)
    correction_shapes = blocks_of(capacity, query_cols + key_cols)
    query_first = query_cols // 4
    output_first = part // 2

    (entering,) = call(
        open_kernel,
        [jax.ShapeDtypeStruct((rows, part + HD), jnp.bfloat16)],
        [(entering_hidden, VMEM), (row_adapter_index.transpose(0, 2, 1), SMEM)],
        name="open",
    )
    projections, output_parts, halves, angles = [], [], [], []
    held = ident = None
    result = None
    blocks = []
    for tick in range(segments):
        if tick == 0:

            def load_first():
                sources = [*adapters, key_matrix[0], value_matrix[0], query_weight, *caches]
                small = [(entering, VMEM)]
                shape = (own_rows, span, head_lanes)
                shapes = [source.shape for source in sources[:5]] + [(width, query_first)]
                shapes += [shape] * 4

                def plan(sources, outs):
                    pairs = list(zip(sources[:5], outs[:5]))
                    pairs.append((sources[5].at[:, :query_first], outs[5]))
                    core = lax.axis_index("wide") % 2
                    for n in range(4):
                        for i in range(chips):
                            head = 2 * i + (core if n < 2 else 1 - core)
                            there = pl.ds(pl.multiple_of(head * HD, HD), HD)
                            source = sources[6 + n % 2].at[:, :, there]
                            pairs.append((source, outs[6 + n].at[:, :, pl.ds(i * HD, HD)]))
                    return pairs

                found, (token,) = loaded(
                    sources, shapes, plan, 6 + 4 * chips, small, [TOKEN], token_of
                )
                adapters[:], projections[:] = found[:3], [found[5], found[3], found[4]]
                halves[:] = found[6:]
                return token

            chunks, _ = gathered(entering, load_first)
            normed, held, ident, *found = call(
                functools.partial(enter_kernel, count, own_rows, capacity, tick),
                [normed_shape, held_shape, ident_shape] + correction_shapes,
                [(c, VMEM) for c in chunks]
                + [(near_lengths, pl.BlockSpec(memory_space=pl.ANY)), (gain, VMEM)],
                [pltpu.VMEM((count * rows, part + HD), jnp.float32)],
                kept=adapters,
                through=halves[2:],
                name="enter",
            )
            halves[2:] = [swapped(array, 1) for array in found[chips:]]
        else:
            chunks = passed_on(held, tick - 1)
            held = chunks[0]
            normed, *found = call(
                while_live(tick, functools.partial(norm_kernel, count, capacity)),
                [normed_shape] + correction_shapes,
                [(c, VMEM) for c in chunks] + [(ident, VMEM), (gain, VMEM)],
                kept=adapters,
                name="norm",
            )
        correction = found[:chips]

        def project():
            return call(
                while_live(tick, project_kernel),
                [base_shape],
                [(normed, VMEM)],
                kept=projections,
                cost=16,
                name="project",
            )[0]

        def project_first():
            base, rest = pl.pallas_call(
                functools.partial(project_first_kernel, query_first, tick),
                out_shape=[base_shape, pltpu.VMEM((width, query_cols - query_first), jnp.bfloat16)],
                in_specs=[VMEM, pl.BlockSpec(memory_space=pl.ANY)] + [VMEM] * 3,
                out_specs=[VMEM, VMEM],
                scratch_shapes=[pltpu.SemaphoreType.DMA((query_cols // query_first - 1,))],
                compiler_params=pltpu.CompilerParams(vmem_limit_bytes=8 * MIB),
                cost_estimate=pl.CostEstimate(
                    flops=0, transcendentals=0, bytes_accessed=16 * MIB
                ),
                name="project",
            )(
                normed,
                pltpu.with_memory_space_constraint(query_weight, pltpu.HBM),
                *[resident(array) for array in projections],
            )
            projections[1:1] = [rest]
            return base

        received, base = exchanged(correction, project if tick else project_first)
        received = [part for one in received for part in (one, swapped(one, 1))]
        packed = call(
            while_live(
                tick, functools.partial(correct_kernel, count, capacity, query_cols, key_cols)
            ),
            blocks_of(own_rows, packed_cols),
            [(base, VMEM), (ident, VMEM)] + [(r, VMEM) for r in received],
            name="correct",
        )

        def load_part():
            small = [(lengths, SMEM), (near_lengths, SMEM), (jnp.asarray(inverse), VMEM)]
            found, angles[:] = loaded(
                [output_weight],
                [(width, output_first)],
                lambda sources, outs: [(sources[0].at[:, :output_first], outs[0])],
                1,
                small,
                [angle_shape, angle_shape],
                angle_work,
            )
            output_parts[:] = found
            return angles[0]

        def load_output():
            found, (token,) = loaded(
                [output_weight],
                [(width, part - output_first)],
                lambda sources, outs: [(sources[0].at[:, output_first:], outs[0])],
                1,
                [(attended, VMEM)],
                [TOKEN],
                token_of,
            )
            output_parts[1:] = found
            return token

        arrived, _ = exchanged(packed, None if tick else load_part)
        attended, *_ = call(
            while_live(tick, functools.partial(attend_kernel, chips)),
            [jax.ShapeDtypeStruct((GROUP * 2 * own_rows, head_lanes), jnp.bfloat16)],
            [(lengths, SMEM), (near_lengths, SMEM)]
            + [(a, VMEM) for a in [*arrived, *angles]],
            [
                pltpu.VMEM((chips * GROUP * 2 * own_rows, span), jnp.float32),
                pltpu.VMEM((chips * GROUP * 2 * own_rows, span), jnp.bfloat16),
            ],
            kept=halves,
            name="attend",
        )
        chunks, _ = gathered(attended, None if tick else load_output)
        last = tick == segments - 1
        held, result, *found = call(
            functools.partial(leave_kernel, count, own_rows, tick),
            [held_shape, held_shape] + (blocks_of(own_rows, part) if last else []),
            [(c, VMEM) for c in chunks]
            + [(held, VMEM)] + ([(result, VMEM)] if tick else []),
            [pltpu.VMEM((rows, width), jnp.bfloat16)],
            kept=output_parts,
            name="leave",
        )
        blocks = found
    far, _ = exchanged(blocks)
    far = [part for one in far for part in (one, swapped(one, 1))]
    (joined,) = call(
        functools.partial(join_kernel, count),
        [jax.ShapeDtypeStruct((1, micro, local_rows, width), jnp.bfloat16)],
        [(one, VMEM) for one in far],
        name="join",
    )
    return joined


def passed_along(value, axis, steps):
    count = lax.axis_size(axis)
    leading, last = (max(0, -steps), min(count, count - steps))
    return lax.ppermute(value, axis, [(source, source + steps) for source in range(leading, last)])


def rotary(vectors, positions):
    half = vectors.shape[-1] // 2
    inverse = rope_base ** (-jnp.arange(half, dtype=jnp.float32) / half)
    angles = positions.astype(jnp.float32)[:, None] * inverse[None, :]
    cosine = jnp.cos(angles)[:, None, :]
    sine = jnp.sin(angles)[:, None, :]
    front = vectors[..., :half]
    back = vectors[..., half:]
    return jnp.concatenate([front * cosine - back * sine, back * cosine + front * sine], -1)


def attend(query_vector, new_key, fresh_value, positions, key_block, value_block):
    rows = query_vector.shape[0]
    group = HEADS // KVH
    rotated_rows = rotary(
        query_vector.astype(jnp.float32).reshape(rows, HEADS, HD), positions
    ).astype(jnp.bfloat16)
    rotated_rows = rotated_rows.reshape(rows, KVH, group, HD)
    self_key = rotary(new_key.astype(jnp.float32).reshape(rows, KVH, HD), positions).astype(
        jnp.bfloat16
    )
    keys_past = key_block.reshape(rows, -1, KVH, HD)
    values_past = value_block.reshape(rows, -1, KVH, HD)
    score_scale = HD ** (-0.5)
    past = (
        jnp.einsum("bkgd,bpkd->bkgp", rotated_rows, keys_past, preferred_element_type=jnp.float32)
        * score_scale
    )
    self_scores = (
        jnp.einsum("rice,rie->ric", rotated_rows, self_key, preferred_element_type=jnp.float32)
        * score_scale
    )
    valid = jnp.arange(keys_past.shape[1])[None, :] < positions[:, None]
    past = jnp.where(valid[:, None, None, :], past, -1e30)
    top = jnp.maximum(jnp.max(past, -1), self_scores)
    past_exp = jnp.where(valid[:, None, None, :], jnp.exp(past - top[..., None]), 0.0)
    own_exp = jnp.exp(self_scores - top)
    total = jnp.sum(past_exp, -1) + own_exp
    past_weights = (past_exp / total[..., None]).astype(jnp.bfloat16)
    own_weights = (own_exp / total).astype(jnp.bfloat16)
    mixed = jnp.einsum(
        "bkgp,bpkd->bkgd", past_weights, values_past, preferred_element_type=jnp.float32
    )
    mixed = (
        mixed
        + own_weights.astype(jnp.float32)[..., None]
        * fresh_value.reshape(rows, KVH, HD).astype(jnp.float32)[:, :, None, :]
    )
    return mixed.reshape(rows, HEADS * HD).astype(jnp.bfloat16)


def on_device(
    entering_hidden,
    row_adapter_index,
    lengths,
    input_norm_gain,
    query_matrix,
    key_matrix,
    value_matrix,
    output_matrix,
    adapter_down_maps,
    adapter_up_query,
    adapter_up_value,
    rotated_key_cache,
    cached_values,
):
    segments = lax.axis_size("segment")
    segment = lax.axis_index("segment")
    devices = lax.axis_size("wide")
    owner = lax.axis_index("wide")
    small_batch, local_rows, width = entering_hidden.shape
    listed = lax.all_gather(row_adapter_index, "wide", axis=1, tiled=True)[:, :, 0]
    groups = small_batch // small_batch
    capacity = CAP * small_batch
    kept_entries = adapter_down_maps.shape[1]
    adapters = kept_entries * devices
    mine = owner * kept_entries + jnp.arange(kept_entries)
    gain = input_norm_gain[0].astype(jnp.float32)
    query_cols = query_matrix.shape[2]
    key_cols = key_matrix.shape[2]
    passed = jnp.zeros((small_batch * local_rows, width), jnp.bfloat16)
    results = jnp.zeros((small_batch, local_rows, width), jnp.bfloat16)
    ticks = groups + segments - 1
    for tick in range(ticks):
        if tick < groups:
            fresh = entering_hidden.reshape(small_batch * local_rows, width)
        else:
            fresh = jnp.zeros_like(passed)
        rows = jnp.where(segment == 0, fresh, passed)
        index = tick - segment
        live = (index >= 0) & (index < groups)
        index = jnp.clip(index, 0, groups - 1)
        block_rows = rows.shape[0]
        idents = listed
        idents = idents.reshape(small_batch, devices, local_rows).transpose(1, 0, 2).reshape(-1)
        positions = lengths.reshape(-1)
        key_block = rotated_key_cache[0]
        key_block = key_block.reshape(block_rows, key_block.shape[2], key_block.shape[3])
        value_block = cached_values[0]
        value_block = value_block.reshape(block_rows, value_block.shape[2], value_block.shape[3])
        values = rows.astype(jnp.float32)
        normalized_rows = (
            values * lax.rsqrt(jnp.mean(values * values, 1, keepdims=True) + epsilon) * gain
        ).astype(jnp.bfloat16)
        gathered = lax.all_gather(normalized_rows, "wide", axis=0, tiled=True)
        total_rows = gathered.shape[0]
        matches = (idents[None, :] == mine[:, None]).astype(jnp.int32)
        ranks = jnp.cumsum(matches, 1) - 1
        chosen = (matches[:, None, :] == 1) & (
            ranks[:, None, :] == jnp.arange(capacity)[None, :, None]
        )
        chosen = chosen.reshape(kept_entries * capacity, total_rows)
        selected_rows = jnp.dot(
            chosen.astype(jnp.bfloat16), gathered, preferred_element_type=jnp.float32
        ).astype(jnp.bfloat16)
        selected_rows = selected_rows.reshape(kept_entries, capacity, width)
        reduced = jnp.einsum(
            "bpy,byf->bpf", selected_rows, adapter_down_maps[0], preferred_element_type=jnp.float32
        ).astype(jnp.bfloat16)
        member = (idents[:, None] == jnp.arange(adapters)[None, :]).astype(jnp.int32)
        order = jnp.sum(jnp.cumsum(member, 0) * member, 1) - 1
        slot = idents * capacity + order
        slot_table = slot[:, None] == jnp.arange(adapters * capacity)[None, :]
        query_slots = jnp.einsum(
            "acr,are->ace",
            reduced[..., :ADAPTER_RANK],
            adapter_up_query[0],
            preferred_element_type=jnp.float32,
        )
        value_slots = jnp.einsum(
            "acr,are->ace",
            reduced[..., ADAPTER_RANK:],
            adapter_up_value[0],
            preferred_element_type=jnp.float32,
        )
        joined = jnp.concatenate(
            [
                query_slots.reshape(kept_entries * capacity, devices, -1),
                value_slots.reshape(kept_entries * capacity, devices, -1),
            ],
            2,
        )
        received = lax.all_to_all(joined, "wide", split_axis=1, concat_axis=0, tiled=True)
        received = received.reshape(adapters * capacity, -1)
        placed = jnp.dot(slot_table.astype(jnp.float32), received, precision=lax.Precision.HIGHEST)
        query_adjustment = placed[:, :query_cols]
        value_adjustment = placed[:, query_cols:]
        query_vector = (
            jnp.dot(gathered, query_matrix[0], preferred_element_type=jnp.float32)
            + adapter_scale * query_adjustment
        ).astype(jnp.bfloat16)
        new_key = jnp.dot(gathered, key_matrix[0], preferred_element_type=jnp.float32).astype(
            jnp.bfloat16
        )
        fresh_value = (
            jnp.dot(gathered, value_matrix[0], preferred_element_type=jnp.float32)
            + adapter_scale * value_adjustment
        ).astype(jnp.bfloat16)
        packed = jnp.concatenate([query_vector, new_key, fresh_value], 1)
        arrived = lax.all_to_all(packed, "wide", split_axis=0, concat_axis=1, tiled=True).reshape(
            block_rows, devices, -1
        )
        query_rows_local = arrived[:, :, :query_cols].reshape(block_rows, -1)
        key_rows_local = arrived[:, :, query_cols : query_cols + key_cols].reshape(block_rows, -1)
        value_rows_local = arrived[:, :, query_cols + key_cols :].reshape(block_rows, -1)
        attended = attend(
            query_rows_local, key_rows_local, value_rows_local, positions, key_block, value_block
        )
        columns = jnp.dot(
            lax.all_gather(attended, "wide", axis=0, tiled=True),
            output_matrix[0],
            preferred_element_type=jnp.float32,
        )
        returned = lax.all_to_all(columns, "wide", split_axis=0, concat_axis=1, tiled=True)
        outcome = (values + returned).astype(jnp.bfloat16)
        updated = outcome.reshape(small_batch, local_rows, width)
        results = jnp.where(live, updated, results)
        if tick + 1 < ticks:
            passed = passed_along(outcome, "segment", 1)
    return results[None]


def solution(mesh):
    placed = (
        P(None, "wide", None),
        P(None, "wide", None),
        P(None, "wide"),
        P("segment", None),
        P("segment", None, "wide"),
        P("segment", None, "wide"),
        P("segment", None, "wide"),
        P("segment", None, "wide"),
        P("segment", "wide", None, None),
        P("segment", "wide", None, None),
        P("segment", "wide", None, None),
        P("segment", None, "wide", None, None),
        P("segment", None, "wide", None, None),
    )
    by_head = mesh.shape["wide"] == KVH
    return jax.shard_map(
        on_device_by_head if by_head else on_device,
        mesh=mesh,
        in_specs=placed,
        out_specs=P("segment", None, "wide", None),
        check_vma=False,
    )
```

```python
import functools

import jax
import jax.numpy as jnp
import numpy as np
from jax import lax
from jax.experimental import pallas as pl
from jax.experimental.pallas import tpu as pltpu
from jax.sharding import PartitionSpec as P

HEADS = 64
KVH = 8
HD = 128
ADAPTER_RANK = 64
CAP = 4


adapter_scale = 0.5
rope_base = 500000.0
epsilon = 1e-05

GROUP = HEADS // KVH
MIB = 1 << 20
STEP = 256
VMEM = pl.BlockSpec(memory_space=pltpu.VMEM)
SMEM = pl.BlockSpec(memory_space=pltpu.SMEM)


def swapped(value, bits):
    count = lax.axis_size("wide")
    return lax.ppermute(value, "wide", [(i, i ^ bits) for i in range(count)])


def then(arrays, work):
    if work is None:
        return arrays, None
    done = work()
    arrays = pl.pallas_call(
        lambda *refs: None,
        out_shape=[jax.ShapeDtypeStruct(array.shape, array.dtype) for array in arrays],
        in_specs=[VMEM] * len(arrays) + [pl.BlockSpec(memory_space=pl.ANY)],
        out_specs=[VMEM] * len(arrays),
        input_output_aliases={i: i for i in range(len(arrays))},
        compiler_params=pltpu.CompilerParams(vmem_limit_bytes=MIB),
        name="then",
    )(*arrays, done)
    return arrays, done


def gathered(value, work=None):
    count = lax.axis_size("wide")
    far = [swapped(value, k) for k in range(2, count, 2)]
    far, done = then(far, work)
    found = [part for one in [value, *far] for part in (one, swapped(one, 1))]
    return found, done


def passed_on(value, s):
    count = lax.axis_size("wide")

    def shifted(bits):
        pairs = [(s * count + i, (s + 1) * count + (i ^ bits)) for i in range(count)]
        return lax.ppermute(value, ("segment", "wide"), pairs)

    far = [shifted(bits) for bits in range(0, count, 2)]
    return [part for one in far for part in (one, swapped(one, 1))]


def exchanged(blocks, work=None):
    far = [swapped(block, 2 * k) for k, block in enumerate(blocks) if k]
    far, done = then(far, work)
    return [blocks[0], *far], done


def resident(weight):
    return pltpu.with_memory_space_constraint(weight, pltpu.VMEM)


def call(body, out_shape, operands, scratch=(), limit=8, kept=(), through=(), cost=1, name=None):
    outs, count = list(out_shape), len(operands) + len(kept)
    inner = body
    if through:

        def inner(*refs):
            inputs = count + len(through)
            shown = inputs + len(outs)
            body(*refs[:count], *refs[inputs:shown], *refs[shown + len(through) :])

    found = pl.pallas_call(
        inner,
        out_shape=outs + [pltpu.VMEM(array.shape, array.dtype) for array in through],
        in_specs=[spec for _, spec in operands] + [VMEM] * (len(kept) + len(through)),
        out_specs=[VMEM] * (len(outs) + len(through)),
        input_output_aliases={count + i: len(outs) + i for i in range(len(through))},
        scratch_shapes=list(scratch),
        compiler_params=pltpu.CompilerParams(vmem_limit_bytes=limit * MIB),
        cost_estimate=pl.CostEstimate(flops=0, transcendentals=0, bytes_accessed=cost * MIB),
        name=name,
    )(*[array for array, _ in operands], *[resident(array) for array in [*kept, *through]])
    return list(found)


def load_kernel(sizes, plan, work, *refs):
    sources, small, outs, more = [], [], [], []
    refs = list(refs)
    for group, size in zip((sources, small, outs, more), sizes, strict=True):
        group.extend(refs[:size])
        del refs[:size]
    copies = [
        pltpu.make_async_copy(source, out, refs[0].at[i])
        for i, (source, out) in enumerate(plan(sources, outs))
    ]
    for copy in copies:
        copy.start()
    work(small, more)
    for copy in copies:
        copy.wait()


def loaded(sources, shapes, plan, copies, small, more, work):
    moved = sum(2 * int(np.prod(shape)) for shape in shapes)
    found = pl.pallas_call(
        functools.partial(
            load_kernel, (len(sources), len(small), len(shapes), len(more)), plan, work
        ),
        out_shape=[pltpu.VMEM(shape, jnp.bfloat16) for shape in shapes] + list(more),
        in_specs=[pl.BlockSpec(memory_space=pl.ANY)] * len(sources) + [spec for _, spec in small],
        out_specs=[VMEM] * (len(shapes) + len(more)),
        scratch_shapes=[pltpu.SemaphoreType.DMA((copies,))],
        compiler_params=pltpu.CompilerParams(vmem_limit_bytes=4 * MIB),
        cost_estimate=pl.CostEstimate(flops=0, transcendentals=0, bytes_accessed=moved),
        name="load",
    )(
        *[pltpu.with_memory_space_constraint(source, pltpu.HBM) for source in sources],
        *[array for array, _ in small],
    )
    return found[: len(shapes)], found[len(shapes) :]


TOKEN = jax.ShapeDtypeStruct((8, HD), jnp.float32)


def token_of(small, more):
    more[0][...] = small[0][:8, :HD].astype(jnp.float32)


def dot(left, right):
    return jnp.dot(left, right, preferred_element_type=jnp.float32)


def matmul_into(store, source, weights, step):
    first = 0
    for weight in weights:
        width = min(step, weight.shape[1])

        def one(i, carry, weight=weight, first=first, width=width):
            columns = pl.ds(pl.multiple_of(i * width, width), width)
            target = pl.ds(pl.multiple_of(first + i * width, width), width)
            store(target, dot(source[...], weight[:, columns]))
            return carry

        lax.fori_loop(0, weight.shape[1] // width, one, 0)
        first += weight.shape[1]


def while_live(tick, body):
    def run(*refs):
        pl.when(lax.axis_index("segment") == tick)(lambda: body(*refs))

    return run


def by_part(owner, chunks, own_rows):
    count = len(chunks)
    parts = chunks[0].shape[0] // own_rows
    total = count * parts * own_rows
    stack = jnp.concatenate([chunk[...] for chunk in chunks], 0)
    out = lax.broadcasted_iota(jnp.int32, (total, total), 0)
    src = lax.broadcasted_iota(jnp.int32, (total, total), 1)
    rows = own_rows
    part_out = out // (rows * count)
    device_out = (out // rows) % count
    part_src = (src // rows) % parts
    device_src = (src // (rows * parts)) ^ owner
    hit = (part_out == part_src) & (device_out == device_src) & (out % rows == src % rows)
    return dot(jnp.where(hit, 1.0, 0.0).astype(jnp.bfloat16), stack)


def adapter_part(owner, ident, normed, adapter, outs, capacity):
    down, up_query, up_value = adapter
    rows = normed.shape[0]
    count = 2 * len(outs)
    low = dot(normed[...], down[0]).astype(jnp.bfloat16)
    place = lax.broadcasted_iota(jnp.int32, (rows, rows), 0)
    other = lax.broadcasted_iota(jnp.int32, (rows, rows), 1)
    mine = jnp.where(ident[:, :1] == owner.astype(jnp.float32), 1.0, 0.0)
    flat = jnp.where(place == other, mine, 0.0).astype(jnp.bfloat16)
    before = jnp.where(place < other, mine, 0.0).astype(jnp.bfloat16)
    ones = jnp.ones((capacity, rows), jnp.bfloat16)
    member = dot(ones, flat)
    rank = dot(ones, before)
    slot = lax.broadcasted_iota(jnp.int32, (capacity, rows), 0).astype(jnp.float32)
    chosen = jnp.where((member > 0.5) & (rank == slot), 1.0, 0.0).astype(jnp.bfloat16)
    picked = dot(chosen, low).astype(jnp.bfloat16)
    query_cols = up_query.shape[2] // count
    value_cols = up_value.shape[2] // count
    for j in range(count):
        out, there = outs[j // 2], owner ^ j
        slots = slice((j % 2) * capacity, (j % 2 + 1) * capacity)
        columns = pl.ds(pl.multiple_of(there * query_cols, query_cols), query_cols)
        for_query = dot(picked[:, :ADAPTER_RANK], up_query[0, :, columns]) * adapter_scale
        out[slots, :query_cols] = for_query.astype(jnp.bfloat16)
        columns = pl.ds(pl.multiple_of(there * value_cols, value_cols), value_cols)
        for_value = dot(picked[:, ADAPTER_RANK:], up_value[0, :, columns]) * adapter_scale
        out[slots, query_cols:] = for_value.astype(jnp.bfloat16)


def open_kernel(hidden, names, entering):
    micro, local_rows, width = hidden.shape
    own_rows = micro * local_rows
    part = entering.shape[1] - HD
    count = width // part
    rows = jnp.concatenate([hidden[m].astype(jnp.float32) for m in range(micro)], 0)
    entering[:, :part] = jnp.concatenate(
        [rows[:, i * part : (i + 1) * part] for i in range(count)], 0
    ).astype(jnp.bfloat16)
    row = lax.broadcasted_iota(jnp.int32, (count * own_rows, HD), 0) % own_rows
    name = jnp.zeros((count * own_rows, HD), jnp.float32)
    for r in range(own_rows):
        one = names[r // local_rows, 0, r % local_rows].astype(jnp.float32)
        name = jnp.where(row == r, one, name)
    entering[:, part:] = name.astype(jnp.bfloat16)


def row_lengths(lengths, near_lengths, shape, each=GROUP):
    micro, local_rows = lengths.shape
    own_rows = micro * local_rows
    row = lax.broadcasted_iota(jnp.int32, shape, 0) // each
    found = jnp.zeros(shape, jnp.int32)
    for i in range(2 * own_rows):
        source, r = (lengths, near_lengths)[i // own_rows], i % own_rows
        found = jnp.where(row == i, source[r // local_rows, r % local_rows], found)
    return found


def angle_work(small, more):
    lengths, near_lengths, inverse = small
    cosine, sine = more
    angles = row_lengths(lengths, near_lengths, cosine.shape).astype(jnp.float32) * inverse[...]
    front = lax.broadcasted_iota(jnp.int32, cosine.shape, 1) < HD // 2
    cosine[...] = jnp.cos(angles)
    sine[...] = jnp.where(front, -jnp.sin(angles), jnp.sin(angles))


def enter_kernel(count, own_rows, capacity, tick, *refs):
    chunks, rest = refs[:count], refs[count:]
    _, gain, *adapters, normed, held, ident = rest[:8]
    *correction, spread = rest[8:]
    owner = lax.axis_index("wide")
    rows = count * own_rows
    part = gain.shape[1] // count
    spread[...] = by_part(owner, chunks, own_rows)
    ident[...] = spread[:rows, part:]

    @pl.when(lax.axis_index("segment") == tick)
    def _():
        squares = jnp.zeros((rows, 1), jnp.float32)
        for i in range(count):
            block = spread[i * rows : (i + 1) * rows, :part]
            squares += jnp.sum(block * block, 1, keepdims=True)
        scale = lax.rsqrt(squares / gain.shape[1] + epsilon)
        for i in range(count):
            block = spread[i * rows : (i + 1) * rows, :part]
            columns = slice(i * part, (i + 1) * part)
            weight = gain[:, columns].astype(jnp.float32)
            normed[:, columns] = (block * scale * weight).astype(jnp.bfloat16)
        own = pl.ds(pl.multiple_of(owner * rows, rows), rows)
        held[...] = spread[own, :part].astype(jnp.bfloat16)
        adapter_part(owner, ident, normed, adapters, correction, capacity)


def norm_kernel(count, capacity, *refs):
    chunks, rest = refs[:count], refs[count:]
    ident, gain, *adapters, normed = rest[:6]
    correction = rest[6:]
    owner = lax.axis_index("wide")
    rows, part = chunks[0].shape
    squares = jnp.zeros((rows, 1), jnp.float32)
    for chunk in chunks:
        block = chunk[...].astype(jnp.float32)
        squares += jnp.sum(block * block, 1, keepdims=True)
    scale = lax.rsqrt(squares / gain.shape[1] + epsilon)
    for k, chunk in enumerate(chunks):
        columns = pl.ds(pl.multiple_of((owner ^ k) * part, part), part)
        weight = gain[:, columns].astype(jnp.float32)
        normed[:, columns] = (chunk[...].astype(jnp.float32) * scale * weight).astype(jnp.bfloat16)
    adapter_part(owner, ident, normed, adapters, correction, capacity)


def project_kernel(normed, query, query_rest, key, value, out):
    def store(columns, product):
        out[:, columns] = product

    matmul_into(store, normed, [query, query_rest], STEP)
    narrow_into(normed, key, value, out)


def narrow_into(normed, key, value, out):
    narrow = key.shape[1]
    wide = out.shape[1] - 2 * narrow
    out[:, wide : wide + narrow] = dot(normed[...], key[...])
    out[:, wide + narrow :] = dot(normed[...], value[...])


def project_first_kernel(step, tick, normed, whole_query, query, key, value, out, query_rest, sems):
    first = query.shape[1]
    copies = []
    for i in range(query_rest.shape[1] // step):
        here = pl.ds(i * step, step)
        source = whole_query.at[:, pl.ds(first + i * step, step)]
        copies.append(pltpu.make_async_copy(source, query_rest.at[:, here], sems.at[i]))
    for copy in copies[:2]:
        copy.start()

    live = lax.axis_index("segment") == tick

    def store(columns, product):
        out[:, columns] = product

    @pl.when(live)
    def _():
        narrow_into(normed, key, value, out)
        matmul_into(store, normed, [query], STEP)

    for i, copy in enumerate(copies):
        copy.wait()
        if i + 2 < len(copies):
            copies[i + 2].start()

        @pl.when(live)
        def _():
            here = slice(i * step, (i + 1) * step)
            target = slice(first + i * step, first + (i + 1) * step)
            out[:, target] = dot(normed[...], query_rest[:, here])


def received_rows(received):
    half = received[0].shape[0] // 2
    return [ref[(j % 2) * half : (j % 2 + 1) * half, :] for j, ref in enumerate(received)]


def correct_kernel(count, capacity, query_cols, key_cols, base, ident, *refs):
    received, outs = refs[:count], refs[count:]
    owner = lax.axis_index("wide")
    rows = base.shape[0]
    own_rows = rows // count
    slots = count * capacity
    place = lax.broadcasted_iota(jnp.int32, (rows, rows), 0)
    other = lax.broadcasted_iota(jnp.int32, (rows, rows), 1)
    own = ident[:, :1]
    flat = jnp.where(place == other, own, 0.0).astype(jnp.bfloat16)
    line = dot(jnp.ones((rows, rows), jnp.bfloat16), flat)
    rank = jnp.sum(jnp.where((own == line) & (other < place), 1.0, 0.0), 1, keepdims=True)
    slot = lax.broadcasted_iota(jnp.int32, (rows, slots), 1)
    source = ((slot // capacity) ^ owner).astype(jnp.float32)
    hit = (source == own) & ((slot % capacity).astype(jnp.float32) == rank)
    table = jnp.where(hit, 1.0, 0.0).astype(jnp.bfloat16)
    placed = dot(table, jnp.concatenate(received_rows(received), 0))
    whole = base[...]
    first = whole[:, :query_cols] + placed[:, :query_cols]
    middle = whole[:, query_cols : query_cols + key_cols]
    last = whole[:, query_cols + key_cols :] + placed[:, query_cols:]
    packed = jnp.concatenate([first, middle, last], 1).astype(jnp.bfloat16)
    by_destination(owner, packed, own_rows, outs)


def by_destination(owner, packed, own_rows, outs):
    rows = packed.shape[0]
    place = lax.broadcasted_iota(jnp.int32, (rows, rows), 0)
    other = lax.broadcasted_iota(jnp.int32, (rows, rows), 1)
    hit = (((place // own_rows) ^ owner) == other // own_rows) & (
        place % own_rows == other % own_rows
    )
    order = jnp.where(hit, 1.0, 0.0).astype(jnp.bfloat16)
    sorted_rows = dot(order, packed).astype(jnp.bfloat16)
    for k, out in enumerate(outs):
        out[...] = sorted_rows[k * 2 * own_rows : (k + 1) * 2 * own_rows, :]


def attend_kernel(chips, lengths, near_lengths, *refs):
    arrived, rest = refs[:chips], refs[chips:]
    cosine, sine, keys, values, near_keys, near_values, out, scores, weights = rest
    chip = lax.axis_index("wide") // 2
    own_rows, span = keys.shape[:2]
    chip_rows = 2 * own_rows
    rows = GROUP * chip_rows
    cos, sin = cosine[...], sine[...]
    position = lax.broadcasted_iota(jnp.int32, (2 * rows, span), 1)
    valid = position < row_lengths(lengths, near_lengths, (2 * rows, span), 2 * GROUP)
    score_scale = HD ** (-0.5)

    def turned(vectors):
        return vectors * cos + pltpu.roll(vectors, HD // 2, 1) * sin

    def rounded(vectors):
        return vectors.astype(jnp.bfloat16).astype(jnp.float32)

    pieces = []
    for ref in arrived:
        packed = ref[...].astype(jnp.float32)
        heads = [packed[:, i * HD : (i + 1) * HD] for i in range(GROUP)]
        fresh = [packed[:, GROUP * HD :]] * GROUP
        pieces += [jnp.concatenate(heads, 0), jnp.concatenate(fresh, 0)]
    out_row = lax.broadcasted_iota(jnp.int32, (rows, rows), 0)
    src_row = lax.broadcasted_iota(jnp.int32, (rows, rows), 1)
    same = (out_row // GROUP == src_row % chip_rows) & (out_row % GROUP == src_row // chip_rows)
    order = jnp.where(same, 1.0, 0.0).astype(jnp.bfloat16)
    sorted_rows = dot(order, jnp.concatenate(pieces, 1).astype(jnp.bfloat16))
    band = 2 * GROUP

    def woven(one, two):
        bands = [slice(r * GROUP, (r + 1) * GROUP) for r in range(chip_rows)]
        return jnp.concatenate([part[rows_of] for rows_of in bands for part in (one, two)], 0)

    def pair_lanes(p):
        return pl.ds(pl.multiple_of((chip // 2 ^ p) * 2 * HD, 2 * HD), 2 * HD)

    even = chip % 2 == 0
    zero = jnp.zeros((rows, HD), jnp.float32)
    pairs = range(chips // 2)
    fresh = []
    for p in pairs:
        wide, own, new_values = [], [], []
        for n in range(2):
            piece = sorted_rows[:, (2 * p + n) * 3 * HD : (2 * p + n + 1) * 3 * HD]
            query = rounded(turned(piece[:, :HD]))
            new_key = rounded(turned(piece[:, HD : 2 * HD]))
            own.append(jnp.sum(query * new_key, 1, keepdims=True) * score_scale)
            new_values.append(piece[:, 2 * HD :])
            left = even if n == 0 else jnp.logical_not(even)
            wide.append(
                jnp.concatenate([jnp.where(left, query, zero), jnp.where(left, zero, query)], 1)
            )
        fresh.append((woven(*own), woven(*new_values)))
        wide = woven(*wide).astype(jnp.bfloat16)
        for r in range(chip_rows):
            first = (p * chip_rows + r) * band
            scores[first : first + band, :] = lax.dot_general(
                wide[r * band : (r + 1) * band, :],
                (keys, near_keys)[r // own_rows][r % own_rows, :, pair_lanes(p)],
                (((1,), (1,)), ((), ())),
                preferred_element_type=jnp.float32,
            )
    parts = []
    for p, (own, new_value) in enumerate(fresh):
        here = slice(p * 2 * rows, (p + 1) * 2 * rows)
        found = jnp.where(valid, scores[here, :] * score_scale, -1e30)
        top = jnp.maximum(jnp.max(found, 1, keepdims=True), own)
        past = jnp.where(valid, jnp.exp(found - top), 0.0)
        own = jnp.exp(own - top)
        total = jnp.sum(past, 1, keepdims=True) + own
        weights[here, :] = (past / total).astype(jnp.bfloat16)
        parts.append(rounded(own / total) * new_value)
    for p, own_part in enumerate(parts):
        mixed = []
        for r in range(chip_rows):
            first = (p * chip_rows + r) * band
            found = dot(
                weights[first : first + band, :],
                (values, near_values)[r // own_rows][r % own_rows, :, pair_lanes(p)],
            )
            mine = own_part[r * band : (r + 1) * band, :]
            one = jnp.where(even, found[:GROUP, :HD], found[:GROUP, HD:]) + mine[:GROUP]
            two = jnp.where(even, found[GROUP:, HD:], found[GROUP:, :HD]) + mine[GROUP:]
            both = [jnp.where(even, one, two), jnp.where(even, two, one)]
            mixed.append(jnp.concatenate(both, 1))
        out[:, pair_lanes(p)] = jnp.concatenate(mixed, 0).astype(jnp.bfloat16)


def attended_rows(owner, chunks, own_rows, rows_ref):
    count = len(chunks)
    chips = count // 2
    rows = own_rows * count
    total = rows * GROUP
    out = lax.broadcasted_iota(jnp.int32, (total, total), 0)
    src = lax.broadcasted_iota(jnp.int32, (total, total), 1)
    device_out = (out // own_rows) % count
    chip_rows = 2 * own_rows
    row_src = (src // GROUP) % chip_rows
    near = (out // rows == src % GROUP) & (out % own_rows == row_src % own_rows)
    for core in range(2):
        stack = jnp.concatenate([chunks[2 * k + core][...] for k in range(chips)], 0)
        device_src = owner ^ (2 * (src // (GROUP * chip_rows)) + core) ^ (row_src // own_rows)
        hit = near & (device_out == device_src)
        spread = dot(jnp.where(hit, 1.0, 0.0).astype(jnp.bfloat16), stack).astype(jnp.bfloat16)
        first = (owner ^ core) % 2
        for i in range(chips):
            for j in range(GROUP):
                head = (2 * i + first) * GROUP + j
                rows_ref[:, pl.ds(pl.multiple_of(head * HD, HD), HD)] = spread[
                    j * rows : (j + 1) * rows, i * HD : (i + 1) * HD
                ]


def leave_kernel(count, own_rows, tick, *refs):
    chunks, rest = refs[:count], refs[count:]
    held, result = rest[0], rest[1] if tick else None
    matrix, matrix_rest, out, kept, *outs, rows_ref = rest[2 if tick else 1 :]
    kept[...] = result[...] if tick else jnp.zeros_like(kept)

    @pl.when(lax.axis_index("segment") == tick)
    def _():
        attended_rows(lax.axis_index("wide"), chunks, own_rows, rows_ref)

        def store(columns, product):
            total = held[:, columns].astype(jnp.float32) + product
            out[:, columns] = total.astype(jnp.bfloat16)
            kept[:, columns] = total.astype(jnp.bfloat16)

        matmul_into(store, rows_ref, [matrix, matrix_rest], STEP)

    if outs:
        by_destination(lax.axis_index("wide"), kept[...], own_rows, outs)


def join_kernel(count, *refs):
    blocks, out = refs[:count], refs[count]
    for j, block in enumerate(blocks):
        rows = block.shape[0] // 2
        half = block[(j % 2) * rows : (j % 2 + 1) * rows, :]
        width = half.shape[1]
        columns = pl.ds(pl.multiple_of((lax.axis_index("wide") ^ j) * width, width), width)
        for m in range(out.shape[1]):
            local_rows = out.shape[2]
            out[0, m, :, columns] = half[m * local_rows : (m + 1) * local_rows, :]


def on_device_by_head(
    entering_hidden,
    row_adapter_index,
    lengths,
    input_norm_gain,
    query_matrix,
    key_matrix,
    value_matrix,
    output_matrix,
    adapter_down_maps,
    adapter_up_query,
    adapter_up_value,
    rotated_key_cache,
    cached_values,
):
    segments = lax.axis_size("segment")
    count = lax.axis_size("wide")
    micro, local_rows, width = entering_hidden.shape
    own_rows = micro * local_rows
    rows = own_rows * count
    capacity = CAP * micro
    part = width // count
    query_cols, key_cols = query_matrix.shape[2], key_matrix.shape[2]
    packed_cols = query_cols + 2 * key_cols
    span = rotated_key_cache.shape[3]

    chips = count // 2
    head_lanes = chips * HD
    query_weight = query_matrix[0]
    output_weight = output_matrix[0]
    adapters = [adapter_down_maps[0], adapter_up_query[0], adapter_up_value[0]]
    caches = [cache[0].reshape(own_rows, span, -1) for cache in (rotated_key_cache, cached_values)]
    near_lengths = swapped(lengths, 1)
    gain = input_norm_gain
    half = HD // 2
    inverse = np.tile(rope_base ** (-np.arange(half) / half), 2).astype(np.float32)[None]

    def blocks_of(slots, columns):
        return [jax.ShapeDtypeStruct((2 * slots, columns), jnp.bfloat16)] * chips

    normed_shape = jax.ShapeDtypeStruct((rows, width), jnp.bfloat16)
    held_shape = jax.ShapeDtypeStruct((rows, part), jnp.bfloat16)
    ident_shape = jax.ShapeDtypeStruct((rows, HD), jnp.float32)
    base_shape = jax.ShapeDtypeStruct((rows, packed_cols), jnp.float32)
    angle_shape = jax.ShapeDtypeStruct((GROUP * 2 * own_rows, HD), jnp.float32)
    correction_shapes = blocks_of(capacity, query_cols + key_cols)
    query_first = query_cols // 4
    output_first = part // 2

    (entering,) = call(
        open_kernel,
        [jax.ShapeDtypeStruct((rows, part + HD), jnp.bfloat16)],
        [(entering_hidden, VMEM), (row_adapter_index.transpose(0, 2, 1), SMEM)],
        name="open",
    )
    projections, output_parts, halves, angles = [], [], [], []
    held = ident = None
    result = None
    blocks = []
    for tick in range(segments):
        if tick == 0:

            def load_first():
                sources = [*adapters, key_matrix[0], value_matrix[0], query_weight, *caches]
                small = [(entering, VMEM)]
                shape = (own_rows, span, head_lanes)
                shapes = [source.shape for source in sources[:5]] + [(width, query_first)]
                shapes += [shape] * 4

                def plan(sources, outs):
                    pairs = list(zip(sources[:5], outs[:5]))
                    pairs.append((sources[5].at[:, :query_first], outs[5]))
                    core = lax.axis_index("wide") % 2
                    for n in range(4):
                        for i in range(chips):
                            head = 2 * i + (core if n < 2 else 1 - core)
                            there = pl.ds(pl.multiple_of(head * HD, HD), HD)
                            source = sources[6 + n % 2].at[:, :, there]
                            pairs.append((source, outs[6 + n].at[:, :, pl.ds(i * HD, HD)]))
                    return pairs

                found, (token,) = loaded(
                    sources, shapes, plan, 6 + 4 * chips, small, [TOKEN], token_of
                )
                adapters[:], projections[:] = found[:3], [found[5], found[3], found[4]]
                halves[:] = found[6:]
                return token

            chunks, _ = gathered(entering, load_first)
            normed, held, ident, *found = call(
                functools.partial(enter_kernel, count, own_rows, capacity, tick),
                [normed_shape, held_shape, ident_shape] + correction_shapes,
                [(c, VMEM) for c in chunks]
                + [(near_lengths, pl.BlockSpec(memory_space=pl.ANY)), (gain, VMEM)],
                [pltpu.VMEM((count * rows, part + HD), jnp.float32)],
                kept=adapters,
                through=halves[2:],
                name="enter",
            )
            halves[2:] = [swapped(array, 1) for array in found[chips:]]
        else:
            chunks = passed_on(held, tick - 1)
            held = chunks[0]
            normed, *found = call(
                while_live(tick, functools.partial(norm_kernel, count, capacity)),
                [normed_shape] + correction_shapes,
                [(c, VMEM) for c in chunks] + [(ident, VMEM), (gain, VMEM)],
                kept=adapters,
                name="norm",
            )
        correction = found[:chips]

        def project():
            return call(
                while_live(tick, project_kernel),
                [base_shape],
                [(normed, VMEM)],
                kept=projections,
                cost=16,
                name="project",
            )[0]

        def project_first():
            base, rest = pl.pallas_call(
                functools.partial(project_first_kernel, query_first, tick),
                out_shape=[base_shape, pltpu.VMEM((width, query_cols - query_first), jnp.bfloat16)],
                in_specs=[VMEM, pl.BlockSpec(memory_space=pl.ANY)] + [VMEM] * 3,
                out_specs=[VMEM, VMEM],
                scratch_shapes=[pltpu.SemaphoreType.DMA((query_cols // query_first - 1,))],
                compiler_params=pltpu.CompilerParams(vmem_limit_bytes=8 * MIB),
                cost_estimate=pl.CostEstimate(
                    flops=0, transcendentals=0, bytes_accessed=16 * MIB
                ),
                name="project",
            )(
                normed,
                pltpu.with_memory_space_constraint(query_weight, pltpu.HBM),
                *[resident(array) for array in projections],
            )
            projections[1:1] = [rest]
            return base

        received, base = exchanged(correction, project if tick else project_first)
        received = [part for one in received for part in (one, swapped(one, 1))]
        packed = call(
            while_live(
                tick, functools.partial(correct_kernel, count, capacity, query_cols, key_cols)
            ),
            blocks_of(own_rows, packed_cols),
            [(base, VMEM), (ident, VMEM)] + [(r, VMEM) for r in received],
            name="correct",
        )

        def load_part():
            small = [(lengths, SMEM), (near_lengths, SMEM), (jnp.asarray(inverse), VMEM)]
            found, angles[:] = loaded(
                [output_weight],
                [(width, output_first)],
                lambda sources, outs: [(sources[0].at[:, :output_first], outs[0])],
                1,
                small,
                [angle_shape, angle_shape],
                angle_work,
            )
            output_parts[:] = found
            return angles[0]

        def load_output():
            found, (token,) = loaded(
                [output_weight],
                [(width, part - output_first)],
                lambda sources, outs: [(sources[0].at[:, output_first:], outs[0])],
                1,
                [(attended, VMEM)],
                [TOKEN],
                token_of,
            )
            output_parts[1:] = found
            return token

        arrived, _ = exchanged(packed, None if tick else load_part)
        attended, *_ = call(
            while_live(tick, functools.partial(attend_kernel, chips)),
            [jax.ShapeDtypeStruct((GROUP * 2 * own_rows, head_lanes), jnp.bfloat16)],
            [(lengths, SMEM), (near_lengths, SMEM)]
            + [(a, VMEM) for a in [*arrived, *angles]],
            [
                pltpu.VMEM((chips * GROUP * 2 * own_rows, span), jnp.float32),
                pltpu.VMEM((chips * GROUP * 2 * own_rows, span), jnp.bfloat16),
            ],
            kept=halves,
            name="attend",
        )
        chunks, _ = gathered(attended, None if tick else load_output)
        last = tick == segments - 1
        held, result, *found = call(
            functools.partial(leave_kernel, count, own_rows, tick),
            [held_shape, held_shape] + (blocks_of(own_rows, part) if last else []),
            [(c, VMEM) for c in chunks]
            + [(held, VMEM)] + ([(result, VMEM)] if tick else []),
            [pltpu.VMEM((rows, width), jnp.bfloat16)],
            kept=output_parts,
            name="leave",
        )
        blocks = found
    far, _ = exchanged(blocks)
    far = [part for one in far for part in (one, swapped(one, 1))]
    (joined,) = call(
        functools.partial(join_kernel, count),
        [jax.ShapeDtypeStruct((1, micro, local_rows, width), jnp.bfloat16)],
        [(one, VMEM) for one in far],
        name="join",
    )
    return joined


def passed_along(value, axis, steps):
    count = lax.axis_size(axis)
    leading, last = (max(0, -steps), min(count, count - steps))
    return lax.ppermute(value, axis, [(source, source + steps) for source in range(leading, last)])


def rotary(vectors, positions):
    half = vectors.shape[-1] // 2
    inverse = rope_base ** (-jnp.arange(half, dtype=jnp.float32) / half)
    angles = positions.astype(jnp.float32)[:, None] * inverse[None, :]
    cosine = jnp.cos(angles)[:, None, :]
    sine = jnp.sin(angles)[:, None, :]
    front = vectors[..., :half]
    back = vectors[..., half:]
    return jnp.concatenate([front * cosine - back * sine, back * cosine + front * sine], -1)


def attend(query_vector, new_key, fresh_value, positions, key_block, value_block):
    rows = query_vector.shape[0]
    group = HEADS // KVH
    rotated_rows = rotary(
        query_vector.astype(jnp.float32).reshape(rows, HEADS, HD), positions
    ).astype(jnp.bfloat16)
    rotated_rows = rotated_rows.reshape(rows, KVH, group, HD)
    self_key = rotary(new_key.astype(jnp.float32).reshape(rows, KVH, HD), positions).astype(
        jnp.bfloat16
    )
    keys_past = key_block.reshape(rows, -1, KVH, HD)
    values_past = value_block.reshape(rows, -1, KVH, HD)
    score_scale = HD ** (-0.5)
    past = (
        jnp.einsum("bkgd,bpkd->bkgp", rotated_rows, keys_past, preferred_element_type=jnp.float32)
        * score_scale
    )
    self_scores = (
        jnp.einsum("rice,rie->ric", rotated_rows, self_key, preferred_element_type=jnp.float32)
        * score_scale
    )
    valid = jnp.arange(keys_past.shape[1])[None, :] < positions[:, None]
    past = jnp.where(valid[:, None, None, :], past, -1e30)
    top = jnp.maximum(jnp.max(past, -1), self_scores)
    past_exp = jnp.where(valid[:, None, None, :], jnp.exp(past - top[..., None]), 0.0)
    own_exp = jnp.exp(self_scores - top)
    total = jnp.sum(past_exp, -1) + own_exp
    past_weights = (past_exp / total[..., None]).astype(jnp.bfloat16)
    own_weights = (own_exp / total).astype(jnp.bfloat16)
    mixed = jnp.einsum(
        "bkgp,bpkd->bkgd", past_weights, values_past, preferred_element_type=jnp.float32
    )
    mixed = (
        mixed
        + own_weights.astype(jnp.float32)[..., None]
        * fresh_value.reshape(rows, KVH, HD).astype(jnp.float32)[:, :, None, :]
    )
    return mixed.reshape(rows, HEADS * HD).astype(jnp.bfloat16)


def on_device(
    entering_hidden,
    row_adapter_index,
    lengths,
    input_norm_gain,
    query_matrix,
    key_matrix,
    value_matrix,
    output_matrix,
    adapter_down_maps,
    adapter_up_query,
    adapter_up_value,
    rotated_key_cache,
    cached_values,
):
    segments = lax.axis_size("segment")
    segment = lax.axis_index("segment")
    devices = lax.axis_size("wide")
    owner = lax.axis_index("wide")
    small_batch, local_rows, width = entering_hidden.shape
    listed = lax.all_gather(row_adapter_index, "wide", axis=1, tiled=True)[:, :, 0]
    groups = small_batch // small_batch
    capacity = CAP * small_batch
    kept_entries = adapter_down_maps.shape[1]
    adapters = kept_entries * devices
    mine = owner * kept_entries + jnp.arange(kept_entries)
    gain = input_norm_gain[0].astype(jnp.float32)
    query_cols = query_matrix.shape[2]
    key_cols = key_matrix.shape[2]
    passed = jnp.zeros((small_batch * local_rows, width), jnp.bfloat16)
    results = jnp.zeros((small_batch, local_rows, width), jnp.bfloat16)
    ticks = groups + segments - 1
    for tick in range(ticks):
        if tick < groups:
            fresh = entering_hidden.reshape(small_batch * local_rows, width)
        else:
            fresh = jnp.zeros_like(passed)
        rows = jnp.where(segment == 0, fresh, passed)
        index = tick - segment
        live = (index >= 0) & (index < groups)
        index = jnp.clip(index, 0, groups - 1)
        block_rows = rows.shape[0]
        idents = listed
        idents = idents.reshape(small_batch, devices, local_rows).transpose(1, 0, 2).reshape(-1)
        positions = lengths.reshape(-1)
        key_block = rotated_key_cache[0]
        key_block = key_block.reshape(block_rows, key_block.shape[2], key_block.shape[3])
        value_block = cached_values[0]
        value_block = value_block.reshape(block_rows, value_block.shape[2], value_block.shape[3])
        values = rows.astype(jnp.float32)
        normalized_rows = (
            values * lax.rsqrt(jnp.mean(values * values, 1, keepdims=True) + epsilon) * gain
        ).astype(jnp.bfloat16)
        gathered = lax.all_gather(normalized_rows, "wide", axis=0, tiled=True)
        total_rows = gathered.shape[0]
        matches = (idents[None, :] == mine[:, None]).astype(jnp.int32)
        ranks = jnp.cumsum(matches, 1) - 1
        chosen = (matches[:, None, :] == 1) & (
            ranks[:, None, :] == jnp.arange(capacity)[None, :, None]
        )
        chosen = chosen.reshape(kept_entries * capacity, total_rows)
        selected_rows = jnp.dot(
            chosen.astype(jnp.bfloat16), gathered, preferred_element_type=jnp.float32
        ).astype(jnp.bfloat16)
        selected_rows = selected_rows.reshape(kept_entries, capacity, width)
        reduced = jnp.einsum(
            "bpy,byf->bpf", selected_rows, adapter_down_maps[0], preferred_element_type=jnp.float32
        ).astype(jnp.bfloat16)
        member = (idents[:, None] == jnp.arange(adapters)[None, :]).astype(jnp.int32)
        order = jnp.sum(jnp.cumsum(member, 0) * member, 1) - 1
        slot = idents * capacity + order
        slot_table = slot[:, None] == jnp.arange(adapters * capacity)[None, :]
        query_slots = jnp.einsum(
            "acr,are->ace",
            reduced[..., :ADAPTER_RANK],
            adapter_up_query[0],
            preferred_element_type=jnp.float32,
        )
        value_slots = jnp.einsum(
            "acr,are->ace",
            reduced[..., ADAPTER_RANK:],
            adapter_up_value[0],
            preferred_element_type=jnp.float32,
        )
        joined = jnp.concatenate(
            [
                query_slots.reshape(kept_entries * capacity, devices, -1),
                value_slots.reshape(kept_entries * capacity, devices, -1),
            ],
            2,
        )
        received = lax.all_to_all(joined, "wide", split_axis=1, concat_axis=0, tiled=True)
        received = received.reshape(adapters * capacity, -1)
        placed = jnp.dot(slot_table.astype(jnp.float32), received, precision=lax.Precision.HIGHEST)
        query_adjustment = placed[:, :query_cols]
        value_adjustment = placed[:, query_cols:]
        query_vector = (
            jnp.dot(gathered, query_matrix[0], preferred_element_type=jnp.float32)
            + adapter_scale * query_adjustment
        ).astype(jnp.bfloat16)
        new_key = jnp.dot(gathered, key_matrix[0], preferred_element_type=jnp.float32).astype(
            jnp.bfloat16
        )
        fresh_value = (
            jnp.dot(gathered, value_matrix[0], preferred_element_type=jnp.float32)
            + adapter_scale * value_adjustment
        ).astype(jnp.bfloat16)
        packed = jnp.concatenate([query_vector, new_key, fresh_value], 1)
        arrived = lax.all_to_all(packed, "wide", split_axis=0, concat_axis=1, tiled=True).reshape(
            block_rows, devices, -1
        )
        query_rows_local = arrived[:, :, :query_cols].reshape(block_rows, -1)
        key_rows_local = arrived[:, :, query_cols : query_cols + key_cols].reshape(block_rows, -1)
        value_rows_local = arrived[:, :, query_cols + key_cols :].reshape(block_rows, -1)
        attended = attend(
            query_rows_local, key_rows_local, value_rows_local, positions, key_block, value_block
        )
        columns = jnp.dot(
            lax.all_gather(attended, "wide", axis=0, tiled=True),
            output_matrix[0],
            preferred_element_type=jnp.float32,
        )
        returned = lax.all_to_all(columns, "wide", split_axis=0, concat_axis=1, tiled=True)
        outcome = (values + returned).astype(jnp.bfloat16)
        updated = outcome.reshape(small_batch, local_rows, width)
        results = jnp.where(live, updated, results)
        if tick + 1 < ticks:
            passed = passed_along(outcome, "segment", 1)
    return results[None]


def solution(mesh):
    placed = (
        P(None, "wide", None),
        P(None, "wide", None),
        P(None, "wide"),
        P("segment", None),
        P("segment", None, "wide"),
        P("segment", None, "wide"),
        P("segment", None, "wide"),
        P("segment", None, "wide"),
        P("segment", "wide", None, None),
        P("segment", "wide", None, None),
        P("segment", "wide", None, None),
        P("segment", None, "wide", None, None),
        P("segment", None, "wide", None, None),
    )
    by_head = mesh.shape["wide"] == KVH
    return jax.shard_map(
        on_device_by_head if by_head else on_device,
        mesh=mesh,
        in_specs=placed,
        out_specs=P("segment", None, "wide", None),
        check_vma=False,
    )
```

```python
import functools

import jax
import jax.numpy as jnp
import numpy as np
from jax import lax
from jax.experimental import pallas as pl
from jax.experimental.pallas import tpu as pltpu
from jax.sharding import PartitionSpec as P

HEADS = 64
KVH = 8
HD = 128
ADAPTER_RANK = 64
CAP = 4


adapter_scale = 0.5
rope_base = 500000.0
epsilon = 1e-05

GROUP = HEADS // KVH
MIB = 1 << 20
STEP = 256
VMEM = pl.BlockSpec(memory_space=pltpu.VMEM)
SMEM = pl.BlockSpec(memory_space=pltpu.SMEM)


def swapped(value, bits):
    count = lax.axis_size("wide")
    return lax.ppermute(value, "wide", [(i, i ^ bits) for i in range(count)])


def then(arrays, work):
    if work is None:
        return arrays, None
    done = work()
    arrays = arrays[::-1]
    arrays = pl.pallas_call(
        lambda *refs: None,
        out_shape=[jax.ShapeDtypeStruct(array.shape, array.dtype) for array in arrays],
        in_specs=[VMEM] * len(arrays) + [pl.BlockSpec(memory_space=pl.ANY)],
        out_specs=[VMEM] * len(arrays),
        input_output_aliases={i: i for i in range(len(arrays))},
        compiler_params=pltpu.CompilerParams(vmem_limit_bytes=MIB),
        name="then",
    )(*arrays, done)
    return arrays[::-1], done


def gathered(value, work=None):
    count = lax.axis_size("wide")
    far = [swapped(value, k) for k in range(2, count, 2)]
    far, done = then(far, work)
    found = [part for one in [value, *far] for part in (one, swapped(one, 1))]
    return found, done


def passed_on(value, s):
    count = lax.axis_size("wide")

    def shifted(bits):
        pairs = [(s * count + i, (s + 1) * count + (i ^ bits)) for i in range(count)]
        return lax.ppermute(value, ("segment", "wide"), pairs)

    far = [shifted(bits) for bits in range(0, count, 2)]
    return [part for one in far for part in (one, swapped(one, 1))]


def exchanged(blocks, work=None):
    far = [swapped(block, 2 * k) for k, block in enumerate(blocks) if k]
    far, done = then(far, work)
    return [blocks[0], *far], done


def resident(weight):
    return pltpu.with_memory_space_constraint(weight, pltpu.VMEM)


def call(body, out_shape, operands, scratch=(), limit=8, kept=(), through=(), cost=1, name=None):
    outs, count = list(out_shape), len(operands) + len(kept)
    inner = body
    if through:

        def inner(*refs):
            inputs = count + len(through)
            shown = inputs + len(outs)
            body(*refs[:count], *refs[inputs:shown], *refs[shown + len(through) :])

    found = pl.pallas_call(
        inner,
        out_shape=outs + [pltpu.VMEM(array.shape, array.dtype) for array in through],
        in_specs=[spec for _, spec in operands] + [VMEM] * (len(kept) + len(through)),
        out_specs=[VMEM] * (len(outs) + len(through)),
        input_output_aliases={count + i: len(outs) + i for i in range(len(through))},
        scratch_shapes=list(scratch),
        compiler_params=pltpu.CompilerParams(vmem_limit_bytes=limit * MIB),
        cost_estimate=pl.CostEstimate(flops=0, transcendentals=0, bytes_accessed=cost * MIB),
        name=name,
    )(*[array for array, _ in operands], *[resident(array) for array in [*kept, *through]])
    return list(found)


def load_kernel(sizes, plan, work, *refs):
    sources, small, outs, more = [], [], [], []
    refs = list(refs)
    for group, size in zip((sources, small, outs, more), sizes, strict=True):
        group.extend(refs[:size])
        del refs[:size]
    copies = [
        pltpu.make_async_copy(source, out, refs[0].at[i])
        for i, (source, out) in enumerate(plan(sources, outs))
    ]
    for copy in copies:
        copy.start()
    work(small, more)
    for copy in copies:
        copy.wait()


def loaded(sources, shapes, plan, copies, small, more, work):
    moved = sum(2 * int(np.prod(shape)) for shape in shapes)
    found = pl.pallas_call(
        functools.partial(
            load_kernel, (len(sources), len(small), len(shapes), len(more)), plan, work
        ),
        out_shape=[pltpu.VMEM(shape, jnp.bfloat16) for shape in shapes] + list(more),
        in_specs=[pl.BlockSpec(memory_space=pl.ANY)] * len(sources) + [spec for _, spec in small],
        out_specs=[VMEM] * (len(shapes) + len(more)),
        scratch_shapes=[pltpu.SemaphoreType.DMA((copies,))],
        compiler_params=pltpu.CompilerParams(vmem_limit_bytes=4 * MIB),
        cost_estimate=pl.CostEstimate(flops=0, transcendentals=0, bytes_accessed=moved),
        name="load",
    )(
        *[pltpu.with_memory_space_constraint(source, pltpu.HBM) for source in sources],
        *[array for array, _ in small],
    )
    return found[: len(shapes)], found[len(shapes) :]


def half_of(other, sources, outs):
    core = (lax.axis_index("wide") + other) % 2
    pairs = []
    for source, out in zip(sources, outs, strict=True):
        for i in range(out.shape[2] // HD):
            there = pl.ds(pl.multiple_of((2 * i + core) * HD, HD), HD)
            pairs.append((source.at[:, :, there], out.at[:, :, pl.ds(i * HD, HD)]))
    return pairs


TOKEN = jax.ShapeDtypeStruct((8, HD), jnp.float32)


def token_of(small, more):
    more[0][...] = small[0][:8, :HD].astype(jnp.float32)


def load_rest_kernel(first, source, after, _, out, token, sem):
    copy = pltpu.make_async_copy(source.at[:, first:], out.at[:, first:], sem)
    copy.start()
    token[...] = after[:8, :HD].astype(jnp.float32)
    copy.wait()


def dot(left, right):
    return jnp.dot(left, right, preferred_element_type=jnp.float32)


def matmul_into(store, source, weight, step):
    def one(i, carry):
        columns = pl.ds(pl.multiple_of(i * step, step), step)
        store(columns, dot(source[...], weight[:, columns]))
        return carry

    lax.fori_loop(0, weight.shape[1] // step, one, 0)


def while_live(tick, body):
    def run(*refs):
        pl.when(lax.axis_index("segment") == tick)(lambda: body(*refs))

    return run


def by_part(owner, chunks, own_rows):
    count = len(chunks)
    parts = chunks[0].shape[0] // own_rows
    total = count * parts * own_rows
    stack = jnp.concatenate([chunk[...] for chunk in chunks], 0)
    out = lax.broadcasted_iota(jnp.int32, (total, total), 0)
    src = lax.broadcasted_iota(jnp.int32, (total, total), 1)
    rows = own_rows
    part_out = out // (rows * count)
    device_out = (out // rows) % count
    part_src = (src // rows) % parts
    device_src = (src // (rows * parts)) ^ owner
    hit = (part_out == part_src) & (device_out == device_src) & (out % rows == src % rows)
    return dot(jnp.where(hit, 1.0, 0.0).astype(jnp.bfloat16), stack)


def adapter_part(owner, ident, normed, adapter, outs, capacity):
    down, up_query, up_value = adapter
    rows = normed.shape[0]
    count = 2 * len(outs)
    low = dot(normed[...], down[0]).astype(jnp.bfloat16)
    place = lax.broadcasted_iota(jnp.int32, (rows, rows), 0)
    other = lax.broadcasted_iota(jnp.int32, (rows, rows), 1)
    mine = jnp.where(ident[:, :1] == owner.astype(jnp.float32), 1.0, 0.0)
    flat = jnp.where(place == other, mine, 0.0).astype(jnp.bfloat16)
    before = jnp.where(place < other, mine, 0.0).astype(jnp.bfloat16)
    ones = jnp.ones((capacity, rows), jnp.bfloat16)
    member = dot(ones, flat)
    rank = dot(ones, before)
    slot = lax.broadcasted_iota(jnp.int32, (capacity, rows), 0).astype(jnp.float32)
    chosen = jnp.where((member > 0.5) & (rank == slot), 1.0, 0.0).astype(jnp.bfloat16)
    picked = dot(chosen, low).astype(jnp.bfloat16)
    query_cols = up_query.shape[2] // count
    value_cols = up_value.shape[2] // count
    for j in range(count):
        out, there = outs[j // 2], owner ^ j
        slots = slice((j % 2) * capacity, (j % 2 + 1) * capacity)
        columns = pl.ds(pl.multiple_of(there * query_cols, query_cols), query_cols)
        for_query = dot(picked[:, :ADAPTER_RANK], up_query[0, :, columns]) * adapter_scale
        out[slots, :query_cols] = for_query.astype(jnp.bfloat16)
        columns = pl.ds(pl.multiple_of(there * value_cols, value_cols), value_cols)
        for_value = dot(picked[:, ADAPTER_RANK:], up_value[0, :, columns]) * adapter_scale
        out[slots, query_cols:] = for_value.astype(jnp.bfloat16)


def open_kernel(hidden, names_ref, entering, names, sem):
    copy = pltpu.make_async_copy(names_ref, names, sem)
    copy.start()
    micro, local_rows, width = hidden.shape
    own_rows = micro * local_rows
    part = entering.shape[1] - HD
    count = width // part
    rows = jnp.concatenate([hidden[m].astype(jnp.float32) for m in range(micro)], 0)
    entering[:, :part] = jnp.concatenate(
        [rows[:, i * part : (i + 1) * part] for i in range(count)], 0
    ).astype(jnp.bfloat16)
    row = lax.broadcasted_iota(jnp.int32, (count * own_rows, HD), 0) % own_rows
    name = jnp.zeros((count * own_rows, HD), jnp.float32)
    copy.wait()
    for r in range(own_rows):
        one = names[r // local_rows, 0, r % local_rows].astype(jnp.float32)
        name = jnp.where(row == r, one, name)
    entering[:, part:] = name.astype(jnp.bfloat16)


def row_lengths(lengths, near_lengths, shape, each=GROUP):
    micro, local_rows = lengths.shape
    own_rows = micro * local_rows
    row = lax.broadcasted_iota(jnp.int32, shape, 0) // each
    found = jnp.zeros(shape, jnp.int32)
    for i in range(2 * own_rows):
        source, r = (lengths, near_lengths)[i // own_rows], i % own_rows
        found = jnp.where(row == i, source[r // local_rows, r % local_rows], found)
    return found


def angle_work(small, more):
    lengths, near_lengths, inverse = small
    cosine, sine = more
    angles = row_lengths(lengths, near_lengths, cosine.shape).astype(jnp.float32) * inverse[...]
    front = lax.broadcasted_iota(jnp.int32, cosine.shape, 1) < HD // 2
    cosine[...] = jnp.cos(angles)
    sine[...] = jnp.where(front, -jnp.sin(angles), jnp.sin(angles))


def enter_kernel(count, own_rows, capacity, tick, *refs):
    chunks, rest = refs[:count], refs[count:]
    _, gain, *adapters, normed, held, ident = rest[:8]
    *correction, spread = rest[8:]
    owner = lax.axis_index("wide")
    rows = count * own_rows
    part = gain.shape[1] // count
    spread[...] = by_part(owner, chunks, own_rows)
    ident[...] = spread[:rows, part:]

    @pl.when(lax.axis_index("segment") == tick)
    def _():
        squares = jnp.zeros((rows, 1), jnp.float32)
        for i in range(count):
            block = spread[i * rows : (i + 1) * rows, :part]
            squares += jnp.sum(block * block, 1, keepdims=True)
        scale = lax.rsqrt(squares / gain.shape[1] + epsilon)
        for i in range(count):
            block = spread[i * rows : (i + 1) * rows, :part]
            columns = slice(i * part, (i + 1) * part)
            weight = gain[:, columns].astype(jnp.float32)
            normed[:, columns] = (block * scale * weight).astype(jnp.bfloat16)
        own = pl.ds(pl.multiple_of(owner * rows, rows), rows)
        held[...] = spread[own, :part].astype(jnp.bfloat16)
        adapter_part(owner, ident, normed, adapters, correction, capacity)


def norm_kernel(count, capacity, *refs):
    chunks, rest = refs[:count][::-1], refs[count:]
    ident, gain, *adapters, normed = rest[:6]
    correction = rest[6:]
    owner = lax.axis_index("wide")
    rows, part = chunks[0].shape
    squares = jnp.zeros((rows, 1), jnp.float32)
    for chunk in chunks:
        block = chunk[...].astype(jnp.float32)
        squares += jnp.sum(block * block, 1, keepdims=True)
    scale = lax.rsqrt(squares / gain.shape[1] + epsilon)
    for k, chunk in enumerate(chunks):
        columns = pl.ds(pl.multiple_of((owner ^ k) * part, part), part)
        weight = gain[:, columns].astype(jnp.float32)
        normed[:, columns] = (chunk[...].astype(jnp.float32) * scale * weight).astype(jnp.bfloat16)
    adapter_part(owner, ident, normed, adapters, correction, capacity)


def project_kernel(normed, query, out):
    def store(columns, product):
        out[:, columns] = product

    matmul_into(store, normed, query, STEP)


def narrow_kernel(normed, key, value, out):
    narrow = key.shape[1]
    out[:, :narrow] = dot(normed[...], key[...])
    out[:, narrow:] = dot(normed[...], value[...])


def project_first_kernel(first, tick, normed, whole_query, _, out, query, sems):
    copies = []
    for i in range(1, query.shape[1] // first):
        here = pl.ds(i * first, first)
        copies.append(
            pltpu.make_async_copy(whole_query.at[:, here], query.at[:, here], sems.at[i - 1])
        )
    for copy in copies[:2]:
        copy.start()
    live = lax.axis_index("segment") == tick
    for i in range(len(copies) + 1):
        if i:
            copies[i - 1].wait()
            if i + 1 < len(copies):
                copies[i + 1].start()

        @pl.when(live)
        def _():
            here = slice(i * first, (i + 1) * first)
            out[:, here] = dot(normed[...], query[:, here])


def received_rows(received):
    half = received[0].shape[0] // 2
    return [ref[(j % 2) * half : (j % 2 + 1) * half, :] for j, ref in enumerate(received)]


def correct_kernel(count, capacity, base, narrow, ident, *refs):
    received, outs = refs[:count], refs[count:]
    owner = lax.axis_index("wide")
    rows = base.shape[0]
    own_rows = rows // count
    slots = count * capacity
    place = lax.broadcasted_iota(jnp.int32, (rows, rows), 0)
    other = lax.broadcasted_iota(jnp.int32, (rows, rows), 1)
    own = ident[:, :1]
    flat = jnp.where(place == other, own, 0.0).astype(jnp.bfloat16)
    line = dot(jnp.ones((rows, rows), jnp.bfloat16), flat)
    rank = jnp.sum(jnp.where((own == line) & (other < place), 1.0, 0.0), 1, keepdims=True)
    slot = lax.broadcasted_iota(jnp.int32, (rows, slots), 1)
    source = ((slot // capacity) ^ owner).astype(jnp.float32)
    hit = (source == own) & ((slot % capacity).astype(jnp.float32) == rank)
    table = jnp.where(hit, 1.0, 0.0).astype(jnp.bfloat16)
    placed = dot(table, jnp.concatenate(received_rows(received), 0))
    query_cols, key_cols = base.shape[1], narrow.shape[1] // 2
    first = base[...] + placed[:, :query_cols]
    middle = narrow[:, :key_cols]
    last = narrow[:, key_cols:] + placed[:, query_cols:]
    packed = jnp.concatenate([first, middle, last], 1).astype(jnp.bfloat16)
    by_destination(owner, packed, own_rows, outs)


def by_destination(owner, packed, own_rows, outs):
    rows = packed.shape[0]
    place = lax.broadcasted_iota(jnp.int32, (rows, rows), 0)
    other = lax.broadcasted_iota(jnp.int32, (rows, rows), 1)
    hit = (((place // own_rows) ^ owner) == other // own_rows) & (
        place % own_rows == other % own_rows
    )
    order = jnp.where(hit, 1.0, 0.0).astype(jnp.bfloat16)
    sorted_rows = dot(order, packed).astype(jnp.bfloat16)
    for k, out in enumerate(outs):
        out[...] = sorted_rows[k * 2 * own_rows : (k + 1) * 2 * own_rows, :]


def attend_kernel(chips, lengths, near_lengths, *refs):
    arrived, rest = refs[:chips][::-1], refs[chips:]
    cosine, sine, keys, values, near_keys, near_values, out, scores, weights = rest
    chip = lax.axis_index("wide") // 2
    own_rows, span = keys.shape[:2]
    chip_rows = 2 * own_rows
    rows = GROUP * chip_rows
    cos, sin = cosine[...], sine[...]
    position = lax.broadcasted_iota(jnp.int32, (2 * rows, span), 1)
    valid = position < row_lengths(lengths, near_lengths, (2 * rows, span), 2 * GROUP)
    score_scale = HD ** (-0.5)

    def turned(vectors):
        return vectors * cos + pltpu.roll(vectors, HD // 2, 1) * sin

    def rounded(vectors):
        return vectors.astype(jnp.bfloat16).astype(jnp.float32)

    pieces = []
    for ref in arrived:
        packed = ref[...].astype(jnp.float32)
        heads = [packed[:, i * HD : (i + 1) * HD] for i in range(GROUP)]
        fresh = [packed[:, GROUP * HD :]] * GROUP
        pieces += [jnp.concatenate(heads, 0), jnp.concatenate(fresh, 0)]
    out_row = lax.broadcasted_iota(jnp.int32, (rows, rows), 0)
    src_row = lax.broadcasted_iota(jnp.int32, (rows, rows), 1)
    same = (out_row // GROUP == src_row % chip_rows) & (out_row % GROUP == src_row // chip_rows)
    order = jnp.where(same, 1.0, 0.0).astype(jnp.bfloat16)
    sorted_rows = dot(order, jnp.concatenate(pieces, 1).astype(jnp.bfloat16))
    band = 2 * GROUP

    def woven(one, two):
        bands = [slice(r * GROUP, (r + 1) * GROUP) for r in range(chip_rows)]
        return jnp.concatenate([part[rows_of] for rows_of in bands for part in (one, two)], 0)

    def pair_lanes(p):
        return pl.ds(pl.multiple_of((chip // 2 ^ p) * 2 * HD, 2 * HD), 2 * HD)

    even = chip % 2 == 0
    zero = jnp.zeros((rows, HD), jnp.float32)
    pairs = range(chips // 2)
    fresh = []
    for p in pairs:
        wide, own, new_values = [], [], []
        for n in range(2):
            piece = sorted_rows[:, (2 * p + n) * 3 * HD : (2 * p + n + 1) * 3 * HD]
            query = rounded(turned(piece[:, :HD]))
            new_key = rounded(turned(piece[:, HD : 2 * HD]))
            own.append(jnp.sum(query * new_key, 1, keepdims=True) * score_scale)
            new_values.append(piece[:, 2 * HD :])
            left = even if n == 0 else jnp.logical_not(even)
            wide.append(
                jnp.concatenate([jnp.where(left, query, zero), jnp.where(left, zero, query)], 1)
            )
        fresh.append((woven(*own), woven(*new_values)))
        wide = woven(*wide).astype(jnp.bfloat16)
        for r in range(chip_rows):
            first = (p * chip_rows + r) * band
            scores[first : first + band, :] = lax.dot_general(
                wide[r * band : (r + 1) * band, :],
                (keys, near_keys)[r // own_rows][r % own_rows, :, pair_lanes(p)],
                (((1,), (1,)), ((), ())),
                preferred_element_type=jnp.float32,
            )
    parts = []
    for p, (own, new_value) in enumerate(fresh):
        here = slice(p * 2 * rows, (p + 1) * 2 * rows)
        found = jnp.where(valid, scores[here, :] * score_scale, -1e30)
        top = jnp.maximum(jnp.max(found, 1, keepdims=True), own)
        past = jnp.where(valid, jnp.exp(found - top), 0.0)
        own = jnp.exp(own - top)
        total = jnp.sum(past, 1, keepdims=True) + own
        weights[here, :] = (past / total).astype(jnp.bfloat16)
        parts.append(rounded(own / total) * new_value)
    for p, own_part in enumerate(parts):
        mixed = []
        for r in range(chip_rows):
            first = (p * chip_rows + r) * band
            found = dot(
                weights[first : first + band, :],
                (values, near_values)[r // own_rows][r % own_rows, :, pair_lanes(p)],
            )
            mine = own_part[r * band : (r + 1) * band, :]
            one = jnp.where(even, found[:GROUP, :HD], found[:GROUP, HD:]) + mine[:GROUP]
            two = jnp.where(even, found[GROUP:, HD:], found[GROUP:, :HD]) + mine[GROUP:]
            both = [jnp.where(even, one, two), jnp.where(even, two, one)]
            mixed.append(jnp.concatenate(both, 1))
        out[:, pair_lanes(p)] = jnp.concatenate(mixed, 0).astype(jnp.bfloat16)


def attended_rows(owner, chunks, own_rows, rows_ref):
    count = len(chunks)
    chips = count // 2
    rows = own_rows * count
    total = rows * GROUP
    out = lax.broadcasted_iota(jnp.int32, (total, total), 0)
    src = lax.broadcasted_iota(jnp.int32, (total, total), 1)
    device_out = (out // own_rows) % count
    chip_rows = 2 * own_rows
    row_src = (src // GROUP) % chip_rows
    near = (out // rows == src % GROUP) & (out % own_rows == row_src % own_rows)
    for core in range(2):
        stack = jnp.concatenate([chunks[2 * k + core][...] for k in range(chips)], 0)
        device_src = owner ^ (2 * (src // (GROUP * chip_rows)) + core) ^ (row_src // own_rows)
        hit = near & (device_out == device_src)
        spread = dot(jnp.where(hit, 1.0, 0.0).astype(jnp.bfloat16), stack).astype(jnp.bfloat16)
        first = (owner ^ core) % 2
        for i in range(chips):
            for j in range(GROUP):
                head = (2 * i + first) * GROUP + j
                rows_ref[:, pl.ds(pl.multiple_of(head * HD, HD), HD)] = spread[
                    j * rows : (j + 1) * rows, i * HD : (i + 1) * HD
                ]


def leave_kernel(count, own_rows, tick, *refs):
    chunks, rest = refs[:count], refs[count:]
    held, result = rest[0], rest[1] if tick else None
    matrix, out, kept, *outs, rows_ref = rest[2 if tick else 1 :]
    kept[...] = result[...] if tick else jnp.zeros_like(kept)

    @pl.when(lax.axis_index("segment") == tick)
    def _():
        attended_rows(lax.axis_index("wide"), chunks, own_rows, rows_ref)

        def store(columns, product):
            total = held[:, columns].astype(jnp.float32) + product
            out[:, columns] = total.astype(jnp.bfloat16)
            kept[:, columns] = total.astype(jnp.bfloat16)

        matmul_into(store, rows_ref, matrix, 2 * STEP)

    if outs:
        by_destination(lax.axis_index("wide"), kept[...], own_rows, outs)


def join_kernel(count, *refs):
    blocks, out = refs[:count][::-1], refs[count]
    for j, block in enumerate(blocks):
        rows = block.shape[0] // 2
        half = block[(j % 2) * rows : (j % 2 + 1) * rows, :]
        width = half.shape[1]
        columns = pl.ds(pl.multiple_of((lax.axis_index("wide") ^ j) * width, width), width)
        for m in range(out.shape[1]):
            local_rows = out.shape[2]
            out[0, m, :, columns] = half[m * local_rows : (m + 1) * local_rows, :]


def on_device_by_head(
    entering_hidden,
    row_adapter_index,
    lengths,
    input_norm_gain,
    query_matrix,
    key_matrix,
    value_matrix,
    output_matrix,
    adapter_down_maps,
    adapter_up_query,
    adapter_up_value,
    rotated_key_cache,
    cached_values,
):
    segments = lax.axis_size("segment")
    count = lax.axis_size("wide")
    micro, local_rows, width = entering_hidden.shape
    own_rows = micro * local_rows
    rows = own_rows * count
    capacity = CAP * micro
    part = width // count
    query_cols, key_cols = query_matrix.shape[2], key_matrix.shape[2]
    packed_cols = query_cols + 2 * key_cols
    span = rotated_key_cache.shape[3]

    chips = count // 2
    head_lanes = chips * HD
    query_weight = query_matrix[0]
    output_weight = output_matrix[0]
    adapters = [adapter_down_maps[0], adapter_up_query[0], adapter_up_value[0]]
    caches = [cache[0].reshape(own_rows, span, -1) for cache in (rotated_key_cache, cached_values)]
    near_lengths = swapped(lengths, 1)
    gain = input_norm_gain
    half = HD // 2
    inverse = np.tile(rope_base ** (-np.arange(half) / half), 2).astype(np.float32)[None]

    def blocks_of(slots, columns):
        return [jax.ShapeDtypeStruct((2 * slots, columns), jnp.bfloat16)] * chips

    normed_shape = jax.ShapeDtypeStruct((rows, width), jnp.bfloat16)
    held_shape = jax.ShapeDtypeStruct((rows, part), jnp.bfloat16)
    ident_shape = jax.ShapeDtypeStruct((rows, HD), jnp.float32)
    base_shape = jax.ShapeDtypeStruct((rows, query_cols), jnp.float32)
    narrow_shape = jax.ShapeDtypeStruct((rows, 2 * key_cols), jnp.float32)
    angle_shape = jax.ShapeDtypeStruct((GROUP * 2 * own_rows, HD), jnp.float32)
    correction_shapes = blocks_of(capacity, query_cols + key_cols)
    query_first = query_cols // 4
    output_first = part // 2

    names = pltpu.with_memory_space_constraint(row_adapter_index.transpose(0, 2, 1), pltpu.HBM)
    (entering,) = call(
        open_kernel,
        [jax.ShapeDtypeStruct((rows, part + HD), jnp.bfloat16)],
        [(entering_hidden, VMEM), (names, pl.BlockSpec(memory_space=pl.ANY))],
        [pltpu.SMEM(names.shape, names.dtype), pltpu.SemaphoreType.DMA],
        name="open",
    )
    projections, output_parts, halves, angles = [], [], [None, None], []
    held = ident = None
    result = None
    blocks = []
    for tick in range(segments):
        if tick == 0:

            def load_first():
                sources = [*adapters, key_matrix[0], value_matrix[0], query_weight, *caches]
                small = [(entering, VMEM)]
                shape = (own_rows, span, head_lanes)
                shapes = [source.shape for source in sources[:6]]
                shapes += [shape] * 2

                def plan(sources, outs):
                    pairs = list(zip(sources[:5], outs[:5]))
                    pairs.append((sources[5].at[:, :query_first], outs[5].at[:, :query_first]))
                    return pairs + half_of(1, sources[6:], outs[6:])

                found, (token,) = loaded(
                    sources, shapes, plan, 6 + 2 * chips, small, [TOKEN], token_of
                )
                adapters[:], projections[:] = found[:3], found[3:6]
                halves[2:] = found[6:]
                return token

            chunks, _ = gathered(entering, load_first)
            normed, held, ident, *found = call(
                functools.partial(enter_kernel, count, own_rows, capacity, tick),
                [normed_shape, held_shape, ident_shape] + correction_shapes,
                [(c, VMEM) for c in chunks]
                + [(near_lengths, pl.BlockSpec(memory_space=pl.ANY)), (gain, VMEM)],
                [pltpu.VMEM((count * rows, part + HD), jnp.float32)],
                kept=adapters,
                through=halves[2:],
                name="enter",
            )
            halves[2:] = [swapped(array, 1) for array in found[chips:]]
        else:
            chunks = passed_on(held, tick - 1)
            held = chunks[0]
            normed, *found = call(
                while_live(tick, functools.partial(norm_kernel, count, capacity)),
                [normed_shape] + correction_shapes,
                [(c, VMEM) for c in chunks[::-1]] + [(ident, VMEM), (gain, VMEM)],
                kept=adapters,
                name="norm",
            )
        correction = found[:chips]

        def project():
            return call(
                while_live(tick, project_kernel),
                [base_shape],
                [(normed, VMEM)],
                kept=projections[2:],
                cost=16,
                name="project",
            )[0]

        def project_first():
            base, projections[2] = pl.pallas_call(
                functools.partial(project_first_kernel, query_first, tick),
                out_shape=[base_shape, pltpu.VMEM(query_weight.shape, jnp.bfloat16)],
                in_specs=[VMEM, pl.BlockSpec(memory_space=pl.ANY), VMEM],
                out_specs=[VMEM, VMEM],
                input_output_aliases={2: 1},
                scratch_shapes=[pltpu.SemaphoreType.DMA((query_cols // query_first - 1,))],
                compiler_params=pltpu.CompilerParams(vmem_limit_bytes=8 * MIB),
                cost_estimate=pl.CostEstimate(
                    flops=0, transcendentals=0, bytes_accessed=16 * MIB
                ),
                name="project",
            )(
                normed,
                pltpu.with_memory_space_constraint(query_weight, pltpu.HBM),
                resident(projections[2]),
            )
            return base

        received, base = exchanged(correction, project if tick else project_first)
        received = [part for one in received for part in (one, swapped(one, 1))]
        (narrow,) = call(
            while_live(tick, narrow_kernel),
            [narrow_shape],
            [(normed, VMEM)],
            kept=projections[:2],
            cost=4,
            name="narrow",
        )
        packed = call(
            while_live(
                tick, functools.partial(correct_kernel, count, capacity)
            ),
            blocks_of(own_rows, packed_cols),
            [(base, VMEM), (narrow, VMEM), (ident, VMEM)] + [(r, VMEM) for r in received],
            name="correct",
        )

        def load_part():
            small = [(lengths, SMEM), (near_lengths, SMEM), (jnp.asarray(inverse), VMEM)]
            found, angles[:] = loaded(
                [output_weight, *caches],
                [output_weight.shape] + [(own_rows, span, head_lanes)] * 2,
                lambda sources, outs: [
                    (sources[0].at[:, :output_first], outs[0].at[:, :output_first])
                ]
                + half_of(0, sources[1:], outs[1:]),
                1 + 2 * chips,
                small,
                [angle_shape, angle_shape],
                angle_work,
            )
            output_parts[:], halves[:2] = found[:1], found[1:]
            return angles[0]

        def load_output():
            output_parts[0], token = pl.pallas_call(
                functools.partial(load_rest_kernel, output_first),
                out_shape=[pltpu.VMEM(output_weight.shape, jnp.bfloat16), TOKEN],
                in_specs=[pl.BlockSpec(memory_space=pl.ANY), VMEM, VMEM],
                out_specs=[VMEM, VMEM],
                input_output_aliases={2: 0},
                scratch_shapes=[pltpu.SemaphoreType.DMA],
                compiler_params=pltpu.CompilerParams(vmem_limit_bytes=4 * MIB),
                cost_estimate=pl.CostEstimate(
                    flops=0, transcendentals=0, bytes_accessed=8 * MIB
                ),
                name="load",
            )(
                pltpu.with_memory_space_constraint(output_weight, pltpu.HBM),
                attended,
                resident(output_parts[0]),
            )
            return token

        arrived, _ = exchanged(packed, None if tick else load_part)
        attended, *_ = call(
            while_live(tick, functools.partial(attend_kernel, chips)),
            [jax.ShapeDtypeStruct((GROUP * 2 * own_rows, head_lanes), jnp.bfloat16)],
            [(lengths, SMEM), (near_lengths, SMEM)]
            + [(a, VMEM) for a in [*arrived[::-1], *angles]],
            [
                pltpu.VMEM((chips * GROUP * 2 * own_rows, span), jnp.float32),
                pltpu.VMEM((chips * GROUP * 2 * own_rows, span), jnp.bfloat16),
            ],
            kept=halves,
            name="attend",
        )
        chunks, _ = gathered(attended, None if tick else load_output)
        last = tick == segments - 1
        held, result, *found = call(
            functools.partial(leave_kernel, count, own_rows, tick),
            [held_shape, held_shape] + (blocks_of(own_rows, part) if last else []),
            [(c, VMEM) for c in chunks]
            + [(held, VMEM)] + ([(result, VMEM)] if tick else []),
            [pltpu.VMEM((rows, width), jnp.bfloat16)],
            kept=output_parts,
            name="leave",
        )
        blocks = found
    far, _ = exchanged(blocks)
    far = [part for one in far for part in (one, swapped(one, 1))]
    (joined,) = call(
        functools.partial(join_kernel, count),
        [jax.ShapeDtypeStruct((1, micro, local_rows, width), jnp.bfloat16)],
        [(one, VMEM) for one in far[::-1]],
        name="join",
    )
    return joined


def passed_along(value, axis, steps):
    count = lax.axis_size(axis)
    leading, last = (max(0, -steps), min(count, count - steps))
    return lax.ppermute(value, axis, [(source, source + steps) for source in range(leading, last)])


def rotary(vectors, positions):
    half = vectors.shape[-1] // 2
    inverse = rope_base ** (-jnp.arange(half, dtype=jnp.float32) / half)
    angles = positions.astype(jnp.float32)[:, None] * inverse[None, :]
    cosine = jnp.cos(angles)[:, None, :]
    sine = jnp.sin(angles)[:, None, :]
    front = vectors[..., :half]
    back = vectors[..., half:]
    return jnp.concatenate([front * cosine - back * sine, back * cosine + front * sine], -1)


def attend(query_vector, new_key, fresh_value, positions, key_block, value_block):
    rows = query_vector.shape[0]
    group = HEADS // KVH
    rotated_rows = rotary(
        query_vector.astype(jnp.float32).reshape(rows, HEADS, HD), positions
    ).astype(jnp.bfloat16)
    rotated_rows = rotated_rows.reshape(rows, KVH, group, HD)
    self_key = rotary(new_key.astype(jnp.float32).reshape(rows, KVH, HD), positions).astype(
        jnp.bfloat16
    )
    keys_past = key_block.reshape(rows, -1, KVH, HD)
    values_past = value_block.reshape(rows, -1, KVH, HD)
    score_scale = HD ** (-0.5)
    past = (
        jnp.einsum("bkgd,bpkd->bkgp", rotated_rows, keys_past, preferred_element_type=jnp.float32)
        * score_scale
    )
    self_scores = (
        jnp.einsum("rice,rie->ric", rotated_rows, self_key, preferred_element_type=jnp.float32)
        * score_scale
    )
    valid = jnp.arange(keys_past.shape[1])[None, :] < positions[:, None]
    past = jnp.where(valid[:, None, None, :], past, -1e30)
    top = jnp.maximum(jnp.max(past, -1), self_scores)
    past_exp = jnp.where(valid[:, None, None, :], jnp.exp(past - top[..., None]), 0.0)
    own_exp = jnp.exp(self_scores - top)
    total = jnp.sum(past_exp, -1) + own_exp
    past_weights = (past_exp / total[..., None]).astype(jnp.bfloat16)
    own_weights = (own_exp / total).astype(jnp.bfloat16)
    mixed = jnp.einsum(
        "bkgp,bpkd->bkgd", past_weights, values_past, preferred_element_type=jnp.float32
    )
    mixed = (
        mixed
        + own_weights.astype(jnp.float32)[..., None]
        * fresh_value.reshape(rows, KVH, HD).astype(jnp.float32)[:, :, None, :]
    )
    return mixed.reshape(rows, HEADS * HD).astype(jnp.bfloat16)


def on_device(
    entering_hidden,
    row_adapter_index,
    lengths,
    input_norm_gain,
    query_matrix,
    key_matrix,
    value_matrix,
    output_matrix,
    adapter_down_maps,
    adapter_up_query,
    adapter_up_value,
    rotated_key_cache,
    cached_values,
):
    segments = lax.axis_size("segment")
    segment = lax.axis_index("segment")
    devices = lax.axis_size("wide")
    owner = lax.axis_index("wide")
    small_batch, local_rows, width = entering_hidden.shape
    listed = lax.all_gather(row_adapter_index, "wide", axis=1, tiled=True)[:, :, 0]
    groups = small_batch // small_batch
    capacity = CAP * small_batch
    kept_entries = adapter_down_maps.shape[1]
    adapters = kept_entries * devices
    mine = owner * kept_entries + jnp.arange(kept_entries)
    gain = input_norm_gain[0].astype(jnp.float32)
    query_cols = query_matrix.shape[2]
    key_cols = key_matrix.shape[2]
    passed = jnp.zeros((small_batch * local_rows, width), jnp.bfloat16)
    results = jnp.zeros((small_batch, local_rows, width), jnp.bfloat16)
    ticks = groups + segments - 1
    for tick in range(ticks):
        if tick < groups:
            fresh = entering_hidden.reshape(small_batch * local_rows, width)
        else:
            fresh = jnp.zeros_like(passed)
        rows = jnp.where(segment == 0, fresh, passed)
        index = tick - segment
        live = (index >= 0) & (index < groups)
        index = jnp.clip(index, 0, groups - 1)
        block_rows = rows.shape[0]
        idents = listed
        idents = idents.reshape(small_batch, devices, local_rows).transpose(1, 0, 2).reshape(-1)
        positions = lengths.reshape(-1)
        key_block = rotated_key_cache[0]
        key_block = key_block.reshape(block_rows, key_block.shape[2], key_block.shape[3])
        value_block = cached_values[0]
        value_block = value_block.reshape(block_rows, value_block.shape[2], value_block.shape[3])
        values = rows.astype(jnp.float32)
        normalized_rows = (
            values * lax.rsqrt(jnp.mean(values * values, 1, keepdims=True) + epsilon) * gain
        ).astype(jnp.bfloat16)
        gathered = lax.all_gather(normalized_rows, "wide", axis=0, tiled=True)
        total_rows = gathered.shape[0]
        matches = (idents[None, :] == mine[:, None]).astype(jnp.int32)
        ranks = jnp.cumsum(matches, 1) - 1
        chosen = (matches[:, None, :] == 1) & (
            ranks[:, None, :] == jnp.arange(capacity)[None, :, None]
        )
        chosen = chosen.reshape(kept_entries * capacity, total_rows)
        selected_rows = jnp.dot(
            chosen.astype(jnp.bfloat16), gathered, preferred_element_type=jnp.float32
        ).astype(jnp.bfloat16)
        selected_rows = selected_rows.reshape(kept_entries, capacity, width)
        reduced = jnp.einsum(
            "bpy,byf->bpf", selected_rows, adapter_down_maps[0], preferred_element_type=jnp.float32
        ).astype(jnp.bfloat16)
        member = (idents[:, None] == jnp.arange(adapters)[None, :]).astype(jnp.int32)
        order = jnp.sum(jnp.cumsum(member, 0) * member, 1) - 1
        slot = idents * capacity + order
        slot_table = slot[:, None] == jnp.arange(adapters * capacity)[None, :]
        query_slots = jnp.einsum(
            "acr,are->ace",
            reduced[..., :ADAPTER_RANK],
            adapter_up_query[0],
            preferred_element_type=jnp.float32,
        )
        value_slots = jnp.einsum(
            "acr,are->ace",
            reduced[..., ADAPTER_RANK:],
            adapter_up_value[0],
            preferred_element_type=jnp.float32,
        )
        joined = jnp.concatenate(
            [
                query_slots.reshape(kept_entries * capacity, devices, -1),
                value_slots.reshape(kept_entries * capacity, devices, -1),
            ],
            2,
        )
        received = lax.all_to_all(joined, "wide", split_axis=1, concat_axis=0, tiled=True)
        received = received.reshape(adapters * capacity, -1)
        placed = jnp.dot(slot_table.astype(jnp.float32), received, precision=lax.Precision.HIGHEST)
        query_adjustment = placed[:, :query_cols]
        value_adjustment = placed[:, query_cols:]
        query_vector = (
            jnp.dot(gathered, query_matrix[0], preferred_element_type=jnp.float32)
            + adapter_scale * query_adjustment
        ).astype(jnp.bfloat16)
        new_key = jnp.dot(gathered, key_matrix[0], preferred_element_type=jnp.float32).astype(
            jnp.bfloat16
        )
        fresh_value = (
            jnp.dot(gathered, value_matrix[0], preferred_element_type=jnp.float32)
            + adapter_scale * value_adjustment
        ).astype(jnp.bfloat16)
        packed = jnp.concatenate([query_vector, new_key, fresh_value], 1)
        arrived = lax.all_to_all(packed, "wide", split_axis=0, concat_axis=1, tiled=True).reshape(
            block_rows, devices, -1
        )
        query_rows_local = arrived[:, :, :query_cols].reshape(block_rows, -1)
        key_rows_local = arrived[:, :, query_cols : query_cols + key_cols].reshape(block_rows, -1)
        value_rows_local = arrived[:, :, query_cols + key_cols :].reshape(block_rows, -1)
        attended = attend(
            query_rows_local, key_rows_local, value_rows_local, positions, key_block, value_block
        )
        columns = jnp.dot(
            lax.all_gather(attended, "wide", axis=0, tiled=True),
            output_matrix[0],
            preferred_element_type=jnp.float32,
        )
        returned = lax.all_to_all(columns, "wide", split_axis=0, concat_axis=1, tiled=True)
        outcome = (values + returned).astype(jnp.bfloat16)
        updated = outcome.reshape(small_batch, local_rows, width)
        results = jnp.where(live, updated, results)
        if tick + 1 < ticks:
            passed = passed_along(outcome, "segment", 1)
    return results[None]


def solution(mesh):
    placed = (
        P(None, "wide", None),
        P(None, "wide", None),
        P(None, "wide"),
        P("segment", None),
        P("segment", None, "wide"),
        P("segment", None, "wide"),
        P("segment", None, "wide"),
        P("segment", None, "wide"),
        P("segment", "wide", None, None),
        P("segment", "wide", None, None),
        P("segment", "wide", None, None),
        P("segment", None, "wide", None, None),
        P("segment", None, "wide", None, None),
    )
    by_head = mesh.shape["wide"] == KVH
    return jax.shard_map(
        on_device_by_head if by_head else on_device,
        mesh=mesh,
        in_specs=placed,
        out_specs=P("segment", None, "wide", None),
        check_vma=False,
    )
```

```python
import functools

import jax
import jax.numpy as jnp
import numpy as np
from jax import lax
from jax.experimental import pallas as pl
from jax.experimental.pallas import tpu as pltpu
from jax.sharding import PartitionSpec as P

HEADS = 64
KVH = 8
HD = 128
ADAPTER_RANK = 64
CAP = 4


adapter_scale = 0.5
rope_base = 500000.0
epsilon = 1e-05

GROUP = HEADS // KVH
MIB = 1 << 20
STEP = 256
HOP_ORDER = (2, 3, 1, 0)
WORK_ORDER = (1, 0, 2)
HEAD_ORDER = (2, 3, 1, 0)
ROW_ORDER = (0, 2, 1, 3)
LAST_ORDER = (3, 2, 1, 0)
VMEM = pl.BlockSpec(memory_space=pltpu.VMEM)
SMEM = pl.BlockSpec(memory_space=pltpu.SMEM)


def swapped(value, bits):
    count = lax.axis_size("wide")
    return lax.ppermute(value, "wide", [(i, i ^ bits) for i in range(count)])


def then(arrays, work):
    if work is None:
        return arrays, None
    done = work()
    arrays = [arrays[k] for k in WORK_ORDER]
    arrays = pl.pallas_call(
        lambda *refs: None,
        out_shape=[jax.ShapeDtypeStruct(array.shape, array.dtype) for array in arrays],
        in_specs=[VMEM] * len(arrays) + [pl.BlockSpec(memory_space=pl.ANY)],
        out_specs=[VMEM] * len(arrays),
        input_output_aliases={i: i for i in range(len(arrays))},
        compiler_params=pltpu.CompilerParams(vmem_limit_bytes=MIB),
        name="then",
    )(*arrays, done)
    return [arrays[WORK_ORDER.index(k)] for k in range(len(WORK_ORDER))], done


def gathered(value, work=None):
    count = lax.axis_size("wide")
    far = [swapped(value, k) for k in range(2, count, 2)]
    far, done = then(far, work)
    found = [part for one in [value, *far] for part in (one, swapped(one, 1))]
    return found, done


def passed_on(value, s):
    count = lax.axis_size("wide")

    def shifted(bits):
        pairs = [(s * count + i, (s + 1) * count + (i ^ bits)) for i in range(count)]
        return lax.ppermute(value, ("segment", "wide"), pairs)

    far = [shifted(bits) for bits in range(0, count, 2)]
    return [part for one in far for part in (one, swapped(one, 1))]


def exchanged(blocks, work=None):
    far = [swapped(block, 2 * k) for k, block in enumerate(blocks) if k]
    far, done = then(far, work)
    return [blocks[0], *far], done


def resident(weight):
    return pltpu.with_memory_space_constraint(weight, pltpu.VMEM)


def call(body, out_shape, operands, scratch=(), limit=8, kept=(), through=(), cost=1, name=None):
    outs, count = list(out_shape), len(operands) + len(kept)
    inner = body
    if through:

        def inner(*refs):
            inputs = count + len(through)
            shown = inputs + len(outs)
            body(*refs[:count], *refs[inputs:shown], *refs[shown + len(through) :])

    found = pl.pallas_call(
        inner,
        out_shape=outs + [pltpu.VMEM(array.shape, array.dtype) for array in through],
        in_specs=[spec for _, spec in operands] + [VMEM] * (len(kept) + len(through)),
        out_specs=[VMEM] * (len(outs) + len(through)),
        input_output_aliases={count + i: len(outs) + i for i in range(len(through))},
        scratch_shapes=list(scratch),
        compiler_params=pltpu.CompilerParams(vmem_limit_bytes=limit * MIB),
        cost_estimate=pl.CostEstimate(flops=0, transcendentals=0, bytes_accessed=cost * MIB),
        name=name,
    )(*[array for array, _ in operands], *[resident(array) for array in [*kept, *through]])
    return list(found)


def load_kernel(sizes, plan, work, *refs):
    sources, small, outs, more = [], [], [], []
    refs = list(refs)
    for group, size in zip((sources, small, outs, more), sizes, strict=True):
        group.extend(refs[:size])
        del refs[:size]
    copies = [
        pltpu.make_async_copy(source, out, refs[0].at[i])
        for i, (source, out) in enumerate(plan(sources, outs))
    ]
    for copy in copies:
        copy.start()
    work(small, more)
    for copy in copies:
        copy.wait()


def loaded(sources, shapes, plan, copies, small, more, work):
    moved = sum(2 * int(np.prod(shape)) for shape in shapes)
    found = pl.pallas_call(
        functools.partial(
            load_kernel, (len(sources), len(small), len(shapes), len(more)), plan, work
        ),
        out_shape=[pltpu.VMEM(shape, jnp.bfloat16) for shape in shapes] + list(more),
        in_specs=[pl.BlockSpec(memory_space=pl.ANY)] * len(sources) + [spec for _, spec in small],
        out_specs=[VMEM] * (len(shapes) + len(more)),
        scratch_shapes=[pltpu.SemaphoreType.DMA((copies,))],
        compiler_params=pltpu.CompilerParams(vmem_limit_bytes=4 * MIB),
        cost_estimate=pl.CostEstimate(flops=0, transcendentals=0, bytes_accessed=moved),
        name="load",
    )(
        *[pltpu.with_memory_space_constraint(source, pltpu.HBM) for source in sources],
        *[array for array, _ in small],
    )
    return found[: len(shapes)], found[len(shapes) :]


def half_of(other, sources, outs):
    core = (lax.axis_index("wide") + other) % 2
    pairs = []
    for source, out in zip(sources, outs, strict=True):
        for i in range(out.shape[2] // HD):
            there = pl.ds(pl.multiple_of((2 * i + core) * HD, HD), HD)
            pairs.append((source.at[:, :, there], out.at[:, :, pl.ds(i * HD, HD)]))
    return pairs


TOKEN = jax.ShapeDtypeStruct((8, HD), jnp.float32)


def token_of(small, more):
    more[0][...] = small[0][:8, :HD].astype(jnp.float32)


def load_rest_kernel(first, source, after, _, out, token, sem):
    copy = pltpu.make_async_copy(source.at[:, first:], out.at[:, first:], sem)
    copy.start()
    token[...] = after[:8, :HD].astype(jnp.float32)
    copy.wait()


def dot(left, right):
    return jnp.dot(left, right, preferred_element_type=jnp.float32)


def matmul_into(store, source, weight, step):
    def one(i, carry):
        columns = pl.ds(pl.multiple_of(i * step, step), step)
        store(columns, dot(source[...], weight[:, columns]))
        return carry

    lax.fori_loop(0, weight.shape[1] // step, one, 0)


def while_live(tick, body):
    def run(*refs):
        pl.when(lax.axis_index("segment") == tick)(lambda: body(*refs))

    return run


def by_part(owner, chunks, own_rows):
    count = len(chunks)
    parts = chunks[0].shape[0] // own_rows
    total = count * parts * own_rows
    stack = jnp.concatenate([chunk[...] for chunk in chunks], 0)
    out = lax.broadcasted_iota(jnp.int32, (total, total), 0)
    src = lax.broadcasted_iota(jnp.int32, (total, total), 1)
    rows = own_rows
    part_out = out // (rows * count)
    device_out = (out // rows) % count
    part_src = (src // rows) % parts
    device_src = (src // (rows * parts)) ^ owner
    hit = (part_out == part_src) & (device_out == device_src) & (out % rows == src % rows)
    return dot(jnp.where(hit, 1.0, 0.0).astype(jnp.bfloat16), stack)


def adapter_part(owner, ident, normed, adapter, outs, capacity):
    down, up_query, up_value = adapter
    rows = normed.shape[0]
    count = 2 * len(outs)
    low = dot(normed[...], down[0]).astype(jnp.bfloat16)
    place = lax.broadcasted_iota(jnp.int32, (rows, rows), 0)
    other = lax.broadcasted_iota(jnp.int32, (rows, rows), 1)
    mine = jnp.where(ident[:, :1] == owner.astype(jnp.float32), 1.0, 0.0)
    flat = jnp.where(place == other, mine, 0.0).astype(jnp.bfloat16)
    before = jnp.where(place < other, mine, 0.0).astype(jnp.bfloat16)
    ones = jnp.ones((capacity, rows), jnp.bfloat16)
    member = dot(ones, flat)
    rank = dot(ones, before)
    slot = lax.broadcasted_iota(jnp.int32, (capacity, rows), 0).astype(jnp.float32)
    chosen = jnp.where((member > 0.5) & (rank == slot), 1.0, 0.0).astype(jnp.bfloat16)
    picked = dot(chosen, low).astype(jnp.bfloat16)
    query_cols = up_query.shape[2] // count
    value_cols = up_value.shape[2] // count
    for j in range(count):
        out, there = outs[j // 2], owner ^ j
        slots = slice((j % 2) * capacity, (j % 2 + 1) * capacity)
        columns = pl.ds(pl.multiple_of(there * query_cols, query_cols), query_cols)
        for_query = dot(picked[:, :ADAPTER_RANK], up_query[0, :, columns]) * adapter_scale
        out[slots, :query_cols] = for_query.astype(jnp.bfloat16)
        columns = pl.ds(pl.multiple_of(there * value_cols, value_cols), value_cols)
        for_value = dot(picked[:, ADAPTER_RANK:], up_value[0, :, columns]) * adapter_scale
        out[slots, query_cols:] = for_value.astype(jnp.bfloat16)


def open_kernel(hidden, names_ref, entering, names, sem):
    copy = pltpu.make_async_copy(names_ref, names, sem)
    copy.start()
    micro, local_rows, width = hidden.shape
    own_rows = micro * local_rows
    part = entering.shape[1] - HD
    count = width // part
    rows = jnp.concatenate([hidden[m].astype(jnp.float32) for m in range(micro)], 0)
    entering[:, :part] = jnp.concatenate(
        [rows[:, i * part : (i + 1) * part] for i in range(count)], 0
    ).astype(jnp.bfloat16)
    row = lax.broadcasted_iota(jnp.int32, (count * own_rows, HD), 0) % own_rows
    name = jnp.zeros((count * own_rows, HD), jnp.float32)
    copy.wait()
    for r in range(own_rows):
        one = names[r // local_rows, 0, r % local_rows].astype(jnp.float32)
        name = jnp.where(row == r, one, name)
    entering[:, part:] = name.astype(jnp.bfloat16)


def row_lengths(lengths, near_lengths, shape, each=GROUP):
    micro, local_rows = lengths.shape
    own_rows = micro * local_rows
    row = lax.broadcasted_iota(jnp.int32, shape, 0) // each
    found = jnp.zeros(shape, jnp.int32)
    for i in range(2 * own_rows):
        source, r = (lengths, near_lengths)[i // own_rows], i % own_rows
        found = jnp.where(row == i, source[r // local_rows, r % local_rows], found)
    return found


def angle_work(small, more):
    lengths, near_lengths, inverse = small
    cosine, sine = more
    angles = row_lengths(lengths, near_lengths, cosine.shape).astype(jnp.float32) * inverse[...]
    front = lax.broadcasted_iota(jnp.int32, cosine.shape, 1) < HD // 2
    cosine[...] = jnp.cos(angles)
    sine[...] = jnp.where(front, -jnp.sin(angles), jnp.sin(angles))


def enter_kernel(count, own_rows, capacity, tick, *refs):
    chunks, rest = refs[:count], refs[count:]
    _, gain, *adapters, normed, held, ident = rest[:8]
    *correction, spread = rest[8:]
    owner = lax.axis_index("wide")
    rows = count * own_rows
    part = gain.shape[1] // count
    spread[...] = by_part(owner, chunks, own_rows)
    ident[...] = spread[:rows, part:]

    @pl.when(lax.axis_index("segment") == tick)
    def _():
        squares = jnp.zeros((rows, 1), jnp.float32)
        for i in range(count):
            block = spread[i * rows : (i + 1) * rows, :part]
            squares += jnp.sum(block * block, 1, keepdims=True)
        scale = lax.rsqrt(squares / gain.shape[1] + epsilon)
        for i in range(count):
            block = spread[i * rows : (i + 1) * rows, :part]
            columns = slice(i * part, (i + 1) * part)
            weight = gain[:, columns].astype(jnp.float32)
            normed[:, columns] = (block * scale * weight).astype(jnp.bfloat16)
        own = pl.ds(pl.multiple_of(owner * rows, rows), rows)
        held[...] = spread[own, :part].astype(jnp.bfloat16)
        adapter_part(owner, ident, normed, adapters, correction, capacity)


def norm_kernel(count, capacity, *refs):
    chunks, rest = [None] * count, refs[count:]
    for i, j in enumerate([2 * p + c for p in HOP_ORDER for c in (1, 0)]):
        chunks[j] = refs[i]
    ident, gain, *adapters, normed = rest[:6]
    correction = rest[6:]
    owner = lax.axis_index("wide")
    rows, part = chunks[0].shape
    squares = jnp.zeros((rows, 1), jnp.float32)
    for chunk in chunks:
        block = chunk[...].astype(jnp.float32)
        squares += jnp.sum(block * block, 1, keepdims=True)
    scale = lax.rsqrt(squares / gain.shape[1] + epsilon)
    for k, chunk in enumerate(chunks):
        columns = pl.ds(pl.multiple_of((owner ^ k) * part, part), part)
        weight = gain[:, columns].astype(jnp.float32)
        normed[:, columns] = (chunk[...].astype(jnp.float32) * scale * weight).astype(jnp.bfloat16)
    adapter_part(owner, ident, normed, adapters, correction, capacity)


def project_kernel(normed, query, out):
    def store(columns, product):
        out[:, columns] = product

    matmul_into(store, normed, query, STEP)


def narrow_kernel(normed, key, value, out):
    narrow = key.shape[1]
    out[:, :narrow] = dot(normed[...], key[...])
    out[:, narrow:] = dot(normed[...], value[...])


def project_first_kernel(first, tick, normed, whole_query, _, out, query, sems):
    copies = []
    for i in range(1, query.shape[1] // first):
        here = pl.ds(i * first, first)
        copies.append(
            pltpu.make_async_copy(whole_query.at[:, here], query.at[:, here], sems.at[i - 1])
        )
    for copy in copies[:2]:
        copy.start()
    live = lax.axis_index("segment") == tick
    for i in range(len(copies) + 1):
        if i:
            copies[i - 1].wait()
            if i + 1 < len(copies):
                copies[i + 1].start()

        @pl.when(live)
        def _():
            here = slice(i * first, (i + 1) * first)
            out[:, here] = dot(normed[...], query[:, here])


def received_rows(received):
    half = received[0].shape[0] // 2
    return [ref[(j % 2) * half : (j % 2 + 1) * half, :] for j, ref in enumerate(received)]


def correct_kernel(count, capacity, base, narrow, ident, *refs):
    received, outs = refs[:count], refs[count:]
    owner = lax.axis_index("wide")
    rows = base.shape[0]
    own_rows = rows // count
    slots = count * capacity
    place = lax.broadcasted_iota(jnp.int32, (rows, rows), 0)
    other = lax.broadcasted_iota(jnp.int32, (rows, rows), 1)
    own = ident[:, :1]
    flat = jnp.where(place == other, own, 0.0).astype(jnp.bfloat16)
    line = dot(jnp.ones((rows, rows), jnp.bfloat16), flat)
    rank = jnp.sum(jnp.where((own == line) & (other < place), 1.0, 0.0), 1, keepdims=True)
    slot = lax.broadcasted_iota(jnp.int32, (rows, slots), 1)
    source = ((slot // capacity) ^ owner).astype(jnp.float32)
    hit = (source == own) & ((slot % capacity).astype(jnp.float32) == rank)
    table = jnp.where(hit, 1.0, 0.0).astype(jnp.bfloat16)
    placed = dot(table, jnp.concatenate(received_rows(received), 0))
    query_cols, key_cols = base.shape[1], narrow.shape[1] // 2
    first = base[...] + placed[:, :query_cols]
    middle = narrow[:, :key_cols]
    last = narrow[:, key_cols:] + placed[:, query_cols:]
    packed = jnp.concatenate([first, middle, last], 1).astype(jnp.bfloat16)
    by_destination(owner, packed, own_rows, outs)


def by_destination(owner, packed, own_rows, outs):
    rows = packed.shape[0]
    place = lax.broadcasted_iota(jnp.int32, (rows, rows), 0)
    other = lax.broadcasted_iota(jnp.int32, (rows, rows), 1)
    hit = (((place // own_rows) ^ owner) == other // own_rows) & (
        place % own_rows == other % own_rows
    )
    order = jnp.where(hit, 1.0, 0.0).astype(jnp.bfloat16)
    sorted_rows = dot(order, packed).astype(jnp.bfloat16)
    for k, out in enumerate(outs):
        out[...] = sorted_rows[k * 2 * own_rows : (k + 1) * 2 * own_rows, :]


def attend_kernel(chips, lengths, near_lengths, *refs):
    arrived, rest = [refs[HEAD_ORDER.index(k)] for k in range(chips)], refs[chips:]
    cosine, sine, keys, values, near_keys, near_values, out, scores, weights = rest
    chip = lax.axis_index("wide") // 2
    own_rows, span = keys.shape[:2]
    chip_rows = 2 * own_rows
    rows = GROUP * chip_rows
    cos, sin = cosine[...], sine[...]
    position = lax.broadcasted_iota(jnp.int32, (2 * rows, span), 1)
    valid = position < row_lengths(lengths, near_lengths, (2 * rows, span), 2 * GROUP)
    score_scale = HD ** (-0.5)

    def turned(vectors):
        return vectors * cos + pltpu.roll(vectors, HD // 2, 1) * sin

    def rounded(vectors):
        return vectors.astype(jnp.bfloat16).astype(jnp.float32)

    pieces = []
    for ref in arrived:
        packed = ref[...].astype(jnp.float32)
        heads = [packed[:, i * HD : (i + 1) * HD] for i in range(GROUP)]
        fresh = [packed[:, GROUP * HD :]] * GROUP
        pieces += [jnp.concatenate(heads, 0), jnp.concatenate(fresh, 0)]
    out_row = lax.broadcasted_iota(jnp.int32, (rows, rows), 0)
    src_row = lax.broadcasted_iota(jnp.int32, (rows, rows), 1)
    same = (out_row // GROUP == src_row % chip_rows) & (out_row % GROUP == src_row // chip_rows)
    order = jnp.where(same, 1.0, 0.0).astype(jnp.bfloat16)
    sorted_rows = dot(order, jnp.concatenate(pieces, 1).astype(jnp.bfloat16))
    band = 2 * GROUP

    def woven(one, two):
        bands = [slice(r * GROUP, (r + 1) * GROUP) for r in range(chip_rows)]
        return jnp.concatenate([part[rows_of] for rows_of in bands for part in (one, two)], 0)

    def pair_lanes(p):
        return pl.ds(pl.multiple_of((chip // 2 ^ p) * 2 * HD, 2 * HD), 2 * HD)

    even = chip % 2 == 0
    zero = jnp.zeros((rows, HD), jnp.float32)
    pairs = range(chips // 2)
    fresh = []
    for p in pairs:
        wide, own, new_values = [], [], []
        for n in range(2):
            piece = sorted_rows[:, (2 * p + n) * 3 * HD : (2 * p + n + 1) * 3 * HD]
            query = rounded(turned(piece[:, :HD]))
            new_key = rounded(turned(piece[:, HD : 2 * HD]))
            own.append(jnp.sum(query * new_key, 1, keepdims=True) * score_scale)
            new_values.append(piece[:, 2 * HD :])
            left = even if n == 0 else jnp.logical_not(even)
            wide.append(
                jnp.concatenate([jnp.where(left, query, zero), jnp.where(left, zero, query)], 1)
            )
        fresh.append((woven(*own), woven(*new_values)))
        wide = woven(*wide).astype(jnp.bfloat16)
        for r in range(chip_rows):
            first = (p * chip_rows + r) * band
            scores[first : first + band, :] = lax.dot_general(
                wide[r * band : (r + 1) * band, :],
                (keys, near_keys)[r // own_rows][r % own_rows, :, pair_lanes(p)],
                (((1,), (1,)), ((), ())),
                preferred_element_type=jnp.float32,
            )
    parts = []
    for p, (own, new_value) in enumerate(fresh):
        here = slice(p * 2 * rows, (p + 1) * 2 * rows)
        found = jnp.where(valid, scores[here, :] * score_scale, -1e30)
        top = jnp.maximum(jnp.max(found, 1, keepdims=True), own)
        past = jnp.where(valid, jnp.exp(found - top), 0.0)
        own = jnp.exp(own - top)
        total = jnp.sum(past, 1, keepdims=True) + own
        weights[here, :] = (past / total).astype(jnp.bfloat16)
        parts.append(rounded(own / total) * new_value)
    for p, own_part in enumerate(parts):
        mixed = []
        for r in range(chip_rows):
            first = (p * chip_rows + r) * band
            found = dot(
                weights[first : first + band, :],
                (values, near_values)[r // own_rows][r % own_rows, :, pair_lanes(p)],
            )
            mine = own_part[r * band : (r + 1) * band, :]
            one = jnp.where(even, found[:GROUP, :HD], found[:GROUP, HD:]) + mine[:GROUP]
            two = jnp.where(even, found[GROUP:, HD:], found[GROUP:, :HD]) + mine[GROUP:]
            both = [jnp.where(even, one, two), jnp.where(even, two, one)]
            mixed.append(jnp.concatenate(both, 1))
        out[:, pair_lanes(p)] = jnp.concatenate(mixed, 0).astype(jnp.bfloat16)


def attended_rows(owner, chunks, own_rows, rows_ref):
    count = len(chunks)
    chips = count // 2
    rows = own_rows * count
    total = rows * GROUP
    out = lax.broadcasted_iota(jnp.int32, (total, total), 0)
    src = lax.broadcasted_iota(jnp.int32, (total, total), 1)
    device_out = (out // own_rows) % count
    chip_rows = 2 * own_rows
    row_src = (src // GROUP) % chip_rows
    near = (out // rows == src % GROUP) & (out % own_rows == row_src % own_rows)
    for core in range(2):
        stack = jnp.concatenate([chunks[2 * k + core][...] for k in range(chips)], 0)
        device_src = owner ^ (2 * (src // (GROUP * chip_rows)) + core) ^ (row_src // own_rows)
        hit = near & (device_out == device_src)
        spread = dot(jnp.where(hit, 1.0, 0.0).astype(jnp.bfloat16), stack).astype(jnp.bfloat16)
        first = (owner ^ core) % 2
        for i in range(chips):
            for j in range(GROUP):
                head = (2 * i + first) * GROUP + j
                rows_ref[:, pl.ds(pl.multiple_of(head * HD, HD), HD)] = spread[
                    j * rows : (j + 1) * rows, i * HD : (i + 1) * HD
                ]


def leave_kernel(count, own_rows, tick, *refs):
    chunks, rest = [None] * count, refs[count:]
    for i, j in enumerate([2 * p + c for p in ROW_ORDER for c in (0, 1)]):
        chunks[j] = refs[i]
    held, result = rest[0], rest[1] if tick else None
    matrix, out, kept, *outs, rows_ref = rest[2 if tick else 1 :]
    kept[...] = result[...] if tick else jnp.zeros_like(kept)

    @pl.when(lax.axis_index("segment") == tick)
    def _():
        attended_rows(lax.axis_index("wide"), chunks, own_rows, rows_ref)

        def store(columns, product):
            total = held[:, columns].astype(jnp.float32) + product
            out[:, columns] = total.astype(jnp.bfloat16)
            kept[:, columns] = total.astype(jnp.bfloat16)

        matmul_into(store, rows_ref, matrix, 2 * STEP)

    if outs:
        by_destination(lax.axis_index("wide"), kept[...], own_rows, outs)


def join_kernel(count, *refs):
    blocks, out = [None] * count, refs[count]
    for i, j in enumerate([2 * p + c for p in LAST_ORDER for c in (1, 0)]):
        blocks[j] = refs[i]
    for j, block in enumerate(blocks):
        rows = block.shape[0] // 2
        half = block[(j % 2) * rows : (j % 2 + 1) * rows, :]
        width = half.shape[1]
        columns = pl.ds(pl.multiple_of((lax.axis_index("wide") ^ j) * width, width), width)
        for m in range(out.shape[1]):
            local_rows = out.shape[2]
            out[0, m, :, columns] = half[m * local_rows : (m + 1) * local_rows, :]


def on_device_by_head(
    entering_hidden,
    row_adapter_index,
    lengths,
    input_norm_gain,
    query_matrix,
    key_matrix,
    value_matrix,
    output_matrix,
    adapter_down_maps,
    adapter_up_query,
    adapter_up_value,
    rotated_key_cache,
    cached_values,
):
    segments = lax.axis_size("segment")
    count = lax.axis_size("wide")
    micro, local_rows, width = entering_hidden.shape
    own_rows = micro * local_rows
    rows = own_rows * count
    capacity = CAP * micro
    part = width // count
    query_cols, key_cols = query_matrix.shape[2], key_matrix.shape[2]
    packed_cols = query_cols + 2 * key_cols
    span = rotated_key_cache.shape[3]

    chips = count // 2
    head_lanes = chips * HD
    query_weight = query_matrix[0]
    output_weight = output_matrix[0]
    adapters = [adapter_down_maps[0], adapter_up_query[0], adapter_up_value[0]]
    caches = [cache[0].reshape(own_rows, span, -1) for cache in (rotated_key_cache, cached_values)]
    near_lengths = swapped(lengths, 1)
    gain = input_norm_gain
    half = HD // 2
    inverse = np.tile(rope_base ** (-np.arange(half) / half), 2).astype(np.float32)[None]

    def blocks_of(slots, columns):
        return [jax.ShapeDtypeStruct((2 * slots, columns), jnp.bfloat16)] * chips

    normed_shape = jax.ShapeDtypeStruct((rows, width), jnp.bfloat16)
    held_shape = jax.ShapeDtypeStruct((rows, part), jnp.bfloat16)
    ident_shape = jax.ShapeDtypeStruct((rows, HD), jnp.float32)
    base_shape = jax.ShapeDtypeStruct((rows, query_cols), jnp.float32)
    narrow_shape = jax.ShapeDtypeStruct((rows, 2 * key_cols), jnp.float32)
    angle_shape = jax.ShapeDtypeStruct((GROUP * 2 * own_rows, HD), jnp.float32)
    correction_shapes = blocks_of(capacity, query_cols + key_cols)
    query_first = query_cols // 4
    output_first = part // 2

    names = pltpu.with_memory_space_constraint(row_adapter_index.transpose(0, 2, 1), pltpu.HBM)
    (entering,) = call(
        open_kernel,
        [jax.ShapeDtypeStruct((rows, part + HD), jnp.bfloat16)],
        [(entering_hidden, VMEM), (names, pl.BlockSpec(memory_space=pl.ANY))],
        [pltpu.SMEM(names.shape, names.dtype), pltpu.SemaphoreType.DMA],
        name="open",
    )
    projections, output_parts, halves, angles = [], [], [None, None], []
    held = ident = None
    result = None
    blocks = []
    for tick in range(segments):
        if tick == 0:

            def load_first():
                sources = [*adapters, key_matrix[0], value_matrix[0], query_weight, *caches]
                small = [(entering, VMEM)]
                shape = (own_rows, span, head_lanes)
                shapes = [source.shape for source in sources[:6]]
                shapes += [shape] * 2

                def plan(sources, outs):
                    pairs = list(zip(sources[:5], outs[:5]))
                    pairs.append((sources[5].at[:, :query_first], outs[5].at[:, :query_first]))
                    return pairs + half_of(1, sources[6:], outs[6:])

                found, (token,) = loaded(
                    sources, shapes, plan, 6 + 2 * chips, small, [TOKEN], token_of
                )
                adapters[:], projections[:] = found[:3], found[3:6]
                halves[2:] = found[6:]
                return token

            chunks, _ = gathered(entering, load_first)
            normed, held, ident, *found = call(
                functools.partial(enter_kernel, count, own_rows, capacity, tick),
                [normed_shape, held_shape, ident_shape] + correction_shapes,
                [(c, VMEM) for c in chunks]
                + [(near_lengths, pl.BlockSpec(memory_space=pl.ANY)), (gain, VMEM)],
                [pltpu.VMEM((count * rows, part + HD), jnp.float32)],
                kept=adapters,
                through=halves[2:],
                name="enter",
            )
            halves[2:] = [swapped(array, 1) for array in found[chips:]]
        else:
            chunks = passed_on(held, tick - 1)
            held = chunks[0]
            normed, *found = call(
                while_live(tick, functools.partial(norm_kernel, count, capacity)),
                [normed_shape] + correction_shapes,
                [(chunks[2 * p + c], VMEM) for p in HOP_ORDER for c in (1, 0)]
                + [(ident, VMEM), (gain, VMEM)],
                kept=adapters,
                name="norm",
            )
        correction = found[:chips]

        def project():
            return call(
                while_live(tick, project_kernel),
                [base_shape],
                [(normed, VMEM)],
                kept=projections[2:],
                cost=16,
                name="project",
            )[0]

        def project_first():
            base, projections[2] = pl.pallas_call(
                functools.partial(project_first_kernel, query_first, tick),
                out_shape=[base_shape, pltpu.VMEM(query_weight.shape, jnp.bfloat16)],
                in_specs=[VMEM, pl.BlockSpec(memory_space=pl.ANY), VMEM],
                out_specs=[VMEM, VMEM],
                input_output_aliases={2: 1},
                scratch_shapes=[pltpu.SemaphoreType.DMA((query_cols // query_first - 1,))],
                compiler_params=pltpu.CompilerParams(vmem_limit_bytes=8 * MIB),
                cost_estimate=pl.CostEstimate(
                    flops=0, transcendentals=0, bytes_accessed=16 * MIB
                ),
                name="project",
            )(
                normed,
                pltpu.with_memory_space_constraint(query_weight, pltpu.HBM),
                resident(projections[2]),
            )
            return base

        received, base = exchanged(correction, project if tick else project_first)
        received = [part for one in received for part in (one, swapped(one, 1))]
        (narrow,) = call(
            while_live(tick, narrow_kernel),
            [narrow_shape],
            [(normed, VMEM)],
            kept=projections[:2],
            cost=4,
            name="narrow",
        )
        packed = call(
            while_live(
                tick, functools.partial(correct_kernel, count, capacity)
            ),
            blocks_of(own_rows, packed_cols),
            [(base, VMEM), (narrow, VMEM), (ident, VMEM)] + [(r, VMEM) for r in received],
            name="correct",
        )

        def load_part():
            small = [(lengths, SMEM), (near_lengths, SMEM), (jnp.asarray(inverse), VMEM)]
            found, angles[:] = loaded(
                [output_weight, *caches],
                [output_weight.shape] + [(own_rows, span, head_lanes)] * 2,
                lambda sources, outs: [
                    (sources[0].at[:, :output_first], outs[0].at[:, :output_first])
                ]
                + half_of(0, sources[1:], outs[1:]),
                1 + 2 * chips,
                small,
                [angle_shape, angle_shape],
                angle_work,
            )
            output_parts[:], halves[:2] = found[:1], found[1:]
            return angles[0]

        def load_output():
            output_parts[0], token = pl.pallas_call(
                functools.partial(load_rest_kernel, output_first),
                out_shape=[pltpu.VMEM(output_weight.shape, jnp.bfloat16), TOKEN],
                in_specs=[pl.BlockSpec(memory_space=pl.ANY), VMEM, VMEM],
                out_specs=[VMEM, VMEM],
                input_output_aliases={2: 0},
                scratch_shapes=[pltpu.SemaphoreType.DMA],
                compiler_params=pltpu.CompilerParams(vmem_limit_bytes=4 * MIB),
                cost_estimate=pl.CostEstimate(
                    flops=0, transcendentals=0, bytes_accessed=8 * MIB
                ),
                name="load",
            )(
                pltpu.with_memory_space_constraint(output_weight, pltpu.HBM),
                attended,
                resident(output_parts[0]),
            )
            return token

        arrived, _ = exchanged(packed, None if tick else load_part)
        attended, *_ = call(
            while_live(tick, functools.partial(attend_kernel, chips)),
            [jax.ShapeDtypeStruct((GROUP * 2 * own_rows, head_lanes), jnp.bfloat16)],
            [(lengths, SMEM), (near_lengths, SMEM)]
            + [(a, VMEM) for a in [*[arrived[k] for k in HEAD_ORDER], *angles]],
            [
                pltpu.VMEM((chips * GROUP * 2 * own_rows, span), jnp.float32),
                pltpu.VMEM((chips * GROUP * 2 * own_rows, span), jnp.bfloat16),
            ],
            kept=halves,
            name="attend",
        )
        chunks, _ = gathered(attended, None if tick else load_output)
        last = tick == segments - 1
        held, result, *found = call(
            functools.partial(leave_kernel, count, own_rows, tick),
            [held_shape, held_shape] + (blocks_of(own_rows, part) if last else []),
            [(chunks[2 * p + c], VMEM) for p in ROW_ORDER for c in (0, 1)]
            + [(held, VMEM)] + ([(result, VMEM)] if tick else []),
            [pltpu.VMEM((rows, width), jnp.bfloat16)],
            kept=output_parts,
            name="leave",
        )
        blocks = found
    far, _ = exchanged(blocks)
    far = [part for one in far for part in (one, swapped(one, 1))]
    (joined,) = call(
        functools.partial(join_kernel, count),
        [jax.ShapeDtypeStruct((1, micro, local_rows, width), jnp.bfloat16)],
        [(far[2 * p + c], VMEM) for p in LAST_ORDER for c in (1, 0)],
        name="join",
    )
    return joined


def passed_along(value, axis, steps):
    count = lax.axis_size(axis)
    leading, last = (max(0, -steps), min(count, count - steps))
    return lax.ppermute(value, axis, [(source, source + steps) for source in range(leading, last)])


def rotary(vectors, positions):
    half = vectors.shape[-1] // 2
    inverse = rope_base ** (-jnp.arange(half, dtype=jnp.float32) / half)
    angles = positions.astype(jnp.float32)[:, None] * inverse[None, :]
    cosine = jnp.cos(angles)[:, None, :]
    sine = jnp.sin(angles)[:, None, :]
    front = vectors[..., :half]
    back = vectors[..., half:]
    return jnp.concatenate([front * cosine - back * sine, back * cosine + front * sine], -1)


def attend(query_vector, new_key, fresh_value, positions, key_block, value_block):
    rows = query_vector.shape[0]
    group = HEADS // KVH
    rotated_rows = rotary(
        query_vector.astype(jnp.float32).reshape(rows, HEADS, HD), positions
    ).astype(jnp.bfloat16)
    rotated_rows = rotated_rows.reshape(rows, KVH, group, HD)
    self_key = rotary(new_key.astype(jnp.float32).reshape(rows, KVH, HD), positions).astype(
        jnp.bfloat16
    )
    keys_past = key_block.reshape(rows, -1, KVH, HD)
    values_past = value_block.reshape(rows, -1, KVH, HD)
    score_scale = HD ** (-0.5)
    past = (
        jnp.einsum("bkgd,bpkd->bkgp", rotated_rows, keys_past, preferred_element_type=jnp.float32)
        * score_scale
    )
    self_scores = (
        jnp.einsum("rice,rie->ric", rotated_rows, self_key, preferred_element_type=jnp.float32)
        * score_scale
    )
    valid = jnp.arange(keys_past.shape[1])[None, :] < positions[:, None]
    past = jnp.where(valid[:, None, None, :], past, -1e30)
    top = jnp.maximum(jnp.max(past, -1), self_scores)
    past_exp = jnp.where(valid[:, None, None, :], jnp.exp(past - top[..., None]), 0.0)
    own_exp = jnp.exp(self_scores - top)
    total = jnp.sum(past_exp, -1) + own_exp
    past_weights = (past_exp / total[..., None]).astype(jnp.bfloat16)
    own_weights = (own_exp / total).astype(jnp.bfloat16)
    mixed = jnp.einsum(
        "bkgp,bpkd->bkgd", past_weights, values_past, preferred_element_type=jnp.float32
    )
    mixed = (
        mixed
        + own_weights.astype(jnp.float32)[..., None]
        * fresh_value.reshape(rows, KVH, HD).astype(jnp.float32)[:, :, None, :]
    )
    return mixed.reshape(rows, HEADS * HD).astype(jnp.bfloat16)


def on_device(
    entering_hidden,
    row_adapter_index,
    lengths,
    input_norm_gain,
    query_matrix,
    key_matrix,
    value_matrix,
    output_matrix,
    adapter_down_maps,
    adapter_up_query,
    adapter_up_value,
    rotated_key_cache,
    cached_values,
):
    segments = lax.axis_size("segment")
    segment = lax.axis_index("segment")
    devices = lax.axis_size("wide")
    owner = lax.axis_index("wide")
    small_batch, local_rows, width = entering_hidden.shape
    listed = lax.all_gather(row_adapter_index, "wide", axis=1, tiled=True)[:, :, 0]
    groups = small_batch // small_batch
    capacity = CAP * small_batch
    kept_entries = adapter_down_maps.shape[1]
    adapters = kept_entries * devices
    mine = owner * kept_entries + jnp.arange(kept_entries)
    gain = input_norm_gain[0].astype(jnp.float32)
    query_cols = query_matrix.shape[2]
    key_cols = key_matrix.shape[2]
    passed = jnp.zeros((small_batch * local_rows, width), jnp.bfloat16)
    results = jnp.zeros((small_batch, local_rows, width), jnp.bfloat16)
    ticks = groups + segments - 1
    for tick in range(ticks):
        if tick < groups:
            fresh = entering_hidden.reshape(small_batch * local_rows, width)
        else:
            fresh = jnp.zeros_like(passed)
        rows = jnp.where(segment == 0, fresh, passed)
        index = tick - segment
        live = (index >= 0) & (index < groups)
        index = jnp.clip(index, 0, groups - 1)
        block_rows = rows.shape[0]
        idents = listed
        idents = idents.reshape(small_batch, devices, local_rows).transpose(1, 0, 2).reshape(-1)
        positions = lengths.reshape(-1)
        key_block = rotated_key_cache[0]
        key_block = key_block.reshape(block_rows, key_block.shape[2], key_block.shape[3])
        value_block = cached_values[0]
        value_block = value_block.reshape(block_rows, value_block.shape[2], value_block.shape[3])
        values = rows.astype(jnp.float32)
        normalized_rows = (
            values * lax.rsqrt(jnp.mean(values * values, 1, keepdims=True) + epsilon) * gain
        ).astype(jnp.bfloat16)
        gathered = lax.all_gather(normalized_rows, "wide", axis=0, tiled=True)
        total_rows = gathered.shape[0]
        matches = (idents[None, :] == mine[:, None]).astype(jnp.int32)
        ranks = jnp.cumsum(matches, 1) - 1
        chosen = (matches[:, None, :] == 1) & (
            ranks[:, None, :] == jnp.arange(capacity)[None, :, None]
        )
        chosen = chosen.reshape(kept_entries * capacity, total_rows)
        selected_rows = jnp.dot(
            chosen.astype(jnp.bfloat16), gathered, preferred_element_type=jnp.float32
        ).astype(jnp.bfloat16)
        selected_rows = selected_rows.reshape(kept_entries, capacity, width)
        reduced = jnp.einsum(
            "bpy,byf->bpf", selected_rows, adapter_down_maps[0], preferred_element_type=jnp.float32
        ).astype(jnp.bfloat16)
        member = (idents[:, None] == jnp.arange(adapters)[None, :]).astype(jnp.int32)
        order = jnp.sum(jnp.cumsum(member, 0) * member, 1) - 1
        slot = idents * capacity + order
        slot_table = slot[:, None] == jnp.arange(adapters * capacity)[None, :]
        query_slots = jnp.einsum(
            "acr,are->ace",
            reduced[..., :ADAPTER_RANK],
            adapter_up_query[0],
            preferred_element_type=jnp.float32,
        )
        value_slots = jnp.einsum(
            "acr,are->ace",
            reduced[..., ADAPTER_RANK:],
            adapter_up_value[0],
            preferred_element_type=jnp.float32,
        )
        joined = jnp.concatenate(
            [
                query_slots.reshape(kept_entries * capacity, devices, -1),
                value_slots.reshape(kept_entries * capacity, devices, -1),
            ],
            2,
        )
        received = lax.all_to_all(joined, "wide", split_axis=1, concat_axis=0, tiled=True)
        received = received.reshape(adapters * capacity, -1)
        placed = jnp.dot(slot_table.astype(jnp.float32), received, precision=lax.Precision.HIGHEST)
        query_adjustment = placed[:, :query_cols]
        value_adjustment = placed[:, query_cols:]
        query_vector = (
            jnp.dot(gathered, query_matrix[0], preferred_element_type=jnp.float32)
            + adapter_scale * query_adjustment
        ).astype(jnp.bfloat16)
        new_key = jnp.dot(gathered, key_matrix[0], preferred_element_type=jnp.float32).astype(
            jnp.bfloat16
        )
        fresh_value = (
            jnp.dot(gathered, value_matrix[0], preferred_element_type=jnp.float32)
            + adapter_scale * value_adjustment
        ).astype(jnp.bfloat16)
        packed = jnp.concatenate([query_vector, new_key, fresh_value], 1)
        arrived = lax.all_to_all(packed, "wide", split_axis=0, concat_axis=1, tiled=True).reshape(
            block_rows, devices, -1
        )
        query_rows_local = arrived[:, :, :query_cols].reshape(block_rows, -1)
        key_rows_local = arrived[:, :, query_cols : query_cols + key_cols].reshape(block_rows, -1)
        value_rows_local = arrived[:, :, query_cols + key_cols :].reshape(block_rows, -1)
        attended = attend(
            query_rows_local, key_rows_local, value_rows_local, positions, key_block, value_block
        )
        columns = jnp.dot(
            lax.all_gather(attended, "wide", axis=0, tiled=True),
            output_matrix[0],
            preferred_element_type=jnp.float32,
        )
        returned = lax.all_to_all(columns, "wide", split_axis=0, concat_axis=1, tiled=True)
        outcome = (values + returned).astype(jnp.bfloat16)
        updated = outcome.reshape(small_batch, local_rows, width)
        results = jnp.where(live, updated, results)
        if tick + 1 < ticks:
            passed = passed_along(outcome, "segment", 1)
    return results[None]


def solution(mesh):
    placed = (
        P(None, "wide", None),
        P(None, "wide", None),
        P(None, "wide"),
        P("segment", None),
        P("segment", None, "wide"),
        P("segment", None, "wide"),
        P("segment", None, "wide"),
        P("segment", None, "wide"),
        P("segment", "wide", None, None),
        P("segment", "wide", None, None),
        P("segment", "wide", None, None),
        P("segment", None, "wide", None, None),
        P("segment", None, "wide", None, None),
    )
    by_head = mesh.shape["wide"] == KVH
    return jax.shard_map(
        on_device_by_head if by_head else on_device,
        mesh=mesh,
        in_specs=placed,
        out_specs=P("segment", None, "wide", None),
        check_vma=False,
    )
```

```python
import functools

import jax
import jax.numpy as jnp
import numpy as np
from jax import lax
from jax.experimental import pallas as pl
from jax.experimental.pallas import tpu as pltpu
from jax.sharding import PartitionSpec as P

HEADS = 64
KVH = 8
HD = 128
ADAPTER_RANK = 64
CAP = 4


adapter_scale = 0.5
rope_base = 500000.0
epsilon = 1e-05

GROUP = HEADS // KVH
MIB = 1 << 20
STEP = 256
HOP_ORDER = (2, 3, 1, 0)
WORK_ORDER = (1, 0, 2)
HEAD_ORDER = (2, 3, 1, 0)
ROW_ORDER = (0, 2, 1, 3)
LAST_ORDER = (3, 2, 1, 0)
VMEM = pl.BlockSpec(memory_space=pltpu.VMEM)
SMEM = pl.BlockSpec(memory_space=pltpu.SMEM)


def swapped(value, bits):
    count = lax.axis_size("wide")
    return lax.ppermute(value, "wide", [(i, i ^ bits) for i in range(count)])


def then(arrays, work):
    if work is None:
        return arrays, None
    done = work()
    arrays = [arrays[k] for k in WORK_ORDER]
    arrays = pl.pallas_call(
        lambda *refs: None,
        out_shape=[jax.ShapeDtypeStruct(array.shape, array.dtype) for array in arrays],
        in_specs=[VMEM] * len(arrays) + [pl.BlockSpec(memory_space=pl.ANY)],
        out_specs=[VMEM] * len(arrays),
        input_output_aliases={i: i for i in range(len(arrays))},
        compiler_params=pltpu.CompilerParams(vmem_limit_bytes=MIB),
        name="then",
    )(*arrays, done)
    return [arrays[WORK_ORDER.index(k)] for k in range(len(WORK_ORDER))], done


def gathered(value, work=None):
    count = lax.axis_size("wide")
    far = [swapped(value, k) for k in range(2, count, 2)]
    far, done = then(far, work)
    found = [part for one in [value, *far] for part in (one, swapped(one, 1))]
    return found, done


def passed_on(value, s):
    count = lax.axis_size("wide")

    def shifted(bits):
        pairs = [(s * count + i, (s + 1) * count + (i ^ bits)) for i in range(count)]
        return lax.ppermute(value, ("segment", "wide"), pairs)

    far = [shifted(bits) for bits in range(0, count, 2)]
    return [part for one in far for part in (one, swapped(one, 1))]


def exchanged(blocks, work=None):
    far = [swapped(block, 2 * k) for k, block in enumerate(blocks) if k]
    far, done = then(far, work)
    return [blocks[0], *far], done


def resident(weight):
    return pltpu.with_memory_space_constraint(weight, pltpu.VMEM)


def call(body, out_shape, operands, scratch=(), limit=8, kept=(), through=(), cost=1, name=None):
    outs, count = list(out_shape), len(operands) + len(kept)
    inner = body
    if through:

        def inner(*refs):
            inputs = count + len(through)
            shown = inputs + len(outs)
            body(*refs[:count], *refs[inputs:shown], *refs[shown + len(through) :])

    found = pl.pallas_call(
        inner,
        out_shape=outs + [pltpu.VMEM(array.shape, array.dtype) for array in through],
        in_specs=[spec for _, spec in operands] + [VMEM] * (len(kept) + len(through)),
        out_specs=[VMEM] * (len(outs) + len(through)),
        input_output_aliases={count + i: len(outs) + i for i in range(len(through))},
        scratch_shapes=list(scratch),
        compiler_params=pltpu.CompilerParams(vmem_limit_bytes=limit * MIB),
        cost_estimate=pl.CostEstimate(flops=0, transcendentals=0, bytes_accessed=cost * MIB),
        name=name,
    )(*[array for array, _ in operands], *[resident(array) for array in [*kept, *through]])
    return list(found)


def load_kernel(sizes, plan, work, *refs):
    sources, small, outs, more = [], [], [], []
    refs = list(refs)
    for group, size in zip((sources, small, outs, more), sizes, strict=True):
        group.extend(refs[:size])
        del refs[:size]
    copies = [
        pltpu.make_async_copy(source, out, refs[0].at[i])
        for i, (source, out) in enumerate(plan(sources, outs))
    ]
    for copy in copies:
        copy.start()
    work(small, more)
    for copy in copies:
        copy.wait()


def loaded(sources, shapes, plan, copies, small, more, work):
    moved = sum(2 * int(np.prod(shape)) for shape in shapes)
    found = pl.pallas_call(
        functools.partial(
            load_kernel, (len(sources), len(small), len(shapes), len(more)), plan, work
        ),
        out_shape=[pltpu.VMEM(shape, jnp.bfloat16) for shape in shapes] + list(more),
        in_specs=[pl.BlockSpec(memory_space=pl.ANY)] * len(sources) + [spec for _, spec in small],
        out_specs=[VMEM] * (len(shapes) + len(more)),
        scratch_shapes=[pltpu.SemaphoreType.DMA((copies,))],
        compiler_params=pltpu.CompilerParams(vmem_limit_bytes=4 * MIB),
        cost_estimate=pl.CostEstimate(flops=0, transcendentals=0, bytes_accessed=moved),
        name="load",
    )(
        *[pltpu.with_memory_space_constraint(source, pltpu.HBM) for source in sources],
        *[array for array, _ in small],
    )
    return found[: len(shapes)], found[len(shapes) :]


def half_of(other, sources, outs):
    core = (lax.axis_index("wide") + other) % 2
    pairs = []
    for source, out in zip(sources, outs, strict=True):
        for i in range(out.shape[2] // HD):
            there = pl.ds(pl.multiple_of((2 * i + core) * HD, HD), HD)
            pairs.append((source.at[:, :, there], out.at[:, :, pl.ds(i * HD, HD)]))
    return pairs


TOKEN = jax.ShapeDtypeStruct((8, HD), jnp.float32)


def token_of(small, more):
    more[0][...] = small[0][:8, :HD].astype(jnp.float32)


def load_rest_kernel(first, source, after, _, out, token, sem):
    copy = pltpu.make_async_copy(source.at[:, first:], out.at[:, first:], sem)
    copy.start()
    token[...] = after[:8, :HD].astype(jnp.float32)
    copy.wait()


def dot(left, right):
    return jnp.dot(left, right, preferred_element_type=jnp.float32)


def matmul_into(store, source, weight, step):
    def one(i, carry):
        columns = pl.ds(pl.multiple_of(i * step, step), step)
        store(columns, dot(source[...], weight[:, columns]))
        return carry

    lax.fori_loop(0, weight.shape[1] // step, one, 0)


def while_live(tick, body):
    def run(*refs):
        pl.when(lax.axis_index("segment") == tick)(lambda: body(*refs))

    return run


def by_part(owner, chunks, own_rows):
    count = len(chunks)
    parts = chunks[0].shape[0] // own_rows
    total = count * parts * own_rows
    stack = jnp.concatenate([chunk[...] for chunk in chunks], 0)
    out = lax.broadcasted_iota(jnp.int32, (total, total), 0)
    src = lax.broadcasted_iota(jnp.int32, (total, total), 1)
    rows = own_rows
    part_out = out // (rows * count)
    device_out = (out // rows) % count
    part_src = (src // rows) % parts
    device_src = (src // (rows * parts)) ^ owner
    hit = (part_out == part_src) & (device_out == device_src) & (out % rows == src % rows)
    return dot(jnp.where(hit, 1.0, 0.0).astype(jnp.bfloat16), stack)


def adapter_part(owner, ident, normed, adapter, outs, capacity):
    down, up_query, up_value = adapter
    rows = normed.shape[0]
    count = 2 * len(outs)
    low = dot(normed[...], down[0]).astype(jnp.bfloat16)
    place = lax.broadcasted_iota(jnp.int32, (rows, rows), 0)
    other = lax.broadcasted_iota(jnp.int32, (rows, rows), 1)
    mine = jnp.where(ident[:, :1] == owner.astype(jnp.float32), 1.0, 0.0)
    flat = jnp.where(place == other, mine, 0.0).astype(jnp.bfloat16)
    before = jnp.where(place < other, mine, 0.0).astype(jnp.bfloat16)
    ones = jnp.ones((capacity, rows), jnp.bfloat16)
    member = dot(ones, flat)
    rank = dot(ones, before)
    slot = lax.broadcasted_iota(jnp.int32, (capacity, rows), 0).astype(jnp.float32)
    chosen = jnp.where((member > 0.5) & (rank == slot), 1.0, 0.0).astype(jnp.bfloat16)
    picked = dot(chosen, low).astype(jnp.bfloat16)
    query_cols = up_query.shape[2] // count
    value_cols = up_value.shape[2] // count
    for j in range(count):
        out, there = outs[j // 2], owner ^ j
        slots = slice((j % 2) * capacity, (j % 2 + 1) * capacity)
        columns = pl.ds(pl.multiple_of(there * query_cols, query_cols), query_cols)
        for_query = dot(picked[:, :ADAPTER_RANK], up_query[0, :, columns]) * adapter_scale
        out[slots, :query_cols] = for_query.astype(jnp.bfloat16)
        columns = pl.ds(pl.multiple_of(there * value_cols, value_cols), value_cols)
        for_value = dot(picked[:, ADAPTER_RANK:], up_value[0, :, columns]) * adapter_scale
        out[slots, query_cols:] = for_value.astype(jnp.bfloat16)


def open_kernel(hidden, names_ref, entering, names, sem):
    copy = pltpu.make_async_copy(names_ref, names, sem)
    copy.start()
    micro, local_rows, width = hidden.shape
    own_rows = micro * local_rows
    part = entering.shape[1] - HD
    count = width // part
    rows = jnp.concatenate([hidden[m].astype(jnp.float32) for m in range(micro)], 0)
    entering[:, :part] = jnp.concatenate(
        [rows[:, i * part : (i + 1) * part] for i in range(count)], 0
    ).astype(jnp.bfloat16)
    row = lax.broadcasted_iota(jnp.int32, (count * own_rows, HD), 0) % own_rows
    name = jnp.zeros((count * own_rows, HD), jnp.float32)
    copy.wait()
    for r in range(own_rows):
        one = names[r // local_rows, 0, r % local_rows].astype(jnp.float32)
        name = jnp.where(row == r, one, name)
    entering[:, part:] = name.astype(jnp.bfloat16)


def row_lengths(lengths, near_lengths, shape, each=GROUP):
    micro, local_rows = lengths.shape
    own_rows = micro * local_rows
    row = lax.broadcasted_iota(jnp.int32, shape, 0) // each
    found = jnp.zeros(shape, jnp.int32)
    for i in range(2 * own_rows):
        source, r = (lengths, near_lengths)[i // own_rows], i % own_rows
        found = jnp.where(row == i, source[r // local_rows, r % local_rows], found)
    return found


def angle_work(small, more):
    lengths, near_lengths, inverse = small
    cosine, sine = more
    angles = row_lengths(lengths, near_lengths, cosine.shape).astype(jnp.float32) * inverse[...]
    front = lax.broadcasted_iota(jnp.int32, cosine.shape, 1) < HD // 2
    cosine[...] = jnp.cos(angles)
    sine[...] = jnp.where(front, -jnp.sin(angles), jnp.sin(angles))


def enter_kernel(count, own_rows, capacity, tick, *refs):
    chunks, rest = refs[:count], refs[count:]
    _, gain, *adapters, normed, held, ident = rest[:8]
    *correction, spread = rest[8:]
    owner = lax.axis_index("wide")
    rows = count * own_rows
    part = gain.shape[1] // count
    spread[...] = by_part(owner, chunks, own_rows)
    ident[...] = spread[:rows, part:]

    @pl.when(lax.axis_index("segment") == tick)
    def _():
        squares = jnp.zeros((rows, 1), jnp.float32)
        for i in range(count):
            block = spread[i * rows : (i + 1) * rows, :part]
            squares += jnp.sum(block * block, 1, keepdims=True)
        scale = lax.rsqrt(squares / gain.shape[1] + epsilon)
        for i in range(count):
            block = spread[i * rows : (i + 1) * rows, :part]
            columns = slice(i * part, (i + 1) * part)
            weight = gain[:, columns].astype(jnp.float32)
            normed[:, columns] = (block * scale * weight).astype(jnp.bfloat16)
        own = pl.ds(pl.multiple_of(owner * rows, rows), rows)
        held[...] = spread[own, :part].astype(jnp.bfloat16)
        adapter_part(owner, ident, normed, adapters, correction, capacity)


def norm_kernel(count, capacity, *refs):
    chunks, rest = [None] * count, refs[count:]
    for i, j in enumerate([2 * p + c for p in HOP_ORDER for c in (1, 0)]):
        chunks[j] = refs[i]
    ident, gain, *adapters, normed = rest[:6]
    correction = rest[6:]
    owner = lax.axis_index("wide")
    rows, part = chunks[0].shape
    squares = jnp.zeros((rows, 1), jnp.float32)
    for chunk in chunks:
        block = chunk[...].astype(jnp.float32)
        squares += jnp.sum(block * block, 1, keepdims=True)
    scale = lax.rsqrt(squares / gain.shape[1] + epsilon)
    for k, chunk in enumerate(chunks):
        columns = pl.ds(pl.multiple_of((owner ^ k) * part, part), part)
        weight = gain[:, columns].astype(jnp.float32)
        normed[:, columns] = (chunk[...].astype(jnp.float32) * scale * weight).astype(jnp.bfloat16)
    adapter_part(owner, ident, normed, adapters, correction, capacity)


def project_kernel(normed, query, out):
    def store(columns, product):
        out[:, columns] = product

    matmul_into(store, normed, query, 2 * STEP)


def narrow_kernel(normed, key, value, out):
    narrow = key.shape[1]
    out[:, :narrow] = dot(normed[...], key[...])
    out[:, narrow:] = dot(normed[...], value[...])


def project_first_kernel(first, tick, normed, whole_query, _, out, query, sems):
    copies = []
    for i in range(1, query.shape[1] // first):
        here = pl.ds(i * first, first)
        copies.append(
            pltpu.make_async_copy(whole_query.at[:, here], query.at[:, here], sems.at[i - 1])
        )
    for copy in copies[:2]:
        copy.start()
    live = lax.axis_index("segment") == tick
    for i in range(len(copies) + 1):
        if i:
            copies[i - 1].wait()
            if i + 1 < len(copies):
                copies[i + 1].start()

        @pl.when(live)
        def _():
            here = slice(i * first, (i + 1) * first)
            out[:, here] = dot(normed[...], query[:, here])


def received_rows(received):
    half = received[0].shape[0] // 2
    return [ref[(j % 2) * half : (j % 2 + 1) * half, :] for j, ref in enumerate(received)]


def correct_kernel(count, capacity, base, narrow, ident, *refs):
    received, outs = refs[:count], refs[count:]
    owner = lax.axis_index("wide")
    rows = base.shape[0]
    own_rows = rows // count
    slots = count * capacity
    place = lax.broadcasted_iota(jnp.int32, (rows, rows), 0)
    other = lax.broadcasted_iota(jnp.int32, (rows, rows), 1)
    own = ident[:, :1]
    flat = jnp.where(place == other, own, 0.0).astype(jnp.bfloat16)
    line = dot(jnp.ones((rows, rows), jnp.bfloat16), flat)
    rank = jnp.sum(jnp.where((own == line) & (other < place), 1.0, 0.0), 1, keepdims=True)
    slot = lax.broadcasted_iota(jnp.int32, (rows, slots), 1)
    source = ((slot // capacity) ^ owner).astype(jnp.float32)
    hit = (source == own) & ((slot % capacity).astype(jnp.float32) == rank)
    table = jnp.where(hit, 1.0, 0.0).astype(jnp.bfloat16)
    placed = dot(table, jnp.concatenate(received_rows(received), 0))
    query_cols, key_cols = base.shape[1], narrow.shape[1] // 2
    first = base[...] + placed[:, :query_cols]
    middle = narrow[:, :key_cols]
    last = narrow[:, key_cols:] + placed[:, query_cols:]
    packed = jnp.concatenate([first, middle, last], 1).astype(jnp.bfloat16)
    by_destination(owner, packed, own_rows, outs)


def by_destination(owner, packed, own_rows, outs):
    rows = packed.shape[0]
    place = lax.broadcasted_iota(jnp.int32, (rows, rows), 0)
    other = lax.broadcasted_iota(jnp.int32, (rows, rows), 1)
    hit = (((place // own_rows) ^ owner) == other // own_rows) & (
        place % own_rows == other % own_rows
    )
    order = jnp.where(hit, 1.0, 0.0).astype(jnp.bfloat16)
    sorted_rows = dot(order, packed).astype(jnp.bfloat16)
    for k, out in enumerate(outs):
        out[...] = sorted_rows[k * 2 * own_rows : (k + 1) * 2 * own_rows, :]


def attend_kernel(chips, lengths, near_lengths, *refs):
    arrived, rest = [refs[HEAD_ORDER.index(k)] for k in range(chips)], refs[chips:]
    cosine, sine, keys, values, near_keys, near_values, out, scores, weights = rest
    chip = lax.axis_index("wide") // 2
    own_rows, span = keys.shape[:2]
    chip_rows = 2 * own_rows
    rows = GROUP * chip_rows
    cos, sin = cosine[...], sine[...]
    position = lax.broadcasted_iota(jnp.int32, (2 * rows, span), 1)
    valid = position < row_lengths(lengths, near_lengths, (2 * rows, span), 2 * GROUP)
    score_scale = HD ** (-0.5)

    def turned(vectors):
        return vectors * cos + pltpu.roll(vectors, HD // 2, 1) * sin

    def rounded(vectors):
        return vectors.astype(jnp.bfloat16).astype(jnp.float32)

    pieces = []
    for ref in arrived:
        packed = ref[...].astype(jnp.float32)
        heads = [packed[:, i * HD : (i + 1) * HD] for i in range(GROUP)]
        fresh = [packed[:, GROUP * HD :]] * GROUP
        pieces += [jnp.concatenate(heads, 0), jnp.concatenate(fresh, 0)]
    out_row = lax.broadcasted_iota(jnp.int32, (rows, rows), 0)
    src_row = lax.broadcasted_iota(jnp.int32, (rows, rows), 1)
    same = (out_row // GROUP == src_row % chip_rows) & (out_row % GROUP == src_row // chip_rows)
    order = jnp.where(same, 1.0, 0.0).astype(jnp.bfloat16)
    sorted_rows = dot(order, jnp.concatenate(pieces, 1).astype(jnp.bfloat16))
    band = 2 * GROUP

    def woven(one, two):
        bands = [slice(r * GROUP, (r + 1) * GROUP) for r in range(chip_rows)]
        return jnp.concatenate([part[rows_of] for rows_of in bands for part in (one, two)], 0)

    def pair_lanes(p):
        return pl.ds(pl.multiple_of((chip // 2 ^ p) * 2 * HD, 2 * HD), 2 * HD)

    even = chip % 2 == 0
    zero = jnp.zeros((rows, HD), jnp.float32)
    pairs = range(chips // 2)
    fresh = []
    for p in pairs:
        wide, own, new_values = [], [], []
        for n in range(2):
            piece = sorted_rows[:, (2 * p + n) * 3 * HD : (2 * p + n + 1) * 3 * HD]
            query = rounded(turned(piece[:, :HD]))
            new_key = rounded(turned(piece[:, HD : 2 * HD]))
            own.append(jnp.sum(query * new_key, 1, keepdims=True) * score_scale)
            new_values.append(piece[:, 2 * HD :])
            left = even if n == 0 else jnp.logical_not(even)
            wide.append(
                jnp.concatenate([jnp.where(left, query, zero), jnp.where(left, zero, query)], 1)
            )
        fresh.append((woven(*own), woven(*new_values)))
        wide = woven(*wide).astype(jnp.bfloat16)
        for r in range(chip_rows):
            first = (p * chip_rows + r) * band
            scores[first : first + band, :] = lax.dot_general(
                wide[r * band : (r + 1) * band, :],
                (keys, near_keys)[r // own_rows][r % own_rows, :, pair_lanes(p)],
                (((1,), (1,)), ((), ())),
                preferred_element_type=jnp.float32,
            )
    parts = []
    for p, (own, new_value) in enumerate(fresh):
        here = slice(p * 2 * rows, (p + 1) * 2 * rows)
        found = jnp.where(valid, scores[here, :] * score_scale, -1e30)
        top = jnp.maximum(jnp.max(found, 1, keepdims=True), own)
        past = jnp.where(valid, jnp.exp(found - top), 0.0)
        own = jnp.exp(own - top)
        total = jnp.sum(past, 1, keepdims=True) + own
        weights[here, :] = (past / total).astype(jnp.bfloat16)
        parts.append(rounded(own / total) * new_value)
    for p, own_part in enumerate(parts):
        mixed = []
        for r in range(chip_rows):
            first = (p * chip_rows + r) * band
            found = dot(
                weights[first : first + band, :],
                (values, near_values)[r // own_rows][r % own_rows, :, pair_lanes(p)],
            )
            mine = own_part[r * band : (r + 1) * band, :]
            one = jnp.where(even, found[:GROUP, :HD], found[:GROUP, HD:]) + mine[:GROUP]
            two = jnp.where(even, found[GROUP:, HD:], found[GROUP:, :HD]) + mine[GROUP:]
            both = [jnp.where(even, one, two), jnp.where(even, two, one)]
            mixed.append(jnp.concatenate(both, 1))
        out[:, pair_lanes(p)] = jnp.concatenate(mixed, 0).astype(jnp.bfloat16)


def attended_rows(owner, chunks, own_rows, rows_ref):
    count = len(chunks)
    chips = count // 2
    rows = own_rows * count
    total = rows * GROUP
    out = lax.broadcasted_iota(jnp.int32, (total, total), 0)
    src = lax.broadcasted_iota(jnp.int32, (total, total), 1)
    device_out = (out // own_rows) % count
    chip_rows = 2 * own_rows
    row_src = (src // GROUP) % chip_rows
    near = (out // rows == src % GROUP) & (out % own_rows == row_src % own_rows)
    for core in range(2):
        stack = jnp.concatenate([chunks[2 * k + core][...] for k in range(chips)], 0)
        device_src = owner ^ (2 * (src // (GROUP * chip_rows)) + core) ^ (row_src // own_rows)
        hit = near & (device_out == device_src)
        spread = dot(jnp.where(hit, 1.0, 0.0).astype(jnp.bfloat16), stack).astype(jnp.bfloat16)
        first = (owner ^ core) % 2
        for i in range(chips):
            for j in range(GROUP):
                head = (2 * i + first) * GROUP + j
                rows_ref[:, pl.ds(pl.multiple_of(head * HD, HD), HD)] = spread[
                    j * rows : (j + 1) * rows, i * HD : (i + 1) * HD
                ]


def leave_kernel(count, own_rows, tick, *refs):
    chunks, rest = [None] * count, refs[count:]
    for i, j in enumerate([2 * p + c for p in ROW_ORDER for c in (0, 1)]):
        chunks[j] = refs[i]
    held, result = rest[0], rest[1] if tick else None
    matrix, out, kept, *outs, rows_ref = rest[2 if tick else 1 :]
    kept[...] = result[...] if tick else jnp.zeros_like(kept)

    @pl.when(lax.axis_index("segment") == tick)
    def _():
        attended_rows(lax.axis_index("wide"), chunks, own_rows, rows_ref)

        def store(columns, product):
            total = held[:, columns].astype(jnp.float32) + product
            out[:, columns] = total.astype(jnp.bfloat16)
            kept[:, columns] = total.astype(jnp.bfloat16)

        matmul_into(store, rows_ref, matrix, 2 * STEP)

    if outs:
        by_destination(lax.axis_index("wide"), kept[...], own_rows, outs)


def join_kernel(count, *refs):
    blocks, out = [None] * count, refs[count]
    for i, j in enumerate([2 * p + c for p in LAST_ORDER for c in (1, 0)]):
        blocks[j] = refs[i]
    for j, block in enumerate(blocks):
        rows = block.shape[0] // 2
        half = block[(j % 2) * rows : (j % 2 + 1) * rows, :]
        width = half.shape[1]
        columns = pl.ds(pl.multiple_of((lax.axis_index("wide") ^ j) * width, width), width)
        for m in range(out.shape[1]):
            local_rows = out.shape[2]
            out[0, m, :, columns] = half[m * local_rows : (m + 1) * local_rows, :]


def on_device_by_head(
    entering_hidden,
    row_adapter_index,
    lengths,
    input_norm_gain,
    query_matrix,
    key_matrix,
    value_matrix,
    output_matrix,
    adapter_down_maps,
    adapter_up_query,
    adapter_up_value,
    rotated_key_cache,
    cached_values,
):
    segments = lax.axis_size("segment")
    count = lax.axis_size("wide")
    micro, local_rows, width = entering_hidden.shape
    own_rows = micro * local_rows
    rows = own_rows * count
    capacity = CAP * micro
    part = width // count
    query_cols, key_cols = query_matrix.shape[2], key_matrix.shape[2]
    packed_cols = query_cols + 2 * key_cols
    span = rotated_key_cache.shape[3]

    chips = count // 2
    head_lanes = chips * HD
    query_weight = query_matrix[0]
    output_weight = output_matrix[0]
    adapters = [adapter_down_maps[0], adapter_up_query[0], adapter_up_value[0]]
    caches = [cache[0].reshape(own_rows, span, -1) for cache in (rotated_key_cache, cached_values)]
    near_lengths = swapped(lengths, 1)
    gain = input_norm_gain
    half = HD // 2
    inverse = np.tile(rope_base ** (-np.arange(half) / half), 2).astype(np.float32)[None]

    def blocks_of(slots, columns):
        return [jax.ShapeDtypeStruct((2 * slots, columns), jnp.bfloat16)] * chips

    normed_shape = jax.ShapeDtypeStruct((rows, width), jnp.bfloat16)
    held_shape = jax.ShapeDtypeStruct((rows, part), jnp.bfloat16)
    ident_shape = jax.ShapeDtypeStruct((rows, HD), jnp.float32)
    base_shape = jax.ShapeDtypeStruct((rows, query_cols), jnp.float32)
    narrow_shape = jax.ShapeDtypeStruct((rows, 2 * key_cols), jnp.float32)
    angle_shape = jax.ShapeDtypeStruct((GROUP * 2 * own_rows, HD), jnp.float32)
    correction_shapes = blocks_of(capacity, query_cols + key_cols)
    query_first = query_cols // 4
    output_first = part // 2

    names = pltpu.with_memory_space_constraint(row_adapter_index.transpose(0, 2, 1), pltpu.HBM)
    (entering,) = call(
        open_kernel,
        [jax.ShapeDtypeStruct((rows, part + HD), jnp.bfloat16)],
        [(entering_hidden, VMEM), (names, pl.BlockSpec(memory_space=pl.ANY))],
        [pltpu.SMEM(names.shape, names.dtype), pltpu.SemaphoreType.DMA],
        name="open",
    )
    projections, output_parts, halves, angles = [], [], [None, None], []
    held = ident = None
    result = None
    blocks = []
    for tick in range(segments):
        if tick == 0:

            def load_first():
                sources = [*adapters, key_matrix[0], value_matrix[0], query_weight, *caches]
                small = [(entering, VMEM)]
                shape = (own_rows, span, head_lanes)
                shapes = [source.shape for source in sources[:6]]
                shapes += [shape] * 2

                def plan(sources, outs):
                    pairs = list(zip(sources[:5], outs[:5]))
                    pairs.append((sources[5].at[:, :query_first], outs[5].at[:, :query_first]))
                    return pairs + half_of(1, sources[6:], outs[6:])

                found, (token,) = loaded(
                    sources, shapes, plan, 6 + 2 * chips, small, [TOKEN], token_of
                )
                adapters[:], projections[:] = found[:3], found[3:6]
                halves[2:] = found[6:]
                return token

            chunks, _ = gathered(entering, load_first)
            normed, held, ident, *found = call(
                functools.partial(enter_kernel, count, own_rows, capacity, tick),
                [normed_shape, held_shape, ident_shape] + correction_shapes,
                [(c, VMEM) for c in chunks]
                + [(near_lengths, pl.BlockSpec(memory_space=pl.ANY)), (gain, VMEM)],
                [pltpu.VMEM((count * rows, part + HD), jnp.float32)],
                kept=adapters,
                through=halves[2:],
                name="enter",
            )
            halves[2:] = [swapped(array, 1) for array in found[chips:]]
        else:
            chunks = passed_on(held, tick - 1)
            held = chunks[0]
            normed, *found = call(
                while_live(tick, functools.partial(norm_kernel, count, capacity)),
                [normed_shape] + correction_shapes,
                [(chunks[2 * p + c], VMEM) for p in HOP_ORDER for c in (1, 0)]
                + [(ident, VMEM), (gain, VMEM)],
                kept=adapters,
                name="norm",
            )
        correction = found[:chips]

        def project():
            return call(
                while_live(tick, project_kernel),
                [base_shape],
                [(normed, VMEM)],
                kept=projections[2:],
                cost=16,
                name="project",
            )[0]

        def project_first():
            base, projections[2] = pl.pallas_call(
                functools.partial(project_first_kernel, query_first, tick),
                out_shape=[base_shape, pltpu.VMEM(query_weight.shape, jnp.bfloat16)],
                in_specs=[VMEM, pl.BlockSpec(memory_space=pl.ANY), VMEM],
                out_specs=[VMEM, VMEM],
                input_output_aliases={2: 1},
                scratch_shapes=[pltpu.SemaphoreType.DMA((query_cols // query_first - 1,))],
                compiler_params=pltpu.CompilerParams(vmem_limit_bytes=8 * MIB),
                cost_estimate=pl.CostEstimate(
                    flops=0, transcendentals=0, bytes_accessed=16 * MIB
                ),
                name="project",
            )(
                normed,
                pltpu.with_memory_space_constraint(query_weight, pltpu.HBM),
                resident(projections[2]),
            )
            return base

        received, base = exchanged(correction, project if tick else project_first)
        received = [part for one in received for part in (one, swapped(one, 1))]
        (narrow,) = call(
            while_live(tick, narrow_kernel),
            [narrow_shape],
            [(normed, VMEM)],
            kept=projections[:2],
            cost=4,
            name="narrow",
        )
        packed = call(
            while_live(
                tick, functools.partial(correct_kernel, count, capacity)
            ),
            blocks_of(own_rows, packed_cols),
            [(base, VMEM), (narrow, VMEM), (ident, VMEM)] + [(r, VMEM) for r in received],
            name="correct",
        )

        def load_part():
            small = [(lengths, SMEM), (near_lengths, SMEM), (jnp.asarray(inverse), VMEM)]
            found, angles[:] = loaded(
                [output_weight, *caches],
                [output_weight.shape] + [(own_rows, span, head_lanes)] * 2,
                lambda sources, outs: [
                    (sources[0].at[:, :output_first], outs[0].at[:, :output_first])
                ]
                + half_of(0, sources[1:], outs[1:]),
                1 + 2 * chips,
                small,
                [angle_shape, angle_shape],
                angle_work,
            )
            output_parts[:], halves[:2] = found[:1], found[1:]
            return angles[0]

        def load_output():
            output_parts[0], token = pl.pallas_call(
                functools.partial(load_rest_kernel, output_first),
                out_shape=[pltpu.VMEM(output_weight.shape, jnp.bfloat16), TOKEN],
                in_specs=[pl.BlockSpec(memory_space=pl.ANY), VMEM, VMEM],
                out_specs=[VMEM, VMEM],
                input_output_aliases={2: 0},
                scratch_shapes=[pltpu.SemaphoreType.DMA],
                compiler_params=pltpu.CompilerParams(vmem_limit_bytes=4 * MIB),
                cost_estimate=pl.CostEstimate(
                    flops=0, transcendentals=0, bytes_accessed=8 * MIB
                ),
                name="load",
            )(
                pltpu.with_memory_space_constraint(output_weight, pltpu.HBM),
                attended,
                resident(output_parts[0]),
            )
            return token

        arrived, _ = exchanged(packed, None if tick else load_part)
        attended, *_ = call(
            while_live(tick, functools.partial(attend_kernel, chips)),
            [jax.ShapeDtypeStruct((GROUP * 2 * own_rows, head_lanes), jnp.bfloat16)],
            [(lengths, SMEM), (near_lengths, SMEM)]
            + [(a, VMEM) for a in [*[arrived[k] for k in HEAD_ORDER], *angles]],
            [
                pltpu.VMEM((chips * GROUP * 2 * own_rows, span), jnp.float32),
                pltpu.VMEM((chips * GROUP * 2 * own_rows, span), jnp.bfloat16),
            ],
            kept=halves,
            name="attend",
        )
        chunks, _ = gathered(attended, None if tick else load_output)
        last = tick == segments - 1
        held, result, *found = call(
            functools.partial(leave_kernel, count, own_rows, tick),
            [held_shape, held_shape] + (blocks_of(own_rows, part) if last else []),
            [(chunks[2 * p + c], VMEM) for p in ROW_ORDER for c in (0, 1)]
            + [(held, VMEM)] + ([(result, VMEM)] if tick else []),
            [pltpu.VMEM((rows, width), jnp.bfloat16)],
            kept=output_parts,
            name="leave",
        )
        blocks = found
    far, _ = exchanged(blocks)
    far = [part for one in far for part in (one, swapped(one, 1))]
    (joined,) = call(
        functools.partial(join_kernel, count),
        [jax.ShapeDtypeStruct((1, micro, local_rows, width), jnp.bfloat16)],
        [(far[2 * p + c], VMEM) for p in LAST_ORDER for c in (1, 0)],
        name="join",
    )
    return joined


def passed_along(value, axis, steps):
    count = lax.axis_size(axis)
    leading, last = (max(0, -steps), min(count, count - steps))
    return lax.ppermute(value, axis, [(source, source + steps) for source in range(leading, last)])


def rotary(vectors, positions):
    half = vectors.shape[-1] // 2
    inverse = rope_base ** (-jnp.arange(half, dtype=jnp.float32) / half)
    angles = positions.astype(jnp.float32)[:, None] * inverse[None, :]
    cosine = jnp.cos(angles)[:, None, :]
    sine = jnp.sin(angles)[:, None, :]
    front = vectors[..., :half]
    back = vectors[..., half:]
    return jnp.concatenate([front * cosine - back * sine, back * cosine + front * sine], -1)


def attend(query_vector, new_key, fresh_value, positions, key_block, value_block):
    rows = query_vector.shape[0]
    group = HEADS // KVH
    rotated_rows = rotary(
        query_vector.astype(jnp.float32).reshape(rows, HEADS, HD), positions
    ).astype(jnp.bfloat16)
    rotated_rows = rotated_rows.reshape(rows, KVH, group, HD)
    self_key = rotary(new_key.astype(jnp.float32).reshape(rows, KVH, HD), positions).astype(
        jnp.bfloat16
    )
    keys_past = key_block.reshape(rows, -1, KVH, HD)
    values_past = value_block.reshape(rows, -1, KVH, HD)
    score_scale = HD ** (-0.5)
    past = (
        jnp.einsum("bkgd,bpkd->bkgp", rotated_rows, keys_past, preferred_element_type=jnp.float32)
        * score_scale
    )
    self_scores = (
        jnp.einsum("rice,rie->ric", rotated_rows, self_key, preferred_element_type=jnp.float32)
        * score_scale
    )
    valid = jnp.arange(keys_past.shape[1])[None, :] < positions[:, None]
    past = jnp.where(valid[:, None, None, :], past, -1e30)
    top = jnp.maximum(jnp.max(past, -1), self_scores)
    past_exp = jnp.where(valid[:, None, None, :], jnp.exp(past - top[..., None]), 0.0)
    own_exp = jnp.exp(self_scores - top)
    total = jnp.sum(past_exp, -1) + own_exp
    past_weights = (past_exp / total[..., None]).astype(jnp.bfloat16)
    own_weights = (own_exp / total).astype(jnp.bfloat16)
    mixed = jnp.einsum(
        "bkgp,bpkd->bkgd", past_weights, values_past, preferred_element_type=jnp.float32
    )
    mixed = (
        mixed
        + own_weights.astype(jnp.float32)[..., None]
        * fresh_value.reshape(rows, KVH, HD).astype(jnp.float32)[:, :, None, :]
    )
    return mixed.reshape(rows, HEADS * HD).astype(jnp.bfloat16)


def on_device(
    entering_hidden,
    row_adapter_index,
    lengths,
    input_norm_gain,
    query_matrix,
    key_matrix,
    value_matrix,
    output_matrix,
    adapter_down_maps,
    adapter_up_query,
    adapter_up_value,
    rotated_key_cache,
    cached_values,
):
    segments = lax.axis_size("segment")
    segment = lax.axis_index("segment")
    devices = lax.axis_size("wide")
    owner = lax.axis_index("wide")
    small_batch, local_rows, width = entering_hidden.shape
    listed = lax.all_gather(row_adapter_index, "wide", axis=1, tiled=True)[:, :, 0]
    groups = small_batch // small_batch
    capacity = CAP * small_batch
    kept_entries = adapter_down_maps.shape[1]
    adapters = kept_entries * devices
    mine = owner * kept_entries + jnp.arange(kept_entries)
    gain = input_norm_gain[0].astype(jnp.float32)
    query_cols = query_matrix.shape[2]
    key_cols = key_matrix.shape[2]
    passed = jnp.zeros((small_batch * local_rows, width), jnp.bfloat16)
    results = jnp.zeros((small_batch, local_rows, width), jnp.bfloat16)
    ticks = groups + segments - 1
    for tick in range(ticks):
        if tick < groups:
            fresh = entering_hidden.reshape(small_batch * local_rows, width)
        else:
            fresh = jnp.zeros_like(passed)
        rows = jnp.where(segment == 0, fresh, passed)
        index = tick - segment
        live = (index >= 0) & (index < groups)
        index = jnp.clip(index, 0, groups - 1)
        block_rows = rows.shape[0]
        idents = listed
        idents = idents.reshape(small_batch, devices, local_rows).transpose(1, 0, 2).reshape(-1)
        positions = lengths.reshape(-1)
        key_block = rotated_key_cache[0]
        key_block = key_block.reshape(block_rows, key_block.shape[2], key_block.shape[3])
        value_block = cached_values[0]
        value_block = value_block.reshape(block_rows, value_block.shape[2], value_block.shape[3])
        values = rows.astype(jnp.float32)
        normalized_rows = (
            values * lax.rsqrt(jnp.mean(values * values, 1, keepdims=True) + epsilon) * gain
        ).astype(jnp.bfloat16)
        gathered = lax.all_gather(normalized_rows, "wide", axis=0, tiled=True)
        total_rows = gathered.shape[0]
        matches = (idents[None, :] == mine[:, None]).astype(jnp.int32)
        ranks = jnp.cumsum(matches, 1) - 1
        chosen = (matches[:, None, :] == 1) & (
            ranks[:, None, :] == jnp.arange(capacity)[None, :, None]
        )
        chosen = chosen.reshape(kept_entries * capacity, total_rows)
        selected_rows = jnp.dot(
            chosen.astype(jnp.bfloat16), gathered, preferred_element_type=jnp.float32
        ).astype(jnp.bfloat16)
        selected_rows = selected_rows.reshape(kept_entries, capacity, width)
        reduced = jnp.einsum(
            "bpy,byf->bpf", selected_rows, adapter_down_maps[0], preferred_element_type=jnp.float32
        ).astype(jnp.bfloat16)
        member = (idents[:, None] == jnp.arange(adapters)[None, :]).astype(jnp.int32)
        order = jnp.sum(jnp.cumsum(member, 0) * member, 1) - 1
        slot = idents * capacity + order
        slot_table = slot[:, None] == jnp.arange(adapters * capacity)[None, :]
        query_slots = jnp.einsum(
            "acr,are->ace",
            reduced[..., :ADAPTER_RANK],
            adapter_up_query[0],
            preferred_element_type=jnp.float32,
        )
        value_slots = jnp.einsum(
            "acr,are->ace",
            reduced[..., ADAPTER_RANK:],
            adapter_up_value[0],
            preferred_element_type=jnp.float32,
        )
        joined = jnp.concatenate(
            [
                query_slots.reshape(kept_entries * capacity, devices, -1),
                value_slots.reshape(kept_entries * capacity, devices, -1),
            ],
            2,
        )
        received = lax.all_to_all(joined, "wide", split_axis=1, concat_axis=0, tiled=True)
        received = received.reshape(adapters * capacity, -1)
        placed = jnp.dot(slot_table.astype(jnp.float32), received, precision=lax.Precision.HIGHEST)
        query_adjustment = placed[:, :query_cols]
        value_adjustment = placed[:, query_cols:]
        query_vector = (
            jnp.dot(gathered, query_matrix[0], preferred_element_type=jnp.float32)
            + adapter_scale * query_adjustment
        ).astype(jnp.bfloat16)
        new_key = jnp.dot(gathered, key_matrix[0], preferred_element_type=jnp.float32).astype(
            jnp.bfloat16
        )
        fresh_value = (
            jnp.dot(gathered, value_matrix[0], preferred_element_type=jnp.float32)
            + adapter_scale * value_adjustment
        ).astype(jnp.bfloat16)
        packed = jnp.concatenate([query_vector, new_key, fresh_value], 1)
        arrived = lax.all_to_all(packed, "wide", split_axis=0, concat_axis=1, tiled=True).reshape(
            block_rows, devices, -1
        )
        query_rows_local = arrived[:, :, :query_cols].reshape(block_rows, -1)
        key_rows_local = arrived[:, :, query_cols : query_cols + key_cols].reshape(block_rows, -1)
        value_rows_local = arrived[:, :, query_cols + key_cols :].reshape(block_rows, -1)
        attended = attend(
            query_rows_local, key_rows_local, value_rows_local, positions, key_block, value_block
        )
        columns = jnp.dot(
            lax.all_gather(attended, "wide", axis=0, tiled=True),
            output_matrix[0],
            preferred_element_type=jnp.float32,
        )
        returned = lax.all_to_all(columns, "wide", split_axis=0, concat_axis=1, tiled=True)
        outcome = (values + returned).astype(jnp.bfloat16)
        updated = outcome.reshape(small_batch, local_rows, width)
        results = jnp.where(live, updated, results)
        if tick + 1 < ticks:
            passed = passed_along(outcome, "segment", 1)
    return results[None]


def solution(mesh):
    placed = (
        P(None, "wide", None),
        P(None, "wide", None),
        P(None, "wide"),
        P("segment", None),
        P("segment", None, "wide"),
        P("segment", None, "wide"),
        P("segment", None, "wide"),
        P("segment", None, "wide"),
        P("segment", "wide", None, None),
        P("segment", "wide", None, None),
        P("segment", "wide", None, None),
        P("segment", None, "wide", None, None),
        P("segment", None, "wide", None, None),
    )
    by_head = mesh.shape["wide"] == KVH
    return jax.shard_map(
        on_device_by_head if by_head else on_device,
        mesh=mesh,
        in_specs=placed,
        out_specs=P("segment", None, "wide", None),
        check_vma=False,
    )
```
